32 devices in a mesh: dp: 16 (over z, y, x), heads: 2 (over core).
Axes of the slice: x: 2, y: 2, z: 4, core: 2. Of those that a mesh axis runs over, the one named last changes fastest.
Arguments:
- tokens: bfloat16 [38912, 256], P(('dp', 'heads')), may hold values from -6 to 6
- cotangent: bfloat16 [38912, 256], P(('dp', 'heads')), may hold values from -6 to 6
- counts: int32 [64], P('dp'), may hold values from 2 to 6, as said below
- ln1_gain: float32 [2, 256], replicated, may hold values from 0.5 to 1.5
- ln1_bias: float32 [2, 256], replicated, may hold values from -1.75 to 1.75
- w_qkv: bfloat16 [2, 2, 256, 384], P(None, 'heads'), may hold values from -0.375 to 0.375
- lepe_w: float32 [2, 2, 9, 128], P(None, 'heads'), may hold values from -2 to 2
- lepe_b: float32 [2, 2, 128], P(None, 'heads'), may hold values from -1.75 to 1.75
- w_proj: bfloat16 [2, 256, 256], replicated, may hold values from -0.375 to 0.375
- b_proj: float32 [2, 256], replicated, may hold values from -1.75 to 1.75
- ln2_gain: float32 [2, 256], replicated, may hold values from 0.5 to 1.5
- ln2_bias: float32 [2, 256], replicated, may hold values from -1.75 to 1.75
- w_fc1: bfloat16 [2, 256, 1024], replicated, may hold values from -0.375 to 0.375
- b_fc1: float32 [2, 1024], replicated, may hold values from -1.75 to 1.75
- w_fc2: bfloat16 [2, 1024, 256], replicated, may hold values from -0.25 to 0.25
- b_fc2: float32 [2, 256], replicated, may hold values from -1.75 to 1.75
Outputs:
- output: bfloat16 [38912, 256], P(('dp', 'heads'))
- grad_tokens: float32 [38912, 256], P(('dp', 'heads'))
- g_ln1_gain: float32 [2, 256], replicated
- g_ln1_bias: float32 [2, 256], replicated
- g_w_qkv: float32 [2, 2, 256, 384], P(None, 'heads')
- g_lepe_w: float32 [2, 2, 9, 128], P(None, 'heads')
- g_lepe_b: float32 [2, 2, 128], P(None, 'heads')
- g_w_proj: float32 [2, 256, 256], replicated
- g_b_proj: float32 [2, 256], replicated
- g_ln2_gain: float32 [2, 256], replicated
- g_ln2_bias: float32 [2, 256], replicated
- g_w_fc1: float32 [2, 256, 1024], replicated
- g_b_fc1: float32 [2, 1024], replicated
- g_w_fc2: float32 [2, 1024, 256], replicated
- g_b_fc2: float32 [2, 256], replicated
The draws below stay inside these ranges and needn't reach their ends.
Inputs may be any that keep to these rules, and one draw needn't show every extreme that they name: Local crop slots from counts on are padding and are masked from the output; some image has 6 local crops and some has 2.
All inputs are finite; a program needn't handle non-finite values.
Results may differ from the reference program's by a relative error of at most 0.018.
Values may be sent and summed in bfloat16 or wider, within the bound.
No kernel may reach another device: no remote copies, remote signals or barrier semaphores. Data moves between devices by JAX's collectives and lax.ppermute only.
A program may use at most 192 MiB of HBM per device.

```python
import jax
import jax.numpy as jnp
from jax import lax

D = 256
FF = 1024
SW = 7
HD = 32
GH = 4
HW = 128
G1 = 14
G2 = 6
SW2 = 6
NG = 2
NL = 6
LAYERS = 2
TOK_IMG = 608
IMAGES = 64
TOKENS = 38912


def draw_counts(key, part):
    key = jax.random.fold_in(key, 7)
    first, second = jax.random.split(key)
    values = jax.random.randint(first, (IMAGES,), 2, NL + 1)
    order = jax.random.permutation(second, IMAGES)
    values = values.at[order[0]].set(NL).at[order[1]].set(2)
    return values.astype(jnp.int32)


def level_of(own_key, dims, pieces, least, largest):
    level = 1.0
    for axis_at, parts in pieces:
        heights = jax.random.uniform(jax.random.fold_in(jax.random.fold_in(own_key, 6), axis_at), (parts,), jnp.float32, least / len(pieces), largest / len(pieces))
        level = level * jnp.repeat(jnp.exp(heights), dims[axis_at] // parts).reshape((-1,) + (1,) * (len(dims) - 1 - axis_at))
    return level


def normal_values(rng, dims, deviation, most, shards=(), kind=jnp.bfloat16):
    values = jax.random.normal(rng, dims, jnp.float32) * deviation
    if len(shards) > 0:
        values = level_of(rng, dims, shards, -0.22, 0.18) * values
    return jnp.clip(values, min=-most, max=most).astype(kind)


def setup_inputs(seed: int = 0) -> dict:
    key_list = jax.random.split(jax.random.key(seed), 17)
    tokens = normal_values(key_list[0], (TOKENS, D), 1.0, 6.0, ((0, 32),))
    cotangent = normal_values(key_list[1], (TOKENS, D), 1.0, 6.0, ((0, 32),))
    counts = draw_counts(jax.random.fold_in(key_list[16], 71), 0)
    ln1_gain = jnp.clip(1.0 + 0.1 * jax.random.normal(key_list[3], (LAYERS, D), jnp.float32), 0.5, 1.5)
    ln1_bias = normal_values(key_list[4], (LAYERS, D), 0.3, 1.75, (), jnp.float32)
    w_qkv = normal_values(key_list[5], (LAYERS, 2, D, 3 * HW), D ** -0.5, 0.375, ((1, 2),))
    lepe_w = normal_values(key_list[6], (LAYERS, 2, 9, HW), 9 ** -0.5, 2.0, ((1, 2),), jnp.float32)
    lepe_b = normal_values(key_list[7], (LAYERS, 2, HW), 0.3, 1.75, ((1, 2),), jnp.float32)
    w_proj = normal_values(key_list[8], (LAYERS, D, D), D ** -0.5, 0.375)
    b_proj = normal_values(key_list[9], (LAYERS, D), 0.3, 1.75, (), jnp.float32)
    ln2_gain = jnp.clip(1.0 + 0.1 * jax.random.normal(key_list[10], (LAYERS, D), jnp.float32), 0.5, 1.5)
    ln2_bias = normal_values(key_list[11], (LAYERS, D), 0.3, 1.75, (), jnp.float32)
    w_fc1 = normal_values(key_list[12], (LAYERS, D, FF), D ** -0.5, 0.375)
    b_fc1 = normal_values(key_list[13], (LAYERS, FF), 0.3, 1.75, (), jnp.float32)
    w_fc2 = normal_values(key_list[14], (LAYERS, FF, D), (FF // 2) ** -0.5, 0.25)
    b_fc2 = normal_values(key_list[15], (LAYERS, D), 0.3, 1.75, (), jnp.float32)
    return dict(tokens=tokens, cotangent=cotangent, counts=counts, ln1_gain=ln1_gain, ln1_bias=ln1_bias, w_qkv=w_qkv, lepe_w=lepe_w, lepe_b=lepe_b, w_proj=w_proj, b_proj=b_proj, ln2_gain=ln2_gain, ln2_bias=ln2_bias, w_fc1=w_fc1, b_fc1=b_fc1, w_fc2=w_fc2, b_fc2=b_fc2)


@jax.custom_vjp
def low(v):
    return lax.optimization_barrier(v.astype(jnp.bfloat16)).astype(jnp.float32)

@jax.custom_vjp
def low_back(v):
    return v

def low_keep(v):
    return (low(v), None)

def low_pass(kept, grad):
    return (grad,)

def back_keep(v):
    return (v, None)

def back_low(kept, grad):
    return (low(grad),)
low.defvjp(low_keep, low_pass)
low_back.defvjp(back_keep, back_low)
EPSILON = 1e-05
HIGH = lax.Precision.HIGHEST

def layer_norm(value, gain, bias):
    center = value - lax.optimization_barrier(jnp.mean(value, axis=-1, keepdims=True))
    spread = lax.optimization_barrier(jnp.mean(center * center, axis=-1, keepdims=True))
    return center * lax.rsqrt(spread + EPSILON) * gain + bias

def stripe_group(qkv, weight, bias, grid, width, vertical):
    count = qkv.shape[0]
    field = qkv.reshape(count, grid, grid, 3 * HW)
    if vertical:
        field = jnp.swapaxes(field, 1, 2)
    nwin = count * (grid // width)
    span = width * grid
    wins = field.reshape(nwin, span, 3 * HW)
    query = wins[:, :, :HW].reshape(nwin, span, GH, HD)
    keyset = wins[:, :, HW:2 * HW].reshape(nwin, span, GH, HD)
    values = wins[:, :, 2 * HW:]
    scores = low_back(jnp.einsum('wqhd,wkhd->whqk', query, keyset, precision=HIGH) * HD ** (-0.5))
    probs = low(jax.nn.softmax(scores, axis=-1))
    mixed = jnp.einsum('whqk,wkhd->wqhd', probs, values.reshape(nwin, span, GH, HD), precision=HIGH)
    padded = jnp.pad(values.reshape(nwin, width, grid, HW), ((0, 0), (1, 1), (1, 1), (0, 0)))
    local = jnp.zeros((nwin, width, grid, HW), jnp.float32) + bias
    for first in range(3):
        for second in range(3):
            local = local + weight[3 * first + second] * padded[:, first:first + width, second:second + grid]
    result = (mixed.reshape(nwin, span, HW) + local.reshape(nwin, span, HW)).reshape(count, grid, grid, HW)
    if vertical:
        result = jnp.swapaxes(result, 1, 2)
    return result.reshape(count, grid * grid, HW)

def attention(normed, w_qkv, lepe_w, lepe_b):
    total = normed.shape[0]
    images = total // TOK_IMG
    split = NG * G1 * G1
    outputs = []
    for group in range(2):
        qkv = low_back(low(jnp.dot(normed, w_qkv[group], precision=HIGH, preferred_element_type=jnp.float32)))
        per_image = qkv.reshape(images, TOK_IMG, 3 * HW)
        large = stripe_group(per_image[:, :split].reshape(images * NG, G1 * G1, 3 * HW), lepe_w[group], lepe_b[group], G1, SW, group == 1)
        small = stripe_group(per_image[:, split:].reshape(images * NL, G2 * G2, 3 * HW), lepe_w[group], lepe_b[group], G2, SW2, group == 1)
        joined = jnp.concatenate([large.reshape(images, split, HW), small.reshape(images, TOK_IMG - split, HW)], axis=1)
        outputs.append(joined.reshape(total, HW))
    return jnp.concatenate(outputs, axis=1)

def block(value, layer):
    gain1, bias1, w_qkv, lepe_w, lepe_b, w_proj, b_proj, gain2, bias2, w_fc1, b_fc1, w_fc2, b_fc2 = layer
    normed = low(layer_norm(value, gain1, bias1))
    heads = low_back(low(attention(normed, w_qkv, lepe_w, lepe_b)))
    inner = value + low_back(jnp.dot(heads, w_proj, precision=HIGH, preferred_element_type=jnp.float32) + b_proj)
    normed2 = low(layer_norm(inner, gain2, bias2))
    hidden = low_back(jnp.dot(normed2, w_fc1, precision=HIGH, preferred_element_type=jnp.float32) + b_fc1)
    act = low(jax.nn.gelu(hidden, approximate=False))
    return inner + low_back(jnp.dot(act, w_fc2, precision=HIGH, preferred_element_type=jnp.float32) + b_fc2)

def reference(tokens, cotangent, counts, ln1_gain, ln1_bias, w_qkv, lepe_w, lepe_b, w_proj, b_proj, ln2_gain, ln2_bias, w_fc1, b_fc1, w_fc2, b_fc2):
    params = tuple((item.astype(jnp.float32) for item in (ln1_gain, ln1_bias, w_qkv, lepe_w, lepe_b, w_proj, b_proj, ln2_gain, ln2_bias, w_fc1, b_fc1, w_fc2, b_fc2)))
    index = jnp.arange(TOKENS, dtype=jnp.int32)
    image = index // TOK_IMG
    place = index % TOK_IMG
    split = NG * G1 * G1
    crop = (place - split) // (G2 * G2)
    keep = jnp.where((place < split) | (crop < counts[image]), 1.0, 0.0).astype(jnp.float32)[:, None]

    def forward(value, *weights):
        for layer in range(LAYERS):
            value = block(value, tuple((item[layer] for item in weights)))
        return value * keep
    result, pull = jax.vjp(forward, tokens.astype(jnp.float32), *params)
    grads = pull(cotangent.astype(jnp.float32))
    return (result.astype(jnp.bfloat16), grads[0], grads[1], grads[2], grads[3], grads[4], grads[5], grads[6], grads[7], grads[8], grads[9], grads[10], grads[11], grads[12], grads[13])
```

```python
import functools
import math

import jax
import jax.numpy as jnp
import numpy as np
from jax import lax
from jax.experimental import pallas as pl
from jax.experimental.pallas import tpu as pltpu
from jax.sharding import PartitionSpec as P

D = 256
FF = 1024
HD = 32
GH = 4
HW = 128
LAYERS = 2
TOK_IMG = 608
SPLIT = 392
EPSILON = 1e-05

QUAD = 56
BLOCK = 2 * QUAD
CHUNK = 2 * BLOCK
IMG = 6 * BLOCK
KEYS = 128
SPAN = GH * KEYS
TAPS = 9
SCALE = HD**-0.5
EXP_SCALE = SCALE * math.log2(math.e)
BF = jnp.bfloat16
F32 = jnp.float32

FC1_AT = 0
FC2_AT = 1024
PROJ_AT = 2048
QKV_AT = 2304
SMALL_AT = 3072
SMALL = 32
PACKED = SMALL_AT + SMALL


def place_table():
    table = np.zeros((IMG, TOK_IMG), np.float32)
    for crop in range(2):
        for quad in range(4):
            for cell in range(49):
                row = (quad // 2) * 7 + cell // 7
                col = (quad % 2) * 7 + cell % 7
                table[crop * 224 + quad * QUAD + cell, crop * 196 + row * 14 + col] = 1
    for group in range(2):
        for cell in range(108):
            table[448 + group * BLOCK + cell, SPLIT + group * 108 + cell] = 1
    return table


def block_cells(kind):
    cells = [None] * BLOCK
    if kind == 2:
        for cell in range(108):
            cells[cell] = (cell // 36, (cell % 36) // 6, cell % 6)
    else:
        for half in range(2):
            for cell in range(49):
                row, col = cell // 7, cell % 7
                shifted = (0, row, col + 7 * half) if kind == 0 else (0, row + 7 * half, col)
                cells[half * QUAD + cell] = shifted
    return cells


def shift_tables():
    wide = np.zeros((3, BLOCK, TAPS * KEYS), np.float32)
    tall = np.zeros((3, TAPS * BLOCK, KEYS), np.float32)
    for kind in range(3):
        cells = block_cells(kind)
        where = {cell: place for place, cell in enumerate(cells) if cell is not None}
        for tap in range(TAPS):
            for place, cell in enumerate(cells):
                if cell is None:
                    continue
                other = where.get((cell[0], cell[1] + tap // 3 - 1, cell[2] + tap % 3 - 1))
                if other is not None:
                    wide[kind, place, tap * KEYS + other] = 1
                    tall[kind, tap * BLOCK + place, other] = 1
    return wide, tall


def bias_table():
    bias = np.full((2, BLOCK, KEYS), -1e30, np.float32)
    bias[0, :, :49] = 0
    bias[0, :, QUAD : QUAD + 49] = 0
    for row in range(BLOCK):
        if row < 108:
            first = 36 * (row // 36)
            bias[1, row, first : first + 36] = 0
        else:
            bias[1, row, :108] = 0
    return bias


def head_table():
    table = np.zeros((SPAN, HW), np.float32)
    for head in range(GH):
        table[head * KEYS : (head + 1) * KEYS, head * HD : (head + 1) * HD] = 1
    return table


def dot(left, right):
    return lax.dot_general(left, right, (((1,), (0,)), ((), ())), preferred_element_type=F32)


def dot_nt(left, right):
    return lax.dot_general(left, right, (((1,), (1,)), ((), ())), preferred_element_type=F32)


def dot_tn(left, right):
    return lax.dot_general(left, right, (((0,), (0,)), ((), ())), preferred_element_type=F32)


def norm_parts(value):
    center = value - jnp.mean(value, axis=-1, keepdims=True)
    scale = lax.rsqrt(jnp.mean(center * center, axis=-1, keepdims=True) + EPSILON)
    return center * scale, scale


def norm_back(dout, value, gain):
    xhat, scale = norm_parts(value)
    grown = dout * gain
    mean = jnp.mean(grown, axis=-1, keepdims=True)
    cross = jnp.mean(grown * xhat, axis=-1, keepdims=True)
    return scale * (grown - mean - xhat * cross), dout * xhat


def fold_rows(value):
    return jnp.sum(value.reshape(value.shape[0] // 8, 8, value.shape[1]), axis=0)


def head_stack(value, heads_ref):
    rows = []
    pad = jnp.zeros((KEYS - BLOCK, HW), BF)
    for head in range(GH):
        rows.append(value * heads_ref[head * KEYS : head * KEYS + 1, :])
        rows.append(pad)
    return jnp.concatenate(rows, axis=0)


def swap_quads(value):
    return jnp.concatenate(
        [value[:QUAD], value[2 * QUAD : 3 * QUAD], value[QUAD : 2 * QUAD], value[3 * QUAD :]], axis=0
    )


def halves(block, direction):
    inside = lax.rem(block, 6)
    first = block * BLOCK
    second = first + QUAD
    if direction == 1:
        crop = (block - lax.rem(inside, 2)) * BLOCK
        large = inside < 4
        first = jnp.where(large, crop + QUAD * lax.rem(inside, 2), first)
        second = jnp.where(large, crop + BLOCK + QUAD * lax.rem(inside, 2), second)
    return pl.multiple_of(first, 8), pl.multiple_of(second, 8)


def tap_row(direction, tap):
    return tap if direction == 0 else 3 * (tap % 3) + tap // 3


def step_kernel(
    meta,
    tok_ref,
    cot_ref,
    g1_ref,
    b1_ref,
    wqkv_ref,
    lepe_ref,
    wproj_ref,
    bproj_ref,
    g2_ref,
    b2_ref,
    wfc1_ref,
    bfc1_ref,
    wfc2_ref,
    bfc2_ref,
    place_ref,
    wide_ref,
    tall_ref,
    bias_ref,
    heads_ref,
    out_ref,
    dtok_ref,
    packed_ref,
    h_ref,
    normed_ref,
    qkv_ref,
    expo_ref,
    mixed_ref,
    hf_ref,
    hb_ref,
    inner_ref,
    normed2_ref,
    act_ref,
    slope_ref,
    dh_ref,
    dz_ref,
    dhid_ref,
    acc_ref,
    accff_ref,
    acclepe_ref,
    small_ref,
    stage_ref,
):
    rows_all = h_ref.shape[1]
    images = rows_all // IMG
    chunks = rows_all // CHUNK
    blocks = rows_all // BLOCK
    parts = packed_ref.shape[1]
    part_rows = packed_ref.shape[3]
    core = meta[0]
    mine = meta[1]

    def chunk_rows(index):
        return pl.ds(pl.multiple_of(index * CHUNK, 16), CHUNK)

    def block_rows(index):
        return pl.ds(pl.multiple_of(index * BLOCK, 16), BLOCK)

    def keep_of(image):
        place = lax.broadcasted_iota(jnp.int32, (IMG, 1), 0)
        limit = meta[2 + image]
        group = (place - 448) // BLOCK
        inside = (place - 448) % BLOCK
        return (place < 448) | (inside < 36 * (limit - 3 * group))

    for image in range(images):
        spot = pl.ds(image * TOK_IMG, TOK_IMG)
        h_ref[0, pl.ds(image * IMG, IMG), :] = dot(place_ref[...], tok_ref[spot, :])

    def forward(layer, carry):
        def project(index, carry):
            rows = chunk_rows(index)
            xhat, _ = norm_parts(h_ref[layer, rows, :])
            normed = xhat * g1_ref[pl.ds(layer, 1), :] + b1_ref[pl.ds(layer, 1), :]
            large = lax.rem(index, 3) < 2
            turned = jnp.where(large, swap_quads(normed), normed)
            for direction, value in enumerate((normed, turned)):
                value = value.astype(BF)
                normed_ref[layer, direction, rows, :] = value
                qkv_ref[layer, direction, rows, :] = dot(value, wqkv_ref[direction, layer]).astype(BF)
            return carry

        lax.fori_loop(0, chunks, project, 0)

        def attend(index, carry):
            rows = block_rows(index)
            large = lax.rem(index, 6) < 4
            bias = bias_ref[jnp.where(large, 0, 1)]
            for direction in range(2):
                kind = jnp.where(large, direction, 2)
                query = qkv_ref[layer, direction, rows, :HW]
                keyset = qkv_ref[layer, direction, rows, HW : 2 * HW]
                values = qkv_ref[layer, direction, rows, 2 * HW :]
                scores = dot_nt(query, head_stack(keyset, heads_ref))
                expo = []
                for head in range(GH):
                    part = scores[:, head * KEYS : (head + 1) * KEYS] + bias
                    top = jnp.max(part, axis=-1, keepdims=True)
                    expo.append(jnp.exp2((part - top) * EXP_SCALE).astype(BF))
                expo = jnp.concatenate(expo, axis=1)
                expo_ref[layer, direction, rows, :] = expo
                both = dot(expo, jnp.concatenate([head_stack(values, heads_ref), heads_ref[...]], axis=1))
                recip = 1.0 / both[:, HW:]
                mixed = both[:, :HW] * recip
                mixed_ref[layer, direction, rows, :] = mixed
                wide_values = jnp.concatenate([values.astype(F32), jnp.zeros((KEYS - BLOCK, HW), F32)], axis=0)
                scaled = [
                    (wide_values * lepe_ref[direction, layer, pl.ds(tap_row(direction, tap), 1), :]).astype(BF)
                    for tap in range(TAPS)
                ]
                local = dot(wide_ref[kind], jnp.concatenate(scaled, axis=0))
                result = mixed + local + lepe_ref[direction, layer, TAPS : TAPS + 1, :]
                first, second = halves(index, direction)
                lanes = slice(direction * HW, (direction + 1) * HW)
                hf_ref[pl.ds(first, QUAD), lanes] = result[:QUAD]
                hf_ref[pl.ds(second, QUAD), lanes] = result[QUAD:]
            return carry

        lax.fori_loop(0, blocks, attend, 0)

        def feed(index, carry):
            rows = chunk_rows(index)
            heads = hf_ref[rows, :].astype(BF)
            hb_ref[layer, rows, :] = heads
            inner = h_ref[layer, rows, :] + dot(heads, wproj_ref[layer]) + bproj_ref[pl.ds(layer, 1), :]
            inner_ref[layer, rows, :] = inner
            xhat, _ = norm_parts(inner)
            normed2 = (xhat * g2_ref[pl.ds(layer, 1), :] + b2_ref[pl.ds(layer, 1), :]).astype(BF)
            normed2_ref[layer, rows, :] = normed2
            hidden = dot(normed2, wfc1_ref[layer]) + bfc1_ref[pl.ds(layer, 1), :]
            cdf = 0.5 + 0.5 * lax.erf(hidden * math.sqrt(0.5))
            act = (hidden * cdf).astype(BF)
            act_ref[layer, rows, :] = act
            slope = cdf + hidden * jnp.exp(-0.5 * hidden * hidden) * (1.0 / math.sqrt(2 * math.pi))
            slope_ref[layer, rows, :] = slope.astype(BF)
            h_ref[layer + 1, rows, :] = inner + dot(act, wfc2_ref[layer]) + bfc2_ref[pl.ds(layer, 1), :]
            return carry

        lax.fori_loop(0, chunks, feed, 0)
        return carry

    lax.fori_loop(0, LAYERS, forward, 0)

    for image in range(images):
        spot = pl.ds(image * TOK_IMG, TOK_IMG)
        wide = pl.ds(image * IMG, IMG)
        keep = keep_of(image)
        result = jnp.where(keep, h_ref[LAYERS, wide, :], 0.0).astype(BF)
        out_ref[spot, :] = dot_tn(place_ref[...], result).astype(BF)
        dh_ref[wide, :] = jnp.where(keep, dot(place_ref[...], cot_ref[spot, :]), 0.0)

    def backward(step, carry):
        layer = LAYERS - 1 - step
        acc_ref[...] = jnp.zeros_like(acc_ref)
        accff_ref[...] = jnp.zeros_like(accff_ref)
        acclepe_ref[...] = jnp.zeros_like(acclepe_ref)

        def feed(index, carry):
            rows = chunk_rows(index)
            grad = dh_ref[rows, :]
            dz = grad.astype(BF)
            dz_ref[rows, :] = dz
            acc_ref[5] += fold_rows(dz.astype(F32))
            dhid = (dot_nt(dz, wfc2_ref[layer]) * slope_ref[layer, rows, :].astype(F32)).astype(BF)
            dhid_ref[rows, :] = dhid
            accff_ref[...] += fold_rows(dhid.astype(F32))
            dnormed = dot_nt(dhid, wfc1_ref[layer])
            dvalue, dgain = norm_back(dnormed, inner_ref[layer, rows, :], g2_ref[pl.ds(layer, 1), :])
            acc_ref[3] += fold_rows(dgain)
            acc_ref[4] += fold_rows(dnormed)
            dinner = grad + dvalue
            dh_ref[rows, :] = dinner
            return carry

        lax.fori_loop(0, chunks, feed, 0)

        def feed_weights(index, carry):
            cols = pl.ds(pl.multiple_of(index * 256, 256), 256)
            half = index // 2
            first = dot_tn(normed2_ref[layer], dhid_ref[:, cols]).astype(BF)
            second = dot_tn(dz_ref[...], act_ref[layer, :, cols]).astype(BF)
            for piece in range(2):
                at = pl.multiple_of((lax.rem(index, 2) * 2 + piece) * 256, 256)
                lanes = slice(piece * HW, (piece + 1) * HW)
                stage_ref[half, pl.ds(FC1_AT + at, 256), :] = first[:, lanes]
                stage_ref[half, pl.ds(FC2_AT + at, 256), :] = second[:, lanes]
            return carry

        lax.fori_loop(0, 4, feed_weights, 0)

        def project(index, carry):
            rows = chunk_rows(index)
            dy = dh_ref[rows, :].astype(BF)
            dz_ref[rows, :] = dy
            acc_ref[2] += fold_rows(dy.astype(F32))
            hf_ref[rows, :] = dot_nt(dy, wproj_ref[layer])
            return carry

        lax.fori_loop(0, chunks, project, 0)
        gproj = dot_tn(hb_ref[layer], dz_ref[...]).astype(BF)
        for half in range(2):
            stage_ref[half, PROJ_AT : PROJ_AT + D, :] = gproj[:, half * HW : (half + 1) * HW]

        def attend(index, carry):
            rows = block_rows(index)
            large = lax.rem(index, 6) < 4
            for direction in range(2):
                kind = jnp.where(large, direction, 2)
                first, second = halves(index, direction)
                lanes = slice(direction * HW, (direction + 1) * HW)
                grad = jnp.concatenate(
                    [hf_ref[pl.ds(first, QUAD), lanes], hf_ref[pl.ds(second, QUAD), lanes]], axis=0
                ).astype(BF)
                grad32 = grad.astype(F32)
                query = qkv_ref[layer, direction, rows, :HW]
                keyset = qkv_ref[layer, direction, rows, HW : 2 * HW]
                values = qkv_ref[layer, direction, rows, 2 * HW :]
                expo = expo_ref[layer, direction, rows, :]
                recip = 1.0 / dot(expo, heads_ref[...])
                inner = grad32 * mixed_ref[layer, direction, rows, :]
                inner_high = inner.astype(BF)
                inner_low = (inner - inner_high.astype(F32)).astype(BF)
                masks = heads_ref[...]
                dprobs = dot_nt(
                    jnp.concatenate([grad, -inner_high, -inner_low], axis=1),
                    jnp.concatenate([head_stack(values, heads_ref), masks, masks], axis=1),
                )
                dscores = (expo.astype(F32) * dprobs).astype(BF)
                dquery = dot(dscores, head_stack(keyset, heads_ref)) * recip * SCALE
                dkeys_all = dot_tn((query.astype(F32) * recip * SCALE).astype(BF), dscores)
                dvalues_all = dot_tn((grad32 * recip).astype(BF), expo)
                dkeys = jnp.concatenate(
                    [
                        dkeys_all[head * HD : (head + 1) * HD, head * KEYS : (head + 1) * KEYS]
                        for head in range(GH)
                    ],
                    axis=0,
                ).T[:BLOCK]
                dvalues = jnp.concatenate(
                    [
                        dvalues_all[head * HD : (head + 1) * HD, head * KEYS : (head + 1) * KEYS]
                        for head in range(GH)
                    ],
                    axis=0,
                ).T[:BLOCK]
                wide_grad = jnp.concatenate([grad32, jnp.zeros((KEYS - BLOCK, HW), F32)], axis=0)
                scaled = [
                    (
                        wide_grad * lepe_ref[direction, layer, pl.ds(tap_row(direction, TAPS - 1 - tap), 1), :]
                    ).astype(BF)
                    for tap in range(TAPS)
                ]
                dvalues = dvalues + dot(wide_ref[kind], jnp.concatenate(scaled, axis=0))
                dhid_ref[rows, direction * 3 * HW : direction * 3 * HW + HW] = dquery.astype(BF)
                dhid_ref[rows, direction * 3 * HW + HW : direction * 3 * HW + 2 * HW] = dkeys.astype(BF)
                dhid_ref[rows, direction * 3 * HW + 2 * HW : direction * 3 * HW + 3 * HW] = dvalues.astype(BF)
                shifted = dot(
                    tall_ref[kind], jnp.concatenate([values, jnp.zeros((KEYS - BLOCK, HW), BF)], axis=0)
                )
                for tap in range(TAPS):
                    acclepe_ref[direction, tap_row(direction, tap)] += fold_rows(
                        grad32 * shifted[tap * BLOCK : (tap + 1) * BLOCK]
                    )
                acclepe_ref[direction, TAPS] += fold_rows(grad32)
            return carry

        lax.fori_loop(0, blocks, attend, 0)

        def normalize(index, carry):
            rows = chunk_rows(index)
            turned = dot_nt(dhid_ref[rows, 3 * HW : 6 * HW], wqkv_ref[1, layer])
            turned = jnp.where(lax.rem(index, 3) < 2, swap_quads(turned), turned)
            dnormed = dot_nt(dhid_ref[rows, : 3 * HW], wqkv_ref[0, layer]) + turned
            dvalue, dgain = norm_back(dnormed, h_ref[layer, rows, :], g1_ref[pl.ds(layer, 1), :])
            acc_ref[0] += fold_rows(dgain)
            acc_ref[1] += fold_rows(dnormed)
            dh_ref[rows, :] = dh_ref[rows, :] + dvalue
            return carry

        lax.fori_loop(0, chunks, normalize, 0)
        small_ref[...] = jnp.zeros_like(small_ref)
        for direction in range(2):
            gqkv = dot_tn(normed_ref[layer, direction], dhid_ref[:, direction * 3 * HW : (direction + 1) * 3 * HW]).astype(BF)
            for piece in range(3):
                at = QKV_AT + 256 * piece
                stage_ref[direction, at : at + 256, :] = gqkv[:, piece * HW : (piece + 1) * HW]
            small_ref[direction, :10, :] = jnp.sum(acclepe_ref[direction], axis=1)
        sums = jnp.sum(acc_ref[...], axis=1)
        for piece in range(2):
            small_ref[0, 10 + 6 * piece : 16 + 6 * piece, :] = sums[:, piece * HW : (piece + 1) * HW]
        sums = jnp.sum(accff_ref[...], axis=0, keepdims=True)
        for piece in range(8):
            small_ref[1, 10 + piece : 11 + piece, :] = sums[:, piece * HW : (piece + 1) * HW]
        stage_ref[:, SMALL_AT:PACKED, :] = small_ref[...].astype(BF)

        for half in range(2):
            slot = jnp.bitwise_xor(core, half)

            def hand_out(part, carry):
                place = digits_reversed(jnp.bitwise_xor(part, mine), parts)
                at = pl.ds(pl.multiple_of(part * part_rows, 16), part_rows)
                packed_ref[slot, place, layer] = stage_ref[half, at, :]
                return carry

            lax.fori_loop(0, parts, hand_out, 0)
        return carry

    stage_ref[:, PACKED:, :] = jnp.zeros((2, stage_ref.shape[1] - PACKED, HW), BF)
    lax.fori_loop(0, LAYERS, backward, 0)

    for image in range(images):
        value = dh_ref[pl.ds(image * IMG, IMG), :]
        high = value.astype(BF)
        low = (value - high.astype(F32)).astype(BF)
        spot = pl.ds(image * TOK_IMG, TOK_IMG)
        dtok_ref[spot, :] = dot_tn(place_ref[...], high) + dot_tn(place_ref[...], low)


def digit_sizes(parts):
    sizes = []
    while parts > 1:
        size = 4 if parts % 4 == 0 else 2
        sizes.append(size)
        parts //= size
    return sizes


def digits_reversed(index, parts):
    place = 0
    for size in digit_sizes(parts):
        place = place * size + lax.rem(index, size)
        index = index // size
    return place


def unpack_kernel(
    meta,
    own_ref,
    other_ref,
    g1_ref,
    b1_ref,
    gqkv_ref,
    glepe_ref,
    glepeb_ref,
    gproj_ref,
    gbproj_ref,
    g2_ref,
    b2_ref,
    gfc1_ref,
    gbfc1_ref,
    gfc2_ref,
    gbfc2_ref,
    stage_ref,
):
    parts = own_ref.shape[0]
    part_rows = own_ref.shape[2]
    core = meta[0]
    mine = meta[1]

    for layer in range(LAYERS):

        def collect(part, carry):
            place = digits_reversed(jnp.bitwise_xor(part, mine), parts)
            at = pl.ds(pl.multiple_of(part * part_rows, 16), part_rows)
            stage_ref[core, at, :] = own_ref[place, layer]
            stage_ref[1 - core, at, :] = other_ref[place, layer]
            return carry

        lax.fori_loop(0, parts, collect, 0)
        for half in range(2):
            for piece in range(4):
                lanes = slice(half * 512 + piece * HW, half * 512 + (piece + 1) * HW)
                at = FC1_AT + 256 * piece
                gfc1_ref[layer, :, lanes] = stage_ref[half, at : at + 256, :].astype(F32)
                at = FC2_AT + 256 * piece
                gfc2_ref[layer, lanes, :] = stage_ref[half, at : at + 256, :].astype(F32).T
            gproj_ref[layer, :, half * HW : (half + 1) * HW] = stage_ref[
                half, PROJ_AT : PROJ_AT + 256, :
            ].astype(F32)
        for piece in range(3):
            at = QKV_AT + 256 * piece
            gqkv_ref[layer, 0, :, piece * HW : (piece + 1) * HW] = stage_ref[core, at : at + 256, :].astype(F32)
        small = stage_ref[core, SMALL_AT:PACKED, :].astype(F32)
        glepe_ref[layer, 0] = small[:TAPS]
        glepeb_ref[layer] = small[TAPS : TAPS + 1]
        small = stage_ref[0, SMALL_AT:PACKED, :].astype(F32)
        for place, ref in enumerate((g1_ref, b1_ref, gbproj_ref, g2_ref, b2_ref, gbfc2_ref)):
            for piece in range(2):
                row = 10 + 6 * piece + place
                ref[layer : layer + 1, piece * HW : (piece + 1) * HW] = small[row : row + 1]
        small = stage_ref[1, SMALL_AT:PACKED, :].astype(F32)
        for piece in range(8):
            gbfc1_ref[layer : layer + 1, piece * HW : (piece + 1) * HW] = small[10 + piece : 11 + piece]


SMEM = pl.BlockSpec(memory_space=pltpu.SMEM)
VMEM = pl.BlockSpec(memory_space=pltpu.VMEM)


def shards(
    dp,
    tokens,
    cotangent,
    counts,
    ln1_gain,
    ln1_bias,
    w_qkv,
    lepe_w,
    lepe_b,
    w_proj,
    b_proj,
    ln2_gain,
    ln2_bias,
    w_fc1,
    b_fc1,
    w_fc2,
    b_fc2,
):
    tokens_here = tokens.shape[0]
    images = tokens_here // TOK_IMG
    rows = images * IMG
    core = lax.axis_index("heads")
    mine = lax.axis_index("dp")
    own_counts = lax.dynamic_slice(counts, (core * images,), (images,))
    meta = jnp.concatenate([jnp.stack([core, mine]).astype(jnp.int32), own_counts])
    wqkv_all = lax.all_gather(w_qkv.reshape(LAYERS, D, 3 * HW), "heads", axis=0)
    lepe = jnp.concatenate([lepe_w[:, 0], lepe_b], axis=1)
    lepe_all = lax.all_gather(lepe, "heads", axis=0)
    part_rows = -(-PACKED // (16 * dp)) * 16
    wide, tall = shift_tables()
    table = place_table()
    scratch = [
        pltpu.VMEM((LAYERS + 1, rows, D), F32),
        pltpu.VMEM((LAYERS, 2, rows, D), BF),
        pltpu.VMEM((LAYERS, 2, rows, 3 * HW), BF),
        pltpu.VMEM((LAYERS, 2, rows, SPAN), BF),
        pltpu.VMEM((LAYERS, 2, rows, HW), F32),
        pltpu.VMEM((rows, D), F32),
        pltpu.VMEM((LAYERS, rows, D), BF),
        pltpu.VMEM((LAYERS, rows, D), F32),
        pltpu.VMEM((LAYERS, rows, D), BF),
        pltpu.VMEM((LAYERS, rows, FF), BF),
        pltpu.VMEM((LAYERS, rows, FF), BF),
        pltpu.VMEM((rows, D), F32),
        pltpu.VMEM((rows, D), BF),
        pltpu.VMEM((rows, FF), BF),
        pltpu.VMEM((6, 8, D), F32),
        pltpu.VMEM((8, FF), F32),
        pltpu.VMEM((2, TAPS + 1, 8, HW), F32),
        pltpu.VMEM((2, SMALL, HW), F32),
        pltpu.VMEM((2, part_rows * dp, HW), BF),
    ]
    result, grad, packed = pl.pallas_call(
        step_kernel,
        out_shape=(
            jax.ShapeDtypeStruct((tokens_here, D), BF),
            jax.ShapeDtypeStruct((tokens_here, D), F32),
            jax.ShapeDtypeStruct((2, dp, LAYERS, part_rows, HW), BF),
        ),
        in_specs=[SMEM] + [VMEM] * 19,
        out_specs=(VMEM,) * 3,
        scratch_shapes=scratch,
        compiler_params=pltpu.CompilerParams(vmem_limit_bytes=60 * 1024 * 1024),
        name="step",
    )(
        meta,
        tokens,
        cotangent,
        ln1_gain,
        ln1_bias,
        wqkv_all,
        lepe_all,
        w_proj,
        b_proj,
        ln2_gain,
        ln2_bias,
        w_fc1,
        b_fc1,
        w_fc2,
        b_fc2,
        jnp.asarray(table, BF),
        jnp.asarray(wide, BF),
        jnp.asarray(tall, BF),
        jnp.asarray(bias_table()),
        jnp.asarray(head_table(), BF),
    )

    def add(first, *rest):
        total = first.astype(F32)
        for item in rest:
            total = total + item.astype(F32)
        return total.astype(BF)

    swap = [(0, 1), (1, 0)]
    own = add(packed[0], lax.ppermute(packed[1], "heads", swap))
    digits = []
    stride = 1
    for size in digit_sizes(dp):
        digits.append((size, stride))
        stride *= size
    for size, stride in digits:
        pieces = own.reshape((size, own.shape[0] // size) + own.shape[1:])
        arrived = [
            lax.ppermute(pieces[step], "dp", [(i, i ^ (step * stride)) for i in range(dp)])
            for step in range(1, size)
        ]
        own = add(pieces[0], *arrived)
    for size, stride in reversed(digits):
        own = jnp.concatenate(
            [own]
            + [
                lax.ppermute(own, "dp", [(i, i ^ (step * stride)) for i in range(dp)])
                for step in range(1, size)
            ],
            axis=0,
        )
    other = lax.ppermute(own, "heads", swap)
    grads = pl.pallas_call(
        unpack_kernel,
        out_shape=(
            jax.ShapeDtypeStruct((LAYERS, D), F32),
            jax.ShapeDtypeStruct((LAYERS, D), F32),
            jax.ShapeDtypeStruct((LAYERS, 1, D, 3 * HW), F32),
            jax.ShapeDtypeStruct((LAYERS, 1, TAPS, HW), F32),
            jax.ShapeDtypeStruct((LAYERS, 1, HW), F32),
            jax.ShapeDtypeStruct((LAYERS, D, D), F32),
            jax.ShapeDtypeStruct((LAYERS, D), F32),
            jax.ShapeDtypeStruct((LAYERS, D), F32),
            jax.ShapeDtypeStruct((LAYERS, D), F32),
            jax.ShapeDtypeStruct((LAYERS, D, FF), F32),
            jax.ShapeDtypeStruct((LAYERS, FF), F32),
            jax.ShapeDtypeStruct((LAYERS, FF, D), F32),
            jax.ShapeDtypeStruct((LAYERS, D), F32),
        ),
        in_specs=[SMEM] + [VMEM] * 2,
        out_specs=(VMEM,) * 13,
        scratch_shapes=[pltpu.VMEM((2, part_rows * dp, HW), BF)],
        compiler_params=pltpu.CompilerParams(vmem_limit_bytes=48 * 1024 * 1024),
        name="unpack",
    )(meta, own, other)
    return (result, grad) + tuple(grads)


def solution(mesh):
    spread = P(("dp", "heads"), None)
    group = (P(None, "heads", None, None), P(None, "heads", None, None), P(None, "heads", None))
    in_specs = (spread, spread, P("dp"), P(), P()) + group + (P(),) * 8
    out_specs = (spread, spread, P(), P()) + group + (P(),) * 8
    return jax.shard_map(
        functools.partial(shards, mesh.shape["dp"]),
        mesh=mesh,
        in_specs=in_specs,
        out_specs=out_specs,
        check_vma=False,
    )
```

```python
import functools
import math

import jax
import jax.numpy as jnp
import numpy as np
from jax import lax
from jax.experimental import pallas as pl
from jax.experimental.pallas import tpu as pltpu
from jax.sharding import PartitionSpec as P

D = 256
FF = 1024
HD = 32
GH = 4
HW = 128
LAYERS = 2
TOK_IMG = 608
SPLIT = 392
EPSILON = 1e-05

TILE = 8
TILES = 14
BLOCK = TILES * TILE
CHUNK = 2 * BLOCK
IMG = 6 * BLOCK
KEYS = 128
SPAN = GH * KEYS
TAPS = 9
SCALE = HD**-0.5
EXP_SCALE = SCALE * math.log2(math.e)
BF = jnp.bfloat16
F32 = jnp.float32

FC1_AT = 0
FC2_AT = 1024
PROJ_AT = 2048
QKV_AT = 2304
SMALL_AT = 3072
SMALL = 32
PACKED = SMALL_AT + SMALL


def place_table():
    table = np.zeros((IMG, TOK_IMG), np.float32)
    for crop in range(2):
        for row in range(14):
            for col in range(14):
                place = crop * CHUNK + row * 16 + (col // 7) * TILE + col % 7
                table[place, crop * 196 + row * 14 + col] = 1
    for group in range(2):
        for cell in range(108):
            table[2 * CHUNK + group * BLOCK + cell, SPLIT + group * 108 + cell] = 1
    return table


def shift_tables():
    wide = np.zeros((BLOCK, TAPS * KEYS), np.float32)
    tall = np.zeros((TAPS * BLOCK, KEYS), np.float32)
    for cell in range(108):
        for tap in range(TAPS):
            row, col = (cell % 36) // 6 + tap // 3 - 1, cell % 6 + tap % 3 - 1
            if 0 <= row < 6 and 0 <= col < 6:
                other = 36 * (cell // 36) + 6 * row + col
                wide[cell, tap * KEYS + other] = 1
                tall[tap * BLOCK + cell, other] = 1
    return wide, tall


def bias_table():
    bias = np.full((2, BLOCK, KEYS), -1e30, np.float32)
    bias[0, [key for key in range(BLOCK) if key % TILE < 7]] = 0
    for query in range(KEYS):
        first, last = (36 * (query // 36), 36 * (query // 36) + 36) if query < 108 else (0, 108)
        bias[1, first:last, query] = 0
    return bias


def head_table():
    table = np.zeros((SPAN, HW), np.float32)
    for head in range(GH):
        table[head * KEYS : (head + 1) * KEYS, head * HD : (head + 1) * HD] = 1
    return table


def dot(left, right):
    return lax.dot_general(left, right, (((1,), (0,)), ((), ())), preferred_element_type=F32)


def dot_nt(left, right):
    return lax.dot_general(left, right, (((1,), (1,)), ((), ())), preferred_element_type=F32)


def dot_tn(left, right):
    return lax.dot_general(left, right, (((0,), (0,)), ((), ())), preferred_element_type=F32)


def norm_parts(value):
    center = value - jnp.mean(value, axis=-1, keepdims=True)
    scale = lax.rsqrt(jnp.mean(center * center, axis=-1, keepdims=True) + EPSILON)
    return center * scale, scale


def norm_back(dout, value, gain):
    xhat, scale = norm_parts(value)
    grown = dout * gain
    mean = jnp.mean(grown, axis=-1, keepdims=True)
    cross = jnp.mean(grown * xhat, axis=-1, keepdims=True)
    return scale * (grown - mean - xhat * cross), dout * xhat


def fold_rows(value):
    return jnp.sum(value.reshape(value.shape[0] // 8, 8, value.shape[1]), axis=0)


def head_rows(value, heads_ref):
    return jnp.concatenate(
        [value * heads_ref[head * KEYS : head * KEYS + 1, :] for head in range(GH)], axis=0
    )


def head_stack(value, heads_ref):
    rows = []
    pad = jnp.zeros((KEYS - BLOCK, HW), BF)
    for head in range(GH):
        rows.append(value * heads_ref[head * KEYS : head * KEYS + 1, :])
        rows.append(pad)
    return jnp.concatenate(rows, axis=0)


def pad_keys(value):
    return jnp.concatenate([value, jnp.zeros((KEYS - BLOCK, value.shape[1]), value.dtype)], axis=0)


def pipeline(stages, items):
    results = [None] * len(items)
    for step in range(len(items) + len(stages) - 1):
        for place in range(len(stages)):
            item = step - place
            if 0 <= item < len(items):
                results[item] = stages[place](items[item], results[item])
    return results


def split_tiles(value):
    rows = value.shape[0] // 16
    return jnp.concatenate(
        [value[16 * row : 16 * row + 8] for row in range(rows)]
        + [value[16 * row + 8 : 16 * row + 16] for row in range(rows)],
        axis=0,
    )


def join_tiles(value):
    half = value.shape[0] // 2
    pieces = []
    for row in range(half // 8):
        pieces.append(value[8 * row : 8 * row + 8])
        pieces.append(value[half + 8 * row : half + 8 * row + 8])
    return jnp.concatenate(pieces, axis=0)


def as_tiles(value):
    return value.reshape(TILES, TILE, HW)


def live_tiles():
    return lax.broadcasted_iota(jnp.int32, (1, TILE, HW), 1) < TILE - 1


def side_cells(tiles, direction):
    if direction == 1:
        return pltpu.roll(tiles, 1, 1), tiles, pltpu.roll(tiles, TILE - 1, 1)
    last = lax.broadcasted_iota(jnp.int32, (1, TILE, HW), 1) == TILE - 1
    left, right = [], []
    for row in range(TILES // 2):
        near, far = tiles[2 * row : 2 * row + 1], tiles[2 * row + 1 : 2 * row + 2]
        near_left = pltpu.roll(near, 1, 1)
        far_right = pltpu.roll(far, TILE - 1, 1)
        left += [near_left, pltpu.roll(jnp.where(last, near_left, far), 1, 1)]
        right += [pltpu.roll(jnp.where(last, far_right, near), TILE - 1, 1), far_right]
    return jnp.concatenate(left, axis=0), tiles, jnp.concatenate(right, axis=0)


def tap_cells(tiles, direction):
    stride = 2 if direction == 0 else 1
    zeros = jnp.zeros((stride, TILE, HW), F32)
    padded = [jnp.concatenate([zeros, side, zeros], axis=0) for side in side_cells(tiles, direction)]
    return [padded[tap % 3][(tap // 3) * stride : (tap // 3) * stride + TILES] for tap in range(TAPS)]


def tap_row(direction, tap):
    return tap if direction == 0 else 3 * (tap % 3) + tap // 3


def step_kernel(
    meta,
    tok_ref,
    cot_ref,
    g1_ref,
    b1_ref,
    wqkv_ref,
    lepe_ref,
    wproj_ref,
    bproj_ref,
    g2_ref,
    b2_ref,
    wfc1_ref,
    bfc1_ref,
    wfc2_ref,
    bfc2_ref,
    place_ref,
    wide_ref,
    tall_ref,
    bias_ref,
    heads_ref,
    out_ref,
    dtok_ref,
    packed_ref,
    h_ref,
    normed_ref,
    qkv_ref,
    probs_ref,
    hf_ref,
    hb_ref,
    inner_ref,
    normed2_ref,
    act_ref,
    slope_ref,
    dh_ref,
    dz_ref,
    dhid_ref,
    acc_ref,
    accff_ref,
    acclepe_ref,
    small_ref,
    stage_ref,
):
    rows_all = h_ref.shape[1]
    images = rows_all // IMG
    chunks = rows_all // CHUNK
    blocks = rows_all // BLOCK
    parts = packed_ref.shape[1]
    part_rows = packed_ref.shape[3]
    core = meta[0]
    mine = meta[1]

    def chunk_rows(index):
        return pl.ds(pl.multiple_of(index * CHUNK, 16), CHUNK)

    def chunk_tiles(index):
        return pl.ds(index * TILES, TILES)

    def block_rows(index):
        return pl.ds(pl.multiple_of(index * BLOCK, 16), BLOCK)

    def keep_of(image):
        place = lax.broadcasted_iota(jnp.int32, (IMG, 1), 0)
        limit = meta[2 + image]
        group = (place - 448) // BLOCK
        inside = (place - 448) % BLOCK
        return (place < 448) | (inside < 36 * (limit - 3 * group))

    for image in range(images):
        spot = pl.ds(image * TOK_IMG, TOK_IMG)
        h_ref[0, pl.ds(image * IMG, IMG), :] = dot(place_ref[...], tok_ref[spot, :])

    def forward(layer, carry):
        def project(index, carry):
            rows = chunk_rows(index)
            xhat, _ = norm_parts(h_ref[layer, rows, :])
            normed = xhat * g1_ref[pl.ds(layer, 1), :] + b1_ref[pl.ds(layer, 1), :]
            large = lax.rem(index, 3) < 2
            turned = jnp.where(large, split_tiles(normed), normed)
            for direction, value in enumerate((normed, turned)):
                value = value.astype(BF)
                normed_ref[layer, direction, rows, :] = value
                qkv_ref[layer, direction, rows, :] = dot(value, wqkv_ref[direction, layer]).astype(BF)
            return carry

        lax.fori_loop(0, chunks, project, 0, unroll=2)

        def tap_weight(direction, tap):
            return lepe_ref[direction, layer, pl.ds(tap_row(direction, tap), 1), :]

        def score(window, _):
            direction, rows, _, _ = window
            query = qkv_ref[layer, direction, rows, :HW]
            keyset = qkv_ref[layer, direction, rows, HW : 2 * HW]
            return dot_nt(head_rows(keyset, heads_ref), pad_keys(query))

        def weigh(window, scores):
            direction, rows, bias, _ = window
            probs = []
            for head in range(GH):
                part = scores[head * BLOCK : (head + 1) * BLOCK] + bias
                part = jnp.exp2((part - jnp.max(part, axis=0, keepdims=True)) * EXP_SCALE)
                part = part * (1.0 / jnp.sum(part, axis=0, keepdims=True))
                probs.append(part.astype(BF))
                probs_ref[layer, direction, rows, head * KEYS : (head + 1) * KEYS] = probs[head]
            return probs

        def mix(window, probs):
            direction, rows, _, _ = window
            values = qkv_ref[layer, direction, rows, 2 * HW :]
            side = values.T
            mixed = [dot(side[head * HD : (head + 1) * HD], probs[head]) for head in range(GH)]
            return jnp.concatenate(mixed, axis=0)

        def finish(window, mixed):
            direction, rows, _, block = window
            values = qkv_ref[layer, direction, rows, 2 * HW :].astype(F32)
            mixed = mixed.T[:BLOCK] + lepe_ref[direction, layer, TAPS : TAPS + 1, :]
            if block is None:
                return mixed, values
            tiles = jnp.where(live_tiles(), as_tiles(values), 0.0)
            result = as_tiles(mixed)
            for tap, cells in enumerate(tap_cells(tiles, direction)):
                result = result + cells * tap_weight(direction, tap).reshape(1, 1, HW)
            lanes = slice(direction * HW, (direction + 1) * HW)
            if direction == 0:
                hf_ref[pl.ds(block * 7, 7), :, :, lanes] = result.reshape(7, 2, TILE, HW)
            else:
                side = lax.rem(block, 2)
                hf_ref[pl.ds((block - side) * 7, TILES), side, :, lanes] = result
            return None

        stages = (score, weigh, mix, finish)

        def attend_large(index, carry):
            windows = []
            for part in range(2):
                block = 6 * (index // 2) + 2 * lax.rem(index, 2) + part
                windows += [(direction, block_rows(block), bias_ref[0], block) for direction in range(2)]
            pipeline(stages, windows)
            return carry

        lax.fori_loop(0, images * 2, attend_large, 0)

        def attend_small(index, carry):
            windows = []
            for part in range(2):
                rows = block_rows(6 * index + 4 + part)
                windows += [(direction, rows, bias_ref[1], None) for direction in range(2)]
            results = pipeline(stages, windows)
            for part in range(2):
                mixed, scaled = [], []
                for direction in range(2):
                    some, values = results[2 * part + direction]
                    mixed.append(some)
                    padded = pad_keys(values)
                    scaled.append(
                        jnp.concatenate(
                            [(padded * tap_weight(direction, tap)).astype(BF) for tap in range(TAPS)], axis=0
                        )
                    )
                local = dot(wide_ref[...], jnp.concatenate(scaled, axis=1))
                result = jnp.concatenate(mixed, axis=1) + local
                hf_ref[pl.ds((6 * index + 4 + part) * 7, 7)] = result.reshape(7, 2, TILE, D)
            return carry

        lax.fori_loop(0, images, attend_small, 0)

        def feed(index, carry):
            rows = chunk_rows(index)
            heads = hf_ref[chunk_tiles(index)].reshape(CHUNK, D).astype(BF)
            hb_ref[layer, rows, :] = heads
            inner = h_ref[layer, rows, :] + dot(heads, wproj_ref[layer]) + bproj_ref[pl.ds(layer, 1), :]
            inner_ref[layer, rows, :] = inner
            xhat, _ = norm_parts(inner)
            normed2 = (xhat * g2_ref[pl.ds(layer, 1), :] + b2_ref[pl.ds(layer, 1), :]).astype(BF)
            normed2_ref[layer, rows, :] = normed2
            hidden = dot(normed2, wfc1_ref[layer]) + bfc1_ref[pl.ds(layer, 1), :]
            cdf = 0.5 + 0.5 * lax.erf(hidden * math.sqrt(0.5))
            act = (hidden * cdf).astype(BF)
            act_ref[layer, rows, :] = act
            slope = cdf + hidden * jnp.exp2(hidden * hidden * (-0.5 * math.log2(math.e))) * (1.0 / math.sqrt(2 * math.pi))
            slope_ref[layer, rows, :] = slope.astype(BF)
            h_ref[layer + 1, rows, :] = inner + dot(act, wfc2_ref[layer]) + bfc2_ref[pl.ds(layer, 1), :]
            return carry

        lax.fori_loop(0, chunks, feed, 0, unroll=2)
        return carry

    lax.fori_loop(0, LAYERS, forward, 0)

    for image in range(images):
        spot = pl.ds(image * TOK_IMG, TOK_IMG)
        wide = pl.ds(image * IMG, IMG)
        keep = keep_of(image)
        result = jnp.where(keep, h_ref[LAYERS, wide, :], 0.0).astype(BF)
        out_ref[spot, :] = dot_tn(place_ref[...], result).astype(BF)
        dh_ref[wide, :] = jnp.where(keep, dot(place_ref[...], cot_ref[spot, :]), 0.0)

    def backward(step, carry):
        layer = LAYERS - 1 - step
        acc_ref[...] = jnp.zeros_like(acc_ref)
        accff_ref[...] = jnp.zeros_like(accff_ref)
        acclepe_ref[...] = jnp.zeros_like(acclepe_ref)

        def feed(index, carry):
            rows = chunk_rows(index)
            grad = dh_ref[rows, :]
            dz = grad.astype(BF)
            dz_ref[rows, :] = dz
            acc_ref[5] += fold_rows(dz.astype(F32))
            dhid = (dot_nt(dz, wfc2_ref[layer]) * slope_ref[layer, rows, :].astype(F32)).astype(BF)
            dhid_ref[rows, :] = dhid
            accff_ref[...] += fold_rows(dhid.astype(F32))
            dnormed = dot_nt(dhid, wfc1_ref[layer])
            dvalue, dgain = norm_back(dnormed, inner_ref[layer, rows, :], g2_ref[pl.ds(layer, 1), :])
            acc_ref[3] += fold_rows(dgain)
            acc_ref[4] += fold_rows(dnormed)
            dinner = grad + dvalue
            dh_ref[rows, :] = dinner
            return carry

        lax.fori_loop(0, chunks, feed, 0, unroll=2)

        def feed_weights(index, carry):
            cols = pl.ds(pl.multiple_of(index * 256, 256), 256)
            half = index // 2
            first = dot_tn(normed2_ref[layer], dhid_ref[:, cols]).astype(BF)
            second = dot_tn(dz_ref[...], act_ref[layer, :, cols]).astype(BF)
            for piece in range(2):
                at = pl.multiple_of((lax.rem(index, 2) * 2 + piece) * 256, 256)
                lanes = slice(piece * HW, (piece + 1) * HW)
                stage_ref[half, pl.ds(FC1_AT + at, 256), :] = first[:, lanes]
                stage_ref[half, pl.ds(FC2_AT + at, 256), :] = second[:, lanes]
            return carry

        lax.fori_loop(0, 4, feed_weights, 0)

        def project(index, carry):
            rows = chunk_rows(index)
            dy = dh_ref[rows, :].astype(BF)
            dz_ref[rows, :] = dy
            acc_ref[2] += fold_rows(dy.astype(F32))
            hf_ref[chunk_tiles(index)] = dot_nt(dy, wproj_ref[layer]).reshape(TILES, 2, TILE, D)
            return carry

        lax.fori_loop(0, chunks, project, 0, unroll=2)
        gproj = dot_tn(hb_ref[layer], dz_ref[...]).astype(BF)
        for half in range(2):
            stage_ref[half, PROJ_AT : PROJ_AT + D, :] = gproj[:, half * HW : (half + 1) * HW]

        def tap_weight(direction, tap):
            return lepe_ref[direction, layer, pl.ds(tap_row(direction, tap), 1), :]

        def score(window, _):
            direction, rows, grad, _ = window
            values = qkv_ref[layer, direction, rows, 2 * HW :]
            return dot_nt(head_rows(values, heads_ref), pad_keys(grad))

        def weigh(window, dprobs):
            direction, rows, _, _ = window
            dscores = []
            for head in range(GH):
                part = probs_ref[layer, direction, rows, head * KEYS : (head + 1) * KEYS].astype(F32)
                dpart = dprobs[head * BLOCK : (head + 1) * BLOCK]
                inner = jnp.sum(part * dpart, axis=0, keepdims=True)
                dscores.append((part * (dpart - inner)).astype(BF))
            return dscores

        def mix(window, dscores):
            direction, rows, grad, _ = window
            query = qkv_ref[layer, direction, rows, :HW]
            side = qkv_ref[layer, direction, rows, HW : 2 * HW].T
            dkeys = dot(jnp.concatenate(dscores, axis=1), head_stack(query, heads_ref))
            dvalues = dot(probs_ref[layer, direction, rows, :], head_stack(grad, heads_ref))
            dquery = [dot(side[head * HD : (head + 1) * HD], dscores[head]) for head in range(GH)]
            return jnp.concatenate(dquery, axis=0), dkeys, dvalues

        def finish(window, results):
            direction, rows, grad, block = window
            dquery, dkeys, dvalues = results
            values = qkv_ref[layer, direction, rows, 2 * HW :]
            first = direction * 3 * HW
            dhid_ref[rows, first : first + HW] = (dquery * SCALE).T[:BLOCK].astype(BF)
            dhid_ref[rows, first + HW : first + 2 * HW] = (dkeys * SCALE).astype(BF)
            if block is None:
                return values, dvalues
            grad_tiles = as_tiles(grad.astype(F32))
            result = as_tiles(dvalues)
            for tap, cells in enumerate(tap_cells(grad_tiles, direction)):
                result = result + cells * tap_weight(direction, TAPS - 1 - tap).reshape(1, 1, HW)
            result = jnp.where(live_tiles(), result, 0.0).reshape(BLOCK, HW)
            dhid_ref[rows, first + 2 * HW : first + 3 * HW] = result.astype(BF)
            tiles = jnp.where(live_tiles(), as_tiles(values.astype(F32)), 0.0)
            for tap, cells in enumerate(tap_cells(tiles, direction)):
                acclepe_ref[direction, tap_row(direction, tap)] += jnp.sum(grad_tiles * cells, axis=0)
            acclepe_ref[direction, TAPS] += jnp.sum(grad_tiles, axis=0)
            return None

        stages = (score, weigh, mix, finish)

        def attend_large(index, carry):
            windows = []
            for part in range(2):
                block = 6 * (index // 2) + 2 * lax.rem(index, 2) + part
                for direction in range(2):
                    lanes = slice(direction * HW, (direction + 1) * HW)
                    if direction == 0:
                        tiles = hf_ref[pl.ds(block * 7, 7), :, :, lanes]
                    else:
                        side = lax.rem(block, 2)
                        tiles = hf_ref[pl.ds((block - side) * 7, TILES), side, :, lanes]
                    windows.append((direction, block_rows(block), tiles.reshape(BLOCK, HW).astype(BF), block))
            pipeline(stages, windows)
            return carry

        lax.fori_loop(0, images * 2, attend_large, 0)

        def attend_small(index, carry):
            windows = []
            for part in range(2):
                block = 6 * index + 4 + part
                tiles = hf_ref[pl.ds(block * 7, 7)].reshape(BLOCK, D)
                for direction in range(2):
                    grad = tiles[:, direction * HW : (direction + 1) * HW].astype(BF)
                    windows.append((direction, block_rows(block), grad, None))
            results = pipeline(stages, windows)
            for part in range(2):
                rows = windows[2 * part][1]
                grads = [windows[2 * part + direction][2].astype(F32) for direction in range(2)]
                scaled = []
                for direction in range(2):
                    padded = pad_keys(grads[direction])
                    scaled.append(
                        jnp.concatenate(
                            [
                                (padded * tap_weight(direction, TAPS - 1 - tap)).astype(BF)
                                for tap in range(TAPS)
                            ],
                            axis=0,
                        )
                    )
                local = dot(wide_ref[...], jnp.concatenate(scaled, axis=1))
                shifted = dot(
                    tall_ref[...],
                    jnp.concatenate([pad_keys(results[2 * part + direction][0]) for direction in range(2)], axis=1),
                )
                for direction in range(2):
                    lanes = slice(direction * HW, (direction + 1) * HW)
                    first = direction * 3 * HW + 2 * HW
                    dvalues = results[2 * part + direction][1] + local[:, lanes]
                    dhid_ref[rows, first : first + HW] = dvalues.astype(BF)
                    for tap in range(TAPS):
                        acclepe_ref[direction, tap_row(direction, tap)] += fold_rows(
                            grads[direction] * shifted[tap * BLOCK : (tap + 1) * BLOCK, lanes]
                        )
                    acclepe_ref[direction, TAPS] += fold_rows(grads[direction])
            return carry

        lax.fori_loop(0, images, attend_small, 0)

        def normalize(index, carry):
            rows = chunk_rows(index)
            turned = dot_nt(dhid_ref[rows, 3 * HW : 6 * HW], wqkv_ref[1, layer])
            turned = jnp.where(lax.rem(index, 3) < 2, join_tiles(turned), turned)
            dnormed = dot_nt(dhid_ref[rows, : 3 * HW], wqkv_ref[0, layer]) + turned
            dvalue, dgain = norm_back(dnormed, h_ref[layer, rows, :], g1_ref[pl.ds(layer, 1), :])
            acc_ref[0] += fold_rows(dgain)
            acc_ref[1] += fold_rows(dnormed)
            dh_ref[rows, :] = dh_ref[rows, :] + dvalue
            return carry

        lax.fori_loop(0, chunks, normalize, 0, unroll=2)
        small_ref[...] = jnp.zeros_like(small_ref)
        for direction in range(2):
            gqkv = dot_tn(normed_ref[layer, direction], dhid_ref[:, direction * 3 * HW : (direction + 1) * 3 * HW]).astype(BF)
            for piece in range(3):
                at = QKV_AT + 256 * piece
                stage_ref[direction, at : at + 256, :] = gqkv[:, piece * HW : (piece + 1) * HW]
            small_ref[direction, :10, :] = jnp.sum(acclepe_ref[direction], axis=1)
        sums = jnp.sum(acc_ref[...], axis=1)
        for piece in range(2):
            small_ref[0, 10 + 6 * piece : 16 + 6 * piece, :] = sums[:, piece * HW : (piece + 1) * HW]
        sums = jnp.sum(accff_ref[...], axis=0, keepdims=True)
        for piece in range(8):
            small_ref[1, 10 + piece : 11 + piece, :] = sums[:, piece * HW : (piece + 1) * HW]
        stage_ref[:, SMALL_AT:PACKED, :] = small_ref[...].astype(BF)

        for half in range(2):
            slot = jnp.bitwise_xor(core, half)

            def hand_out(part, carry):
                place = digits_reversed(jnp.bitwise_xor(part, mine), parts)
                at = pl.ds(pl.multiple_of(part * part_rows, 16), part_rows)
                packed_ref[slot, place, layer] = stage_ref[half, at, :]
                return carry

            lax.fori_loop(0, parts, hand_out, 0)
        return carry

    stage_ref[:, PACKED:, :] = jnp.zeros((2, stage_ref.shape[1] - PACKED, HW), BF)
    lax.fori_loop(0, LAYERS, backward, 0)

    for image in range(images):
        value = dh_ref[pl.ds(image * IMG, IMG), :]
        high = value.astype(BF)
        low = (value - high.astype(F32)).astype(BF)
        spot = pl.ds(image * TOK_IMG, TOK_IMG)
        dtok_ref[spot, :] = dot_tn(place_ref[...], high) + dot_tn(place_ref[...], low)


def digit_sizes(parts):
    sizes = []
    while parts > 1:
        size = 4 if parts % 4 == 0 else 2
        sizes.append(size)
        parts //= size
    return sizes


def digits_reversed(index, parts):
    place = 0
    for size in digit_sizes(parts):
        place = place * size + lax.rem(index, size)
        index = index // size
    return place


def unpack_kernel(
    meta,
    own_ref,
    other_ref,
    g1_ref,
    b1_ref,
    gqkv_ref,
    glepe_ref,
    glepeb_ref,
    gproj_ref,
    gbproj_ref,
    g2_ref,
    b2_ref,
    gfc1_ref,
    gbfc1_ref,
    gfc2_ref,
    gbfc2_ref,
    stage_ref,
):
    parts = own_ref.shape[0]
    part_rows = own_ref.shape[2]
    core = meta[0]
    mine = meta[1]

    for layer in range(LAYERS):

        def collect(part, carry):
            place = digits_reversed(jnp.bitwise_xor(part, mine), parts)
            at = pl.ds(pl.multiple_of(part * part_rows, 16), part_rows)
            stage_ref[core, at, :] = own_ref[place, layer]
            stage_ref[1 - core, at, :] = other_ref[place, layer]
            return carry

        lax.fori_loop(0, parts, collect, 0)
        for half in range(2):
            for piece in range(4):
                lanes = slice(half * 512 + piece * HW, half * 512 + (piece + 1) * HW)
                at = FC1_AT + 256 * piece
                gfc1_ref[layer, :, lanes] = stage_ref[half, at : at + 256, :].astype(F32)
                at = FC2_AT + 256 * piece
                gfc2_ref[layer, lanes, :] = stage_ref[half, at : at + 256, :].astype(F32).T
            gproj_ref[layer, :, half * HW : (half + 1) * HW] = stage_ref[
                half, PROJ_AT : PROJ_AT + 256, :
            ].astype(F32)
        for piece in range(3):
            at = QKV_AT + 256 * piece
            gqkv_ref[layer, 0, :, piece * HW : (piece + 1) * HW] = stage_ref[core, at : at + 256, :].astype(F32)
        small = stage_ref[core, SMALL_AT:PACKED, :].astype(F32)
        glepe_ref[layer, 0] = small[:TAPS]
        glepeb_ref[layer] = small[TAPS : TAPS + 1]
        small = stage_ref[0, SMALL_AT:PACKED, :].astype(F32)
        for place, ref in enumerate((g1_ref, b1_ref, gbproj_ref, g2_ref, b2_ref, gbfc2_ref)):
            for piece in range(2):
                row = 10 + 6 * piece + place
                ref[layer : layer + 1, piece * HW : (piece + 1) * HW] = small[row : row + 1]
        small = stage_ref[1, SMALL_AT:PACKED, :].astype(F32)
        for piece in range(8):
            gbfc1_ref[layer : layer + 1, piece * HW : (piece + 1) * HW] = small[10 + piece : 11 + piece]


SMEM = pl.BlockSpec(memory_space=pltpu.SMEM)
VMEM = pl.BlockSpec(memory_space=pltpu.VMEM)


def shards(
    dp,
    tokens,
    cotangent,
    counts,
    ln1_gain,
    ln1_bias,
    w_qkv,
    lepe_w,
    lepe_b,
    w_proj,
    b_proj,
    ln2_gain,
    ln2_bias,
    w_fc1,
    b_fc1,
    w_fc2,
    b_fc2,
):
    tokens_here = tokens.shape[0]
    images = tokens_here // TOK_IMG
    rows = images * IMG
    core = lax.axis_index("heads")
    mine = lax.axis_index("dp")
    own_counts = lax.dynamic_slice(counts, (core * images,), (images,))
    meta = jnp.concatenate([jnp.stack([core, mine]).astype(jnp.int32), own_counts])
    wqkv_all = lax.all_gather(w_qkv.reshape(LAYERS, D, 3 * HW), "heads", axis=0)
    lepe = jnp.concatenate([lepe_w[:, 0], lepe_b], axis=1)
    lepe_all = lax.all_gather(lepe, "heads", axis=0)
    part_rows = -(-PACKED // (16 * dp)) * 16
    wide, tall = shift_tables()
    table = place_table()
    scratch = [
        pltpu.VMEM((LAYERS + 1, rows, D), F32),
        pltpu.VMEM((LAYERS, 2, rows, D), BF),
        pltpu.VMEM((LAYERS, 2, rows, 3 * HW), BF),
        pltpu.VMEM((LAYERS, 2, rows, SPAN), BF),
        pltpu.VMEM((rows // 16, 2, TILE, D), F32),
        pltpu.VMEM((LAYERS, rows, D), BF),
        pltpu.VMEM((LAYERS, rows, D), F32),
        pltpu.VMEM((LAYERS, rows, D), BF),
        pltpu.VMEM((LAYERS, rows, FF), BF),
        pltpu.VMEM((LAYERS, rows, FF), BF),
        pltpu.VMEM((rows, D), F32),
        pltpu.VMEM((rows, D), BF),
        pltpu.VMEM((rows, FF), BF),
        pltpu.VMEM((6, 8, D), F32),
        pltpu.VMEM((8, FF), F32),
        pltpu.VMEM((2, TAPS + 1, 8, HW), F32),
        pltpu.VMEM((2, SMALL, HW), F32),
        pltpu.VMEM((2, part_rows * dp, HW), BF),
    ]
    result, grad, packed = pl.pallas_call(
        step_kernel,
        out_shape=(
            jax.ShapeDtypeStruct((tokens_here, D), BF),
            jax.ShapeDtypeStruct((tokens_here, D), F32),
            jax.ShapeDtypeStruct((2, dp, LAYERS, part_rows, HW), BF),
        ),
        in_specs=[SMEM] + [VMEM] * 19,
        out_specs=(VMEM,) * 3,
        scratch_shapes=scratch,
        compiler_params=pltpu.CompilerParams(vmem_limit_bytes=60 * 1024 * 1024),
        name="step",
    )(
        meta,
        tokens,
        cotangent,
        ln1_gain,
        ln1_bias,
        wqkv_all,
        lepe_all,
        w_proj,
        b_proj,
        ln2_gain,
        ln2_bias,
        w_fc1,
        b_fc1,
        w_fc2,
        b_fc2,
        jnp.asarray(table, BF),
        jnp.asarray(wide, BF),
        jnp.asarray(tall, BF),
        jnp.asarray(bias_table()),
        jnp.asarray(head_table(), BF),
    )

    def add(first, *rest):
        total = first.astype(F32)
        for item in rest:
            total = total + item.astype(F32)
        return total.astype(BF)

    swap = [(0, 1), (1, 0)]
    own = add(packed[0], lax.ppermute(packed[1], "heads", swap))
    digits = []
    stride = 1
    for size in digit_sizes(dp):
        digits.append((size, stride))
        stride *= size
    for size, stride in digits:
        pieces = own.reshape((size, own.shape[0] // size) + own.shape[1:])
        arrived = [
            lax.ppermute(pieces[step], "dp", [(i, i ^ (step * stride)) for i in range(dp)])
            for step in range(1, size)
        ]
        own = add(pieces[0], *arrived)
    for size, stride in reversed(digits):
        own = jnp.concatenate(
            [own]
            + [
                lax.ppermute(own, "dp", [(i, i ^ (step * stride)) for i in range(dp)])
                for step in range(1, size)
            ],
            axis=0,
        )
    other = lax.ppermute(own, "heads", swap)
    grads = pl.pallas_call(
        unpack_kernel,
        out_shape=(
            jax.ShapeDtypeStruct((LAYERS, D), F32),
            jax.ShapeDtypeStruct((LAYERS, D), F32),
            jax.ShapeDtypeStruct((LAYERS, 1, D, 3 * HW), F32),
            jax.ShapeDtypeStruct((LAYERS, 1, TAPS, HW), F32),
            jax.ShapeDtypeStruct((LAYERS, 1, HW), F32),
            jax.ShapeDtypeStruct((LAYERS, D, D), F32),
            jax.ShapeDtypeStruct((LAYERS, D), F32),
            jax.ShapeDtypeStruct((LAYERS, D), F32),
            jax.ShapeDtypeStruct((LAYERS, D), F32),
            jax.ShapeDtypeStruct((LAYERS, D, FF), F32),
            jax.ShapeDtypeStruct((LAYERS, FF), F32),
            jax.ShapeDtypeStruct((LAYERS, FF, D), F32),
            jax.ShapeDtypeStruct((LAYERS, D), F32),
        ),
        in_specs=[SMEM] + [VMEM] * 2,
        out_specs=(VMEM,) * 13,
        scratch_shapes=[pltpu.VMEM((2, part_rows * dp, HW), BF)],
        compiler_params=pltpu.CompilerParams(vmem_limit_bytes=48 * 1024 * 1024),
        name="unpack",
    )(meta, own, other)
    return (result, grad) + tuple(grads)


def solution(mesh):
    spread = P(("dp", "heads"), None)
    group = (P(None, "heads", None, None), P(None, "heads", None, None), P(None, "heads", None))
    in_specs = (spread, spread, P("dp"), P(), P()) + group + (P(),) * 8
    out_specs = (spread, spread, P(), P()) + group + (P(),) * 8
    return jax.shard_map(
        functools.partial(shards, mesh.shape["dp"]),
        mesh=mesh,
        in_specs=in_specs,
        out_specs=out_specs,
        check_vma=False,
    )
```

```python
import functools
import math

import jax
import jax.numpy as jnp
import numpy as np
from jax import lax
from jax.experimental import pallas as pl
from jax.experimental.pallas import tpu as pltpu
from jax.sharding import PartitionSpec as P

D = 256
FF = 1024
HD = 32
GH = 4
HW = 128
LAYERS = 2
TOK_IMG = 608
SPLIT = 392
EPSILON = 1e-05

TILE = 8
TILES = 14
BLOCK = TILES * TILE
CHUNK = 2 * BLOCK
IMG = 6 * BLOCK
KEYS = 128
SPAN = GH * KEYS
TAPS = 9
SCALE = HD**-0.5
EXP_SCALE = SCALE * math.log2(math.e)
BF = jnp.bfloat16
F32 = jnp.float32

FC1_AT = 0
FC2_AT = 1024
PROJ_AT = 2048
QKV_AT = 2304
SMALL_AT = 3072
SMALL = 32
PACKED = SMALL_AT + SMALL
ALL_PACKED = LAYERS * PACKED


def place_table():
    table = np.zeros((IMG, TOK_IMG), np.float32)
    for crop in range(2):
        for row in range(14):
            for col in range(14):
                place = crop * CHUNK + row * 16 + (col // 7) * TILE + col % 7
                table[place, crop * 196 + row * 14 + col] = 1
    for group in range(2):
        for cell in range(108):
            table[2 * CHUNK + group * BLOCK + cell, SPLIT + group * 108 + cell] = 1
    return table


def shift_tables():
    wide = np.zeros((BLOCK, TAPS * KEYS), np.float32)
    tall = np.zeros((TAPS * BLOCK, KEYS), np.float32)
    for cell in range(108):
        for tap in range(TAPS):
            row, col = (cell % 36) // 6 + tap // 3 - 1, cell % 6 + tap % 3 - 1
            if 0 <= row < 6 and 0 <= col < 6:
                other = 36 * (cell // 36) + 6 * row + col
                wide[cell, tap * KEYS + other] = 1
                tall[tap * BLOCK + cell, other] = 1
    return wide, tall


def bias_table():
    bias = np.full((2, BLOCK, KEYS), -1e30, np.float32)
    bias[0, [key for key in range(BLOCK) if key % TILE < 7]] = 0
    for query in range(KEYS):
        first, last = (36 * (query // 36), 36 * (query // 36) + 36) if query < 108 else (0, 108)
        bias[1, first:last, query] = 0
    return bias


def head_table():
    table = np.zeros((SPAN, HW), np.float32)
    for head in range(GH):
        table[head * KEYS : (head + 1) * KEYS, head * HD : (head + 1) * HD] = 1
    return table


def dot(left, right):
    return lax.dot_general(left, right, (((1,), (0,)), ((), ())), preferred_element_type=F32)


def dot_nt(left, right):
    return lax.dot_general(left, right, (((1,), (1,)), ((), ())), preferred_element_type=F32)


def dot_tn(left, right):
    return lax.dot_general(left, right, (((0,), (0,)), ((), ())), preferred_element_type=F32)


def norm_parts(value):
    center = value - jnp.mean(value, axis=-1, keepdims=True)
    scale = lax.rsqrt(jnp.mean(center * center, axis=-1, keepdims=True) + EPSILON)
    return center * scale, scale


def norm_back(dout, value, gain):
    xhat, scale = norm_parts(value)
    grown = dout * gain
    mean = jnp.mean(grown, axis=-1, keepdims=True)
    cross = jnp.mean(grown * xhat, axis=-1, keepdims=True)
    return scale * (grown - mean - xhat * cross), dout * xhat


def fold_rows(value):
    return jnp.sum(value.reshape(value.shape[0] // 8, 8, value.shape[1]), axis=0)


def head_rows(value, heads_ref):
    return jnp.concatenate(
        [value * heads_ref[head * KEYS : head * KEYS + 1, :] for head in range(GH)], axis=0
    )


def head_stack(value, heads_ref):
    rows = []
    pad = jnp.zeros((KEYS - BLOCK, HW), BF)
    for head in range(GH):
        rows.append(value * heads_ref[head * KEYS : head * KEYS + 1, :])
        rows.append(pad)
    return jnp.concatenate(rows, axis=0)


def pad_keys(value):
    return jnp.concatenate([value, jnp.zeros((KEYS - BLOCK, value.shape[1]), value.dtype)], axis=0)


def pipeline(stages, items):
    results = [None] * len(items)
    for step in range(len(items) + len(stages) - 1):
        for place in range(len(stages)):
            item = step - place
            if 0 <= item < len(items):
                results[item] = stages[place](items[item], results[item])
    return results


def split_tiles(value):
    rows = value.shape[0] // 16
    return jnp.concatenate(
        [value[16 * row : 16 * row + 8] for row in range(rows)]
        + [value[16 * row + 8 : 16 * row + 16] for row in range(rows)],
        axis=0,
    )


def join_tiles(value):
    half = value.shape[0] // 2
    pieces = []
    for row in range(half // 8):
        pieces.append(value[8 * row : 8 * row + 8])
        pieces.append(value[half + 8 * row : half + 8 * row + 8])
    return jnp.concatenate(pieces, axis=0)


def as_tiles(value):
    return value.reshape(TILES, TILE, HW)


def live_tiles():
    return lax.broadcasted_iota(jnp.int32, (1, TILE, HW), 1) < TILE - 1


def side_cells(tiles, direction):
    if direction == 1:
        return pltpu.roll(tiles, 1, 1), tiles, pltpu.roll(tiles, TILE - 1, 1)
    last = lax.broadcasted_iota(jnp.int32, (1, TILE, HW), 1) == TILE - 1
    left, right = [], []
    for row in range(TILES // 2):
        near, far = tiles[2 * row : 2 * row + 1], tiles[2 * row + 1 : 2 * row + 2]
        near_left = pltpu.roll(near, 1, 1)
        far_right = pltpu.roll(far, TILE - 1, 1)
        left += [near_left, pltpu.roll(jnp.where(last, near_left, far), 1, 1)]
        right += [pltpu.roll(jnp.where(last, far_right, near), TILE - 1, 1), far_right]
    return jnp.concatenate(left, axis=0), tiles, jnp.concatenate(right, axis=0)


def tap_cells(tiles, direction):
    stride = 2 if direction == 0 else 1
    zeros = jnp.zeros((stride, TILE, HW), F32)
    padded = [jnp.concatenate([zeros, side, zeros], axis=0) for side in side_cells(tiles, direction)]
    return [padded[tap % 3][(tap // 3) * stride : (tap // 3) * stride + TILES] for tap in range(TAPS)]


def tap_row(direction, tap):
    return tap if direction == 0 else 3 * (tap % 3) + tap // 3


def step_kernel(
    counts_ref,
    tok_ref,
    cot_ref,
    g1_ref,
    b1_ref,
    own_wqkv_ref,
    other_wqkv_ref,
    own_lepe_ref,
    other_lepe_ref,
    own_lepeb_ref,
    other_lepeb_ref,
    wproj_ref,
    bproj_ref,
    g2_ref,
    b2_ref,
    wfc1_ref,
    bfc1_ref,
    wfc2_ref,
    bfc2_ref,
    place_ref,
    wide_ref,
    tall_ref,
    bias_ref,
    heads_ref,
    out_ref,
    dtok_ref,
    keep_first_ref,
    keep_second_ref,
    send_first_ref,
    send_second_ref,
    wqkv_ref,
    lepe_ref,
    h_ref,
    normed_ref,
    qkv_ref,
    probs_ref,
    hf_ref,
    hb_ref,
    inner_ref,
    normed2_ref,
    act_ref,
    slope_ref,
    dh_ref,
    dz_ref,
    dhid_ref,
    acc_ref,
    accff_ref,
    acclepe_ref,
    small_ref,
    stage_ref,
):
    rows_all = h_ref.shape[1]
    images = rows_all // IMG
    chunks = rows_all // CHUNK
    blocks = rows_all // BLOCK
    parts = keep_first_ref.shape[0]
    first_rows = keep_first_ref.shape[1]
    second_rows = keep_second_ref.shape[1]
    part_rows = first_rows + second_rows
    core = lax.axis_index("heads")
    mine = lax.axis_index("dp")
    for direction, (wqkv, lepe, lepeb) in (
        (core, (own_wqkv_ref, own_lepe_ref, own_lepeb_ref)),
        (1 - core, (other_wqkv_ref, other_lepe_ref, other_lepeb_ref)),
    ):
        wqkv_ref[direction] = wqkv[:, 0]
        lepe_ref[direction, :, :TAPS] = lepe[:, 0]
        lepe_ref[direction, :, TAPS : TAPS + 1] = lepeb[...]

    def chunk_rows(index):
        return pl.ds(pl.multiple_of(index * CHUNK, 16), CHUNK)

    def chunk_tiles(index):
        return pl.ds(index * TILES, TILES)

    def block_rows(index):
        return pl.ds(pl.multiple_of(index * BLOCK, 16), BLOCK)

    def keep_of(image):
        place = lax.broadcasted_iota(jnp.int32, (IMG, 1), 0)
        limit = counts_ref[core * images + image]
        group = (place - 448) // BLOCK
        inside = (place - 448) % BLOCK
        return (place < 448) | (inside < 36 * (limit - 3 * group))

    for image in range(images):
        spot = pl.ds(image * TOK_IMG, TOK_IMG)
        h_ref[0, pl.ds(image * IMG, IMG), :] = dot(place_ref[...], tok_ref[spot, :])

    def forward(layer, carry):
        def project(index, carry):
            rows = chunk_rows(index)
            xhat, _ = norm_parts(h_ref[layer, rows, :])
            normed = xhat * g1_ref[pl.ds(layer, 1), :] + b1_ref[pl.ds(layer, 1), :]
            large = lax.rem(index, 3) < 2
            turned = jnp.where(large, split_tiles(normed), normed)
            for direction, value in enumerate((normed, turned)):
                value = value.astype(BF)
                normed_ref[layer, direction, rows, :] = value
                qkv_ref[layer, direction, rows, :] = dot(value, wqkv_ref[direction, layer]).astype(BF)
            return carry

        lax.fori_loop(0, chunks, project, 0, unroll=2)

        def tap_weight(direction, tap):
            return lepe_ref[direction, layer, pl.ds(tap_row(direction, tap), 1), :]

        def score(window, _):
            direction, rows, _, _ = window
            query = qkv_ref[layer, direction, rows, :HW]
            keyset = qkv_ref[layer, direction, rows, HW : 2 * HW]
            return dot_nt(head_rows(keyset, heads_ref), pad_keys(query))

        def weigh(window, scores):
            direction, rows, bias, _ = window
            probs = []
            for head in range(GH):
                part = scores[head * BLOCK : (head + 1) * BLOCK] + bias
                part = jnp.exp2((part - jnp.max(part, axis=0, keepdims=True)) * EXP_SCALE)
                part = part * (1.0 / jnp.sum(part, axis=0, keepdims=True))
                probs.append(part.astype(BF))
                probs_ref[layer, direction, rows, head * KEYS : (head + 1) * KEYS] = probs[head]
            return probs

        def mix(window, probs):
            direction, rows, _, _ = window
            values = qkv_ref[layer, direction, rows, 2 * HW :]
            side = values.T
            mixed = [dot(side[head * HD : (head + 1) * HD], probs[head]) for head in range(GH)]
            return jnp.concatenate(mixed, axis=0)

        def finish(window, mixed):
            direction, rows, _, block = window
            values = qkv_ref[layer, direction, rows, 2 * HW :].astype(F32)
            mixed = mixed.T[:BLOCK] + lepe_ref[direction, layer, TAPS : TAPS + 1, :]
            if block is None:
                return mixed, values
            tiles = jnp.where(live_tiles(), as_tiles(values), 0.0)
            result = as_tiles(mixed)
            for tap, cells in enumerate(tap_cells(tiles, direction)):
                result = result + cells * tap_weight(direction, tap).reshape(1, 1, HW)
            lanes = slice(direction * HW, (direction + 1) * HW)
            if direction == 0:
                hf_ref[pl.ds(block * 7, 7), :, :, lanes] = result.reshape(7, 2, TILE, HW)
            else:
                side = lax.rem(block, 2)
                hf_ref[pl.ds((block - side) * 7, TILES), side, :, lanes] = result
            return None

        stages = (score, weigh, mix, finish)

        def attend_large(index, carry):
            windows = []
            for part in range(2):
                block = 6 * (index // 2) + 2 * lax.rem(index, 2) + part
                windows += [(direction, block_rows(block), bias_ref[0], block) for direction in range(2)]
            pipeline(stages, windows)
            return carry

        lax.fori_loop(0, images * 2, attend_large, 0)

        def attend_small(index, carry):
            windows = []
            for part in range(2):
                rows = block_rows(6 * index + 4 + part)
                windows += [(direction, rows, bias_ref[1], None) for direction in range(2)]
            results = pipeline(stages, windows)
            for part in range(2):
                mixed, scaled = [], []
                for direction in range(2):
                    some, values = results[2 * part + direction]
                    mixed.append(some)
                    padded = pad_keys(values)
                    scaled.append(
                        jnp.concatenate(
                            [(padded * tap_weight(direction, tap)).astype(BF) for tap in range(TAPS)], axis=0
                        )
                    )
                local = dot(wide_ref[...], jnp.concatenate(scaled, axis=1))
                result = jnp.concatenate(mixed, axis=1) + local
                hf_ref[pl.ds((6 * index + 4 + part) * 7, 7)] = result.reshape(7, 2, TILE, D)
            return carry

        lax.fori_loop(0, images, attend_small, 0)

        def feed(index, carry):
            rows = chunk_rows(index)
            heads = hf_ref[chunk_tiles(index)].reshape(CHUNK, D).astype(BF)
            hb_ref[layer, rows, :] = heads
            inner = h_ref[layer, rows, :] + dot(heads, wproj_ref[layer]) + bproj_ref[pl.ds(layer, 1), :]
            inner_ref[layer, rows, :] = inner
            xhat, _ = norm_parts(inner)
            normed2 = (xhat * g2_ref[pl.ds(layer, 1), :] + b2_ref[pl.ds(layer, 1), :]).astype(BF)
            normed2_ref[layer, rows, :] = normed2
            hidden = dot(normed2, wfc1_ref[layer]) + bfc1_ref[pl.ds(layer, 1), :]
            cdf = 0.5 + 0.5 * lax.erf(hidden * math.sqrt(0.5))
            act = (hidden * cdf).astype(BF)
            act_ref[layer, rows, :] = act
            slope = cdf + hidden * jnp.exp2(hidden * hidden * (-0.5 * math.log2(math.e))) * (1.0 / math.sqrt(2 * math.pi))
            slope_ref[layer, rows, :] = slope.astype(BF)
            h_ref[layer + 1, rows, :] = inner + dot(act, wfc2_ref[layer]) + bfc2_ref[pl.ds(layer, 1), :]
            return carry

        lax.fori_loop(0, chunks, feed, 0, unroll=2)
        return carry

    lax.fori_loop(0, LAYERS, forward, 0)

    for image in range(images):
        spot = pl.ds(image * TOK_IMG, TOK_IMG)
        wide = pl.ds(image * IMG, IMG)
        keep = keep_of(image)
        result = jnp.where(keep, h_ref[LAYERS, wide, :], 0.0).astype(BF)
        out_ref[spot, :] = dot_tn(place_ref[...], result).astype(BF)
        dh_ref[wide, :] = jnp.where(keep, dot(place_ref[...], cot_ref[spot, :]), 0.0)

    def backward(step, carry):
        layer = LAYERS - 1 - step
        base = pl.multiple_of(layer * PACKED, 16)
        acc_ref[...] = jnp.zeros_like(acc_ref)
        accff_ref[...] = jnp.zeros_like(accff_ref)
        acclepe_ref[...] = jnp.zeros_like(acclepe_ref)

        def feed(index, carry):
            rows = chunk_rows(index)
            grad = dh_ref[rows, :]
            dz = grad.astype(BF)
            dz_ref[rows, :] = dz
            acc_ref[5] += fold_rows(dz.astype(F32))
            dhid = (dot_nt(dz, wfc2_ref[layer]) * slope_ref[layer, rows, :].astype(F32)).astype(BF)
            dhid_ref[rows, :] = dhid
            accff_ref[...] += fold_rows(dhid.astype(F32))
            dnormed = dot_nt(dhid, wfc1_ref[layer])
            dvalue, dgain = norm_back(dnormed, inner_ref[layer, rows, :], g2_ref[pl.ds(layer, 1), :])
            acc_ref[3] += fold_rows(dgain)
            acc_ref[4] += fold_rows(dnormed)
            dinner = grad + dvalue
            dh_ref[rows, :] = dinner
            return carry

        lax.fori_loop(0, chunks, feed, 0, unroll=2)

        def feed_weights(index, carry):
            cols = pl.ds(pl.multiple_of(index * 256, 256), 256)
            half = index // 2
            first = dot_tn(normed2_ref[layer], dhid_ref[:, cols]).astype(BF)
            second = dot_tn(dz_ref[...], act_ref[layer, :, cols]).astype(BF)
            for piece in range(2):
                at = pl.multiple_of((lax.rem(index, 2) * 2 + piece) * 256, 256)
                lanes = slice(piece * HW, (piece + 1) * HW)
                stage_ref[half, pl.ds(base + FC1_AT + at, 256), :] = first[:, lanes]
                stage_ref[half, pl.ds(base + FC2_AT + at, 256), :] = second[:, lanes]
            return carry

        lax.fori_loop(0, 4, feed_weights, 0)

        def project(index, carry):
            rows = chunk_rows(index)
            dy = dh_ref[rows, :].astype(BF)
            dz_ref[rows, :] = dy
            acc_ref[2] += fold_rows(dy.astype(F32))
            hf_ref[chunk_tiles(index)] = dot_nt(dy, wproj_ref[layer]).reshape(TILES, 2, TILE, D)
            return carry

        lax.fori_loop(0, chunks, project, 0, unroll=2)
        gproj = dot_tn(hb_ref[layer], dz_ref[...]).astype(BF)
        for half in range(2):
            stage_ref[half, pl.ds(base + PROJ_AT, D), :] = gproj[:, half * HW : (half + 1) * HW]

        def tap_weight(direction, tap):
            return lepe_ref[direction, layer, pl.ds(tap_row(direction, tap), 1), :]

        def score(window, _):
            direction, rows, grad, _ = window
            values = qkv_ref[layer, direction, rows, 2 * HW :]
            return dot_nt(head_rows(values, heads_ref), pad_keys(grad))

        def weigh(window, dprobs):
            direction, rows, _, _ = window
            dscores = []
            for head in range(GH):
                part = probs_ref[layer, direction, rows, head * KEYS : (head + 1) * KEYS].astype(F32)
                dpart = dprobs[head * BLOCK : (head + 1) * BLOCK]
                inner = jnp.sum(part * dpart, axis=0, keepdims=True)
                dscores.append((part * (dpart - inner)).astype(BF))
            return dscores

        def mix(window, dscores):
            direction, rows, grad, _ = window
            query = qkv_ref[layer, direction, rows, :HW]
            side = qkv_ref[layer, direction, rows, HW : 2 * HW].T
            dkeys = dot(jnp.concatenate(dscores, axis=1), head_stack(query, heads_ref))
            dvalues = dot(probs_ref[layer, direction, rows, :], head_stack(grad, heads_ref))
            dquery = [dot(side[head * HD : (head + 1) * HD], dscores[head]) for head in range(GH)]
            return jnp.concatenate(dquery, axis=0), dkeys, dvalues

        def finish(window, results):
            direction, rows, grad, block = window
            dquery, dkeys, dvalues = results
            values = qkv_ref[layer, direction, rows, 2 * HW :]
            first = direction * 3 * HW
            dhid_ref[rows, first : first + HW] = (dquery * SCALE).T[:BLOCK].astype(BF)
            dhid_ref[rows, first + HW : first + 2 * HW] = (dkeys * SCALE).astype(BF)
            if block is None:
                return values, dvalues
            grad_tiles = as_tiles(grad.astype(F32))
            result = as_tiles(dvalues)
            for tap, cells in enumerate(tap_cells(grad_tiles, direction)):
                result = result + cells * tap_weight(direction, TAPS - 1 - tap).reshape(1, 1, HW)
            result = jnp.where(live_tiles(), result, 0.0).reshape(BLOCK, HW)
            dhid_ref[rows, first + 2 * HW : first + 3 * HW] = result.astype(BF)
            tiles = jnp.where(live_tiles(), as_tiles(values.astype(F32)), 0.0)
            for tap, cells in enumerate(tap_cells(tiles, direction)):
                acclepe_ref[direction, tap_row(direction, tap)] += jnp.sum(grad_tiles * cells, axis=0)
            acclepe_ref[direction, TAPS] += jnp.sum(grad_tiles, axis=0)
            return None

        stages = (score, weigh, mix, finish)

        def attend_large(index, carry):
            windows = []
            for part in range(2):
                block = 6 * (index // 2) + 2 * lax.rem(index, 2) + part
                for direction in range(2):
                    lanes = slice(direction * HW, (direction + 1) * HW)
                    if direction == 0:
                        tiles = hf_ref[pl.ds(block * 7, 7), :, :, lanes]
                    else:
                        side = lax.rem(block, 2)
                        tiles = hf_ref[pl.ds((block - side) * 7, TILES), side, :, lanes]
                    windows.append((direction, block_rows(block), tiles.reshape(BLOCK, HW).astype(BF), block))
            pipeline(stages, windows)
            return carry

        lax.fori_loop(0, images * 2, attend_large, 0)

        def attend_small(index, carry):
            windows = []
            for part in range(2):
                block = 6 * index + 4 + part
                tiles = hf_ref[pl.ds(block * 7, 7)].reshape(BLOCK, D)
                for direction in range(2):
                    grad = tiles[:, direction * HW : (direction + 1) * HW].astype(BF)
                    windows.append((direction, block_rows(block), grad, None))
            results = pipeline(stages, windows)
            for part in range(2):
                rows = windows[2 * part][1]
                grads = [windows[2 * part + direction][2].astype(F32) for direction in range(2)]
                scaled = []
                for direction in range(2):
                    padded = pad_keys(grads[direction])
                    scaled.append(
                        jnp.concatenate(
                            [
                                (padded * tap_weight(direction, TAPS - 1 - tap)).astype(BF)
                                for tap in range(TAPS)
                            ],
                            axis=0,
                        )
                    )
                local = dot(wide_ref[...], jnp.concatenate(scaled, axis=1))
                shifted = dot(
                    tall_ref[...],
                    jnp.concatenate([pad_keys(results[2 * part + direction][0]) for direction in range(2)], axis=1),
                )
                for direction in range(2):
                    lanes = slice(direction * HW, (direction + 1) * HW)
                    first = direction * 3 * HW + 2 * HW
                    dvalues = results[2 * part + direction][1] + local[:, lanes]
                    dhid_ref[rows, first : first + HW] = dvalues.astype(BF)
                    for tap in range(TAPS):
                        acclepe_ref[direction, tap_row(direction, tap)] += fold_rows(
                            grads[direction] * shifted[tap * BLOCK : (tap + 1) * BLOCK, lanes]
                        )
                    acclepe_ref[direction, TAPS] += fold_rows(grads[direction])
            return carry

        lax.fori_loop(0, images, attend_small, 0)

        def normalize(index, carry):
            rows = chunk_rows(index)
            turned = dot_nt(dhid_ref[rows, 3 * HW : 6 * HW], wqkv_ref[1, layer])
            turned = jnp.where(lax.rem(index, 3) < 2, join_tiles(turned), turned)
            dnormed = dot_nt(dhid_ref[rows, : 3 * HW], wqkv_ref[0, layer]) + turned
            dvalue, dgain = norm_back(dnormed, h_ref[layer, rows, :], g1_ref[pl.ds(layer, 1), :])
            acc_ref[0] += fold_rows(dgain)
            acc_ref[1] += fold_rows(dnormed)
            dh_ref[rows, :] = dh_ref[rows, :] + dvalue
            return carry

        lax.fori_loop(0, chunks, normalize, 0, unroll=2)
        small_ref[...] = jnp.zeros_like(small_ref)
        for direction in range(2):
            gqkv = dot_tn(normed_ref[layer, direction], dhid_ref[:, direction * 3 * HW : (direction + 1) * 3 * HW]).astype(BF)
            for piece in range(3):
                at = QKV_AT + 256 * piece
                stage_ref[direction, pl.ds(base + at, 256), :] = gqkv[:, piece * HW : (piece + 1) * HW]
            small_ref[direction, :10, :] = jnp.sum(acclepe_ref[direction], axis=1)
        sums = jnp.sum(acc_ref[...], axis=1)
        for piece in range(2):
            small_ref[0, 10 + 6 * piece : 16 + 6 * piece, :] = sums[:, piece * HW : (piece + 1) * HW]
        sums = jnp.sum(accff_ref[...], axis=0, keepdims=True)
        for piece in range(8):
            small_ref[1, 10 + piece : 11 + piece, :] = sums[:, piece * HW : (piece + 1) * HW]
        stage_ref[:, pl.ds(base + SMALL_AT, SMALL), :] = small_ref[...].astype(BF)

        return carry

    stage_ref[:, ALL_PACKED:, :] = jnp.zeros((2, stage_ref.shape[1] - ALL_PACKED, HW), BF)
    lax.fori_loop(0, LAYERS, backward, 0)

    for half in range(2):
        for same, first_ref, second_ref in (
            (True, keep_first_ref, keep_second_ref),
            (False, send_first_ref, send_second_ref),
        ):

            @pl.when((core == half) == same)
            def _():
                def hand_out(part, carry):
                    slot = jnp.bitwise_xor(part, mine)
                    at = pl.multiple_of(part * part_rows, 16)
                    first_ref[place_of(slot, parts, 0)] = stage_ref[half, pl.ds(at, first_rows), :]
                    at = pl.multiple_of(at + first_rows, 16)
                    second_ref[place_of(slot, parts, 1)] = stage_ref[half, pl.ds(at, second_rows), :]
                    return carry

                lax.fori_loop(0, parts, hand_out, 0)

    for image in range(images):
        value = dh_ref[pl.ds(image * IMG, IMG), :]
        high = value.astype(BF)
        low = (value - high.astype(F32)).astype(BF)
        spot = pl.ds(image * TOK_IMG, TOK_IMG)
        dtok_ref[spot, :] = dot_tn(place_ref[...], high) + dot_tn(place_ref[...], low)


def digits_of(parts, which):
    digits, stride = [], 1
    while stride < parts:
        size = 4 if parts // stride % 4 == 0 else 2
        digits.append((size, stride))
        stride *= size
    return digits[which:] + digits[:which]


def place_of(index, parts, which):
    place = 0
    for size, stride in digits_of(parts, which):
        place = place * size + lax.rem(index // stride, size)
    return place


def unpack_kernel(
    own_first_ref,
    own_second_ref,
    other_first_ref,
    other_second_ref,
    g1_ref,
    b1_ref,
    gqkv_ref,
    glepe_ref,
    glepeb_ref,
    gproj_ref,
    gbproj_ref,
    g2_ref,
    b2_ref,
    gfc1_ref,
    gbfc1_ref,
    gfc2_ref,
    gbfc2_ref,
    stage_ref,
):
    parts = own_first_ref.shape[0]
    first_rows = own_first_ref.shape[1]
    second_rows = own_second_ref.shape[1]
    core = lax.axis_index("heads")
    mine = lax.axis_index("dp")

    def collect(part, carry):
        slot = jnp.bitwise_xor(part, mine)
        at = pl.multiple_of(part * (first_rows + second_rows), 16)
        first = place_of(slot, parts, 0)
        second = place_of(slot, parts, 1)
        stage_ref[core, pl.ds(at, first_rows), :] = own_first_ref[first]
        stage_ref[1 - core, pl.ds(at, first_rows), :] = other_first_ref[first]
        at = pl.multiple_of(at + first_rows, 16)
        stage_ref[core, pl.ds(at, second_rows), :] = own_second_ref[second]
        stage_ref[1 - core, pl.ds(at, second_rows), :] = other_second_ref[second]
        return carry

    lax.fori_loop(0, parts, collect, 0)
    for layer in range(LAYERS):
        base = layer * PACKED
        for half in range(2):
            for piece in range(4):
                lanes = slice(half * 512 + piece * HW, half * 512 + (piece + 1) * HW)
                at = base + FC1_AT + 256 * piece
                gfc1_ref[layer, :, lanes] = stage_ref[half, at : at + 256, :].astype(F32)
                at = base + FC2_AT + 256 * piece
                gfc2_ref[layer, lanes, :] = stage_ref[half, at : at + 256, :].astype(F32).T
            gproj_ref[layer, :, half * HW : (half + 1) * HW] = stage_ref[
                half, base + PROJ_AT : base + PROJ_AT + 256, :
            ].astype(F32)
        for piece in range(3):
            at = base + QKV_AT + 256 * piece
            gqkv_ref[layer, 0, :, piece * HW : (piece + 1) * HW] = stage_ref[core, at : at + 256, :].astype(F32)
        small = stage_ref[core, base + SMALL_AT : base + PACKED, :].astype(F32)
        glepe_ref[layer, 0] = small[:TAPS]
        glepeb_ref[layer] = small[TAPS : TAPS + 1]
        small = stage_ref[0, base + SMALL_AT : base + PACKED, :].astype(F32)
        for place, ref in enumerate((g1_ref, b1_ref, gbproj_ref, g2_ref, b2_ref, gbfc2_ref)):
            for piece in range(2):
                row = 10 + 6 * piece + place
                ref[layer : layer + 1, piece * HW : (piece + 1) * HW] = small[row : row + 1]
        small = stage_ref[1, base + SMALL_AT : base + PACKED, :].astype(F32)
        for piece in range(8):
            gbfc1_ref[layer : layer + 1, piece * HW : (piece + 1) * HW] = small[10 + piece : 11 + piece]


SMEM = pl.BlockSpec(memory_space=pltpu.SMEM)
VMEM = pl.BlockSpec(memory_space=pltpu.VMEM)


def shards(
    dp,
    tokens,
    cotangent,
    counts,
    ln1_gain,
    ln1_bias,
    w_qkv,
    lepe_w,
    lepe_b,
    w_proj,
    b_proj,
    ln2_gain,
    ln2_bias,
    w_fc1,
    b_fc1,
    w_fc2,
    b_fc2,
):
    tokens_here = tokens.shape[0]
    images = tokens_here // TOK_IMG
    rows = images * IMG
    swap = [(0, 1), (1, 0)]

    def across(value):
        return lax.ppermute(value, "heads", swap)

    part_rows = -(-ALL_PACKED // (16 * dp)) * 16
    second_rows = (part_rows + 24) // 48 * 16
    first_rows = part_rows - second_rows
    wide, tall = shift_tables()
    table = place_table()
    scratch = [
        pltpu.VMEM((2, LAYERS, D, 3 * HW), BF),
        pltpu.VMEM((2, LAYERS, 16, HW), F32),
        pltpu.VMEM((LAYERS + 1, rows, D), F32),
        pltpu.VMEM((LAYERS, 2, rows, D), BF),
        pltpu.VMEM((LAYERS, 2, rows, 3 * HW), BF),
        pltpu.VMEM((LAYERS, 2, rows, SPAN), BF),
        pltpu.VMEM((rows // 16, 2, TILE, D), F32),
        pltpu.VMEM((LAYERS, rows, D), BF),
        pltpu.VMEM((LAYERS, rows, D), F32),
        pltpu.VMEM((LAYERS, rows, D), BF),
        pltpu.VMEM((LAYERS, rows, FF), BF),
        pltpu.VMEM((LAYERS, rows, FF), BF),
        pltpu.VMEM((rows, D), F32),
        pltpu.VMEM((rows, D), BF),
        pltpu.VMEM((rows, FF), BF),
        pltpu.VMEM((6, 8, D), F32),
        pltpu.VMEM((8, FF), F32),
        pltpu.VMEM((2, TAPS + 1, 8, HW), F32),
        pltpu.VMEM((2, SMALL, HW), F32),
        pltpu.VMEM((2, part_rows * dp, HW), BF),
    ]
    result, grad, *packed = pl.pallas_call(
        step_kernel,
        out_shape=(
            jax.ShapeDtypeStruct((tokens_here, D), BF),
            jax.ShapeDtypeStruct((tokens_here, D), F32),
            *[jax.ShapeDtypeStruct((dp, some, HW), BF) for some in (first_rows, second_rows) * 2],
        ),
        in_specs=[SMEM] + [VMEM] * 23,
        out_specs=(VMEM,) * 6,
        scratch_shapes=scratch,
        compiler_params=pltpu.CompilerParams(vmem_limit_bytes=60 * 1024 * 1024),
        name="step",
    )(
        counts,
        tokens,
        cotangent,
        ln1_gain,
        ln1_bias,
        w_qkv,
        across(w_qkv),
        lepe_w,
        across(lepe_w),
        lepe_b,
        across(lepe_b),
        w_proj,
        b_proj,
        ln2_gain,
        ln2_bias,
        w_fc1,
        b_fc1,
        w_fc2,
        b_fc2,
        jnp.asarray(table, BF),
        jnp.asarray(wide, BF),
        jnp.asarray(tall, BF),
        jnp.asarray(bias_table()),
        jnp.asarray(head_table(), BF),
    )

    def add(first, *rest):
        total = first.astype(F32)
        for item in rest:
            total = total + item.astype(F32)
        return total.astype(BF)

    own = [add(packed[place], across(packed[2 + place])) for place in range(2)]
    orders = [digits_of(dp, place) for place in range(2)]

    def exchange(step, pieces_of):
        sent = []
        for place in (1, 0):
            size, stride = orders[place][step]
            pieces = pieces_of(place, size)
            for hop in range(size - 1, 0, -1):
                pairs = [(device, device ^ (hop * stride)) for device in range(dp)]
                sent.append((place, hop, lax.ppermute(pieces[hop], "dp", pairs)))
        arrived = lax.optimization_barrier(tuple(item[2] for item in sent))
        got = [{}, {}]
        for (place, hop, _), value in zip(sent, arrived):
            got[place][hop] = value
        return [[got[place][hop] for hop in sorted(got[place])] for place in range(2)]

    for step in range(len(orders[0])):

        def cut(place, size):
            value = own[place]
            return value.reshape((size, value.shape[0] // size) + value.shape[1:])

        arrived = exchange(step, cut)
        own = [add(cut(place, orders[place][step][0])[0], *arrived[place]) for place in range(2)]
    for step in reversed(range(len(orders[0]))):
        arrived = exchange(step, lambda place, size: [own[place]] * size)
        own = [jnp.concatenate([own[place]] + arrived[place], axis=0) for place in range(2)]
    other = [across(value) for value in own]
    grads = pl.pallas_call(
        unpack_kernel,
        out_shape=(
            jax.ShapeDtypeStruct((LAYERS, D), F32),
            jax.ShapeDtypeStruct((LAYERS, D), F32),
            jax.ShapeDtypeStruct((LAYERS, 1, D, 3 * HW), F32),
            jax.ShapeDtypeStruct((LAYERS, 1, TAPS, HW), F32),
            jax.ShapeDtypeStruct((LAYERS, 1, HW), F32),
            jax.ShapeDtypeStruct((LAYERS, D, D), F32),
            jax.ShapeDtypeStruct((LAYERS, D), F32),
            jax.ShapeDtypeStruct((LAYERS, D), F32),
            jax.ShapeDtypeStruct((LAYERS, D), F32),
            jax.ShapeDtypeStruct((LAYERS, D, FF), F32),
            jax.ShapeDtypeStruct((LAYERS, FF), F32),
            jax.ShapeDtypeStruct((LAYERS, FF, D), F32),
            jax.ShapeDtypeStruct((LAYERS, D), F32),
        ),
        in_specs=[VMEM] * 4,
        out_specs=(VMEM,) * 13,
        scratch_shapes=[pltpu.VMEM((2, part_rows * dp, HW), BF)],
        compiler_params=pltpu.CompilerParams(vmem_limit_bytes=48 * 1024 * 1024),
        name="unpack",
    )(*own, *other)
    return (result, grad) + tuple(grads)


def solution(mesh):
    spread = P(("dp", "heads"), None)
    group = (P(None, "heads", None, None), P(None, "heads", None, None), P(None, "heads", None))
    in_specs = (spread, spread, P("dp"), P(), P()) + group + (P(),) * 8
    out_specs = (spread, spread, P(), P()) + group + (P(),) * 8
    return jax.shard_map(
        functools.partial(shards, mesh.shape["dp"]),
        mesh=mesh,
        in_specs=in_specs,
        out_specs=out_specs,
        check_vma=False,
    )
```

```python
import functools
import math

import jax
import jax.numpy as jnp
import numpy as np
from jax import lax
from jax.experimental import pallas as pl
from jax.experimental.pallas import tpu as pltpu
from jax.sharding import PartitionSpec as P

D = 256
FF = 1024
HD = 32
GH = 4
HW = 128
LAYERS = 2
TOK_IMG = 608
SPLIT = 392
EPSILON = 1e-05

TILE = 8
TILES = 14
BLOCK = TILES * TILE
CHUNK = 2 * BLOCK
IMG = 6 * BLOCK
KEYS = 128
SPAN = GH * KEYS
TAPS = 9
SCALE = HD**-0.5
EXP_SCALE = SCALE * math.log2(math.e)
BF = jnp.bfloat16
F32 = jnp.float32

FC1_AT = 0
FC2_AT = 1024
PROJ_AT = 2048
QKV_AT = 2304
SMALL_AT = 3072
SMALL = 32
PACKED = SMALL_AT + SMALL
ALL_PACKED = LAYERS * PACKED


def place_table():
    table = np.zeros((IMG, TOK_IMG), np.float32)
    for crop in range(2):
        for row in range(14):
            for col in range(14):
                place = crop * CHUNK + row * 16 + (col // 7) * TILE + col % 7
                table[place, crop * 196 + row * 14 + col] = 1
    for group in range(2):
        for cell in range(108):
            table[2 * CHUNK + group * BLOCK + cell, SPLIT + group * 108 + cell] = 1
    return table


def window_cells(kind):
    cells = [None] * BLOCK
    if kind == 2:
        for place in range(108):
            cells[place] = (place // 36, place % 36 // 6, place % 6)
    else:
        for place in range(BLOCK):
            tile, col = divmod(place, TILE)
            if col < 7:
                cells[place] = (0, tile // 2, 7 * (tile % 2) + col) if kind == 0 else (0, tile, col)
    return cells


def shift_tables():
    wide = np.zeros((3, BLOCK, TAPS * KEYS), np.float32)
    tall = np.zeros((TAPS * BLOCK, KEYS), np.float32)
    for kind in range(3):
        cells = window_cells(kind)
        spots = {cell: place for place, cell in enumerate(cells) if cell is not None}
        for place, cell in enumerate(cells):
            for tap in range(TAPS):
                other = cell and spots.get((cell[0], cell[1] + tap // 3 - 1, cell[2] + tap % 3 - 1))
                if other is not None:
                    wide[kind, place, tap * KEYS + other] = 1
                    if kind == 2:
                        tall[tap * BLOCK + place, other] = 1
    return wide, tall


def bias_table():
    bias = np.full((2, BLOCK, KEYS), -1e30, np.float32)
    bias[0, [key for key in range(BLOCK) if key % TILE < 7]] = 0
    for query in range(KEYS):
        first, last = (36 * (query // 36), 36 * (query // 36) + 36) if query < 108 else (0, 108)
        bias[1, first:last, query] = 0
    return bias


def head_table():
    table = np.zeros((SPAN, HW), np.float32)
    for head in range(GH):
        table[head * KEYS : (head + 1) * KEYS, head * HD : (head + 1) * HD] = 1
    return table


def dot(left, right):
    return lax.dot_general(left, right, (((1,), (0,)), ((), ())), preferred_element_type=F32)


def dot_nt(left, right):
    return lax.dot_general(left, right, (((1,), (1,)), ((), ())), preferred_element_type=F32)


def dot_tn(left, right):
    return lax.dot_general(left, right, (((0,), (0,)), ((), ())), preferred_element_type=F32)


def norm_parts(value):
    center = value - jnp.mean(value, axis=-1, keepdims=True)
    scale = lax.rsqrt(jnp.mean(center * center, axis=-1, keepdims=True) + EPSILON)
    return center * scale, scale


def norm_back(dout, value, gain):
    xhat, scale = norm_parts(value)
    grown = dout * gain
    mean = jnp.mean(grown, axis=-1, keepdims=True)
    cross = jnp.mean(grown * xhat, axis=-1, keepdims=True)
    return scale * (grown - mean - xhat * cross), dout * xhat


def fold_rows(value):
    return jnp.sum(value.reshape(value.shape[0] // 8, 8, value.shape[1]), axis=0)


def head_rows(value, heads_ref):
    return jnp.concatenate(
        [value * heads_ref[head * KEYS : head * KEYS + 1, :] for head in range(GH)], axis=0
    )


def head_stack(value, heads_ref):
    rows = []
    pad = jnp.zeros((KEYS - BLOCK, HW), BF)
    for head in range(GH):
        rows.append(value * heads_ref[head * KEYS : head * KEYS + 1, :])
        rows.append(pad)
    return jnp.concatenate(rows, axis=0)


def pad_keys(value):
    return jnp.concatenate([value, jnp.zeros((KEYS - BLOCK, value.shape[1]), value.dtype)], axis=0)


def pipeline(stages, items, fillers=()):
    results = [None] * len(items)
    fillers = list(fillers)
    for step in range(len(items) + len(stages) - 1):
        if fillers:
            fillers.pop(0)()
        for place in range(len(stages)):
            item = step - place
            if 0 <= item < len(items):
                results[item] = stages[place](items[item], results[item])
    return results


def split_tiles(value):
    rows = value.shape[0] // 16
    return jnp.concatenate(
        [value[16 * row : 16 * row + 8] for row in range(rows)]
        + [value[16 * row + 8 : 16 * row + 16] for row in range(rows)],
        axis=0,
    )


def join_tiles(value):
    half = value.shape[0] // 2
    pieces = []
    for row in range(half // 8):
        pieces.append(value[8 * row : 8 * row + 8])
        pieces.append(value[half + 8 * row : half + 8 * row + 8])
    return jnp.concatenate(pieces, axis=0)


def as_tiles(value):
    return value.reshape(TILES, TILE, HW)


def live_tiles():
    return lax.broadcasted_iota(jnp.int32, (1, TILE, HW), 1) < TILE - 1


def side_cells(tiles, direction):
    if direction == 1:
        return pltpu.roll(tiles, 1, 1), tiles, pltpu.roll(tiles, TILE - 1, 1)
    last = lax.broadcasted_iota(jnp.int32, (1, TILE, HW), 1) == TILE - 1
    left, right = [], []
    for row in range(TILES // 2):
        near, far = tiles[2 * row : 2 * row + 1], tiles[2 * row + 1 : 2 * row + 2]
        near_left = pltpu.roll(near, 1, 1)
        far_right = pltpu.roll(far, TILE - 1, 1)
        left += [near_left, pltpu.roll(jnp.where(last, near_left, far), 1, 1)]
        right += [pltpu.roll(jnp.where(last, far_right, near), TILE - 1, 1), far_right]
    return jnp.concatenate(left, axis=0), tiles, jnp.concatenate(right, axis=0)


def tap_cells(tiles, direction):
    stride = 2 if direction == 0 else 1
    zeros = jnp.zeros((stride, TILE, HW), F32)
    padded = [jnp.concatenate([zeros, side, zeros], axis=0) for side in side_cells(tiles, direction)]
    return [padded[tap % 3][(tap // 3) * stride : (tap // 3) * stride + TILES] for tap in range(TAPS)]


def tap_row(direction, tap):
    return tap if direction == 0 else 3 * (tap % 3) + tap // 3


def compact(ref, image, value):
    first = image * TOK_IMG
    for tile in range(2 * 2 * TILES):
        ref[first + 7 * tile : first + 7 * tile + 7, :] = value[TILE * tile : TILE * tile + 7]
    for group in range(2):
        at = first + SPLIT + 108 * group
        row = 2 * CHUNK + BLOCK * group
        ref[at : at + 108, :] = value[row : row + 108]


def step_kernel(
    counts_ref,
    tok_ref,
    cot_from,
    g1_ref,
    b1_ref,
    own_wqkv_from,
    other_wqkv_from,
    own_lepe_ref,
    other_lepe_ref,
    own_lepeb_ref,
    other_lepeb_ref,
    wproj_from,
    bproj_ref,
    g2_ref,
    b2_ref,
    wfc1_from,
    bfc1_ref,
    wfc2_from,
    bfc2_ref,
    place_ref,
    wide_from,
    tall_from,
    bias_ref,
    heads_ref,
    out_ref,
    dtok_ref,
    keep_ref,
    send_ref,
    cot_ref,
    wproj_ref,
    wfc1_ref,
    half_wfc2_ref,
    wide_ref,
    tall_ref,
    fetched,
    handed,
    wqkv_ref,
    lepe_ref,
    h_ref,
    normed_ref,
    qkv_ref,
    probs_ref,
    hf_ref,
    hb_ref,
    inner_ref,
    normed2_ref,
    act_ref,
    slope_ref,
    dz_ref,
    dy_ref,
    dhid_ref,
    dqkv_ref,
    acc_ref,
    bfc1_sum_ref,
    accproj_ref,
    accqkv_ref,
    acclepe_ref,
    small_ref,
    stage_ref,
):
    rows_all = h_ref.shape[1]
    images = rows_all // IMG
    chunks = rows_all // CHUNK
    blocks = rows_all // BLOCK
    parts = keep_ref.shape[0]
    part_rows = keep_ref.shape[1]
    core = lax.axis_index("heads")
    mine = lax.axis_index("dp")
    moves = (
        (own_wqkv_from.at[:, 0], wqkv_ref.at[core]),
        (other_wqkv_from.at[:, 0], wqkv_ref.at[1 - core]),
        (wproj_from, wproj_ref),
        (wfc1_from, wfc1_ref),
        (wfc2_from, half_wfc2_ref),
        (wide_from, wide_ref),
        (cot_from, cot_ref),
        (tall_from, tall_ref),
    )
    fetches = [pltpu.make_async_copy(*move, fetched.at[place]) for place, move in enumerate(moves)]
    for fetch in fetches:
        fetch.start()
    for direction, (lepe, lepeb) in (
        (core, (own_lepe_ref, own_lepeb_ref)),
        (1 - core, (other_lepe_ref, other_lepeb_ref)),
    ):
        lepe_ref[direction, :, :TAPS] = lepe[:, :, 0]
        lepe_ref[direction, :, TAPS : TAPS + 1] = lepeb[...]

    def chunk_rows(index):
        return pl.ds(index * CHUNK, CHUNK)

    def chunk_tiles(index):
        return pl.ds(index * TILES, TILES)

    def wide_rows(index):
        return pl.ds(index * 2 * CHUNK, 2 * CHUNK)

    def wide_tiles(index):
        return pl.ds(index * 2 * TILES, 2 * TILES)

    def block_rows(index):
        return pl.ds(index * BLOCK, BLOCK)

    def is_small(block):
        return block % 6 >= 4

    def keep_of(image):
        place = lax.broadcasted_iota(jnp.int32, (IMG, 1), 0)
        limit = counts_ref[core * images + image]
        group = (place - 448) // BLOCK
        inside = (place - 448) % BLOCK
        return (place < 448) | (inside < 36 * (limit - 3 * group))

    for image in range(images):
        spot = pl.ds(image * TOK_IMG, TOK_IMG)
        h_ref[0, pl.ds(image * IMG, IMG), :] = dot(place_ref[...], tok_ref[spot, :])

    for fetch in fetches[:6]:
        fetch.wait()
    half_wfc2_ref[...] = half_wfc2_ref[...] * jnp.asarray(0.5, BF)

    def forward(layer, carry):
        gain1, bias1 = g1_ref[pl.ds(layer, 1), :], b1_ref[pl.ds(layer, 1), :]

        def normalize(index, _):
            rows = chunk_rows(index)
            xhat, _ = norm_parts(h_ref[layer, rows, :])
            normed = xhat * gain1 + bias1
            turned = split_tiles(normed) if index % 3 < 2 else normed
            return normed.astype(BF), turned.astype(BF)

        def project(index, values):
            rows = chunk_rows(index)
            for direction, value in enumerate(values):
                normed_ref[layer, direction, rows, :] = value
                qkv_ref[layer, direction, rows, :] = dot(value, wqkv_ref[direction, layer]).astype(BF)

        pipeline((normalize, project), range(chunks))

        def tap_weight(direction, tap):
            return lepe_ref[direction, layer, pl.ds(tap_row(direction, tap), 1), :]

        def score(window, _):
            direction, block = window
            rows = block_rows(block)
            query = qkv_ref[layer, direction, rows, :HW]
            keyset = qkv_ref[layer, direction, rows, HW : 2 * HW]
            return dot_nt(head_rows(keyset, heads_ref), pad_keys(query))

        def weigh(window, scores):
            direction, block = window
            rows = block_rows(block)
            bias = bias_ref[int(is_small(block))]
            probs = []
            for head in range(GH):
                part = scores[head * BLOCK : (head + 1) * BLOCK] + bias
                part = jnp.exp2((part - jnp.max(part, axis=0, keepdims=True)) * EXP_SCALE)
                part = part * (1.0 / jnp.sum(part, axis=0, keepdims=True))
                probs.append(part.astype(BF))
                probs_ref[layer, direction, rows, head * KEYS : (head + 1) * KEYS] = probs[head]
            return probs

        def mix(window, probs):
            direction, block = window
            rows = block_rows(block)
            values = qkv_ref[layer, direction, rows, 2 * HW :]
            side = values.T
            mixed = [dot(side[head * HD : (head + 1) * HD], probs[head]) for head in range(GH)]
            return jnp.concatenate(mixed, axis=0)

        def finish(window, mixed):
            direction, block = window
            lanes = slice(direction * HW, (direction + 1) * HW)
            result = mixed.T[:BLOCK] + lepe_ref[direction, layer, TAPS : TAPS + 1, :] + local[window]
            if direction == 0 or is_small(block):
                hf_ref[block * 7 : block * 7 + 7, :, :, lanes] = result.reshape(7, 2, TILE, HW)
            else:
                side = block % 2
                rows = slice((block - side) * 7, (block - side) * 7 + TILES)
                hf_ref[rows, side, :, lanes] = as_tiles(result)

        local = {}

        def filter_pair(kind, windows):
            scaled = []
            for direction, block in windows:
                values = qkv_ref[layer, direction, block_rows(block), 2 * HW :]
                scaled.append(
                    jnp.concatenate(
                        [pad_keys(values * tap_weight(direction, tap).astype(BF)) for tap in range(TAPS)], axis=0
                    )
                )
            both = dot(wide_ref[kind], jnp.concatenate(scaled, axis=1))
            for place, window in enumerate(windows):
                local[window] = both[:, place * HW : (place + 1) * HW]

        windows, fillers = [], []
        for block in range(blocks):
            windows += [(direction, block) for direction in range(2)]
            if is_small(block):
                fillers.append(functools.partial(filter_pair, 2, windows[-2:]))
            elif block % 2 == 1:
                for direction in range(2):
                    pair = [(direction, block - 1), (direction, block)]
                    fillers.append(functools.partial(filter_pair, direction, pair))
        pipeline((score, weigh, mix, finish), windows, fillers)

        gain2, bias2 = g2_ref[pl.ds(layer, 1), :], b2_ref[pl.ds(layer, 1), :]

        def join(index, _):
            rows = chunk_rows(index)
            heads = hf_ref[chunk_tiles(index)].reshape(CHUNK, D).astype(BF)
            hb_ref[layer, rows, :] = heads
            inner = h_ref[layer, rows, :] + dot(heads, wproj_ref[layer]) + bproj_ref[pl.ds(layer, 1), :]
            inner_ref[layer, rows, :] = inner
            return inner

        def widen(index, inner):
            xhat, _ = norm_parts(inner)
            normed2 = (xhat * gain2 + bias2).astype(BF)
            normed2_ref[layer, chunk_rows(index), :] = normed2
            return dot(normed2, wfc1_ref[layer])

        def narrow(index, hidden):
            rows = chunk_rows(index)
            hidden = hidden + bfc1_ref[pl.ds(layer, 1), :]
            cdf = 1.0 + lax.erf(hidden * math.sqrt(0.5))
            act = (hidden * cdf).astype(BF)
            act_ref[layer, rows, :] = act
            bell = jnp.exp2(hidden * hidden * (-0.5 * math.log2(math.e)))
            slope_ref[layer, rows, :] = (cdf + hidden * bell * math.sqrt(2 / math.pi)).astype(BF)
            return dot(act, half_wfc2_ref[layer])

        def close(index, branch):
            rows = chunk_rows(index)
            h_ref[layer + 1, rows, :] = inner_ref[layer, rows, :] + branch + bfc2_ref[pl.ds(layer, 1), :]

        pipeline((join, widen, narrow, close), range(chunks))
        return carry

    lax.fori_loop(0, LAYERS, forward, 0)
    for fetch in fetches[6:]:
        fetch.wait()

    for image in range(images):
        spot = pl.ds(image * TOK_IMG, TOK_IMG)
        wide = pl.ds(image * IMG, IMG)
        keep = keep_of(image)
        compact(dtok_ref, image, jnp.where(keep, h_ref[LAYERS, wide, :], 0.0))
        h_ref[LAYERS, wide, :] = jnp.where(keep, dot(place_ref[...], cot_ref[spot, :]), 0.0)
    out_ref[...] = dtok_ref[...].astype(BF)

    def backward(step, carry):
        layer = LAYERS - 1 - step
        base = pl.multiple_of(layer * PACKED, 16)
        acc_ref[...] = jnp.zeros_like(acc_ref)
        acclepe_ref[...] = jnp.zeros_like(acclepe_ref)

        accproj_ref[...] = jnp.zeros_like(accproj_ref)
        bfc1_sum_ref[...] = jnp.zeros_like(bfc1_sum_ref)
        gain2 = g2_ref[pl.ds(layer, 1), :]

        def pair_rows(index):
            return pl.ds((index - 1) * CHUNK, 2 * CHUNK)

        def widen(index, _):
            rows = wide_rows(index)
            dz = h_ref[LAYERS, rows, :].astype(BF)
            dz_ref[rows, :] = dz
            acc_ref[5] += fold_rows(dz.astype(F32))
            return dot_nt(dz, half_wfc2_ref[layer])

        def narrow(index, dact):
            rows = wide_rows(index)
            dhid = dact * slope_ref[layer, rows, :].astype(F32)
            bfc1_sum_ref[...] += fold_rows(dhid)
            dhid = dhid.astype(BF)
            dhid_ref[rows, :] = dhid
            return dot_nt(dhid, wfc1_ref[layer])

        def close(index, dnormed):
            rows = wide_rows(index)
            dvalue, dgain = norm_back(dnormed, inner_ref[layer, rows, :], gain2)
            acc_ref[3] += fold_rows(dgain)
            acc_ref[4] += fold_rows(dnormed)
            dinner = h_ref[LAYERS, rows, :] + dvalue
            h_ref[LAYERS, rows, :] = dinner
            dy = dinner.astype(BF)
            dy_ref[rows, :] = dy
            acc_ref[2] += fold_rows(dy.astype(F32))
            return dot_nt(dy, wproj_ref[layer])

        def project(index, dheads):
            hf_ref[wide_tiles(index)] = dheads.reshape(2 * TILES, 2, TILE, D)
            rows = wide_rows(index)
            accproj_ref[...] += dot_tn(hb_ref[layer, rows, :], dy_ref[rows, :])

        pipeline((widen, narrow, close, project), range(chunks // 2))
        for half in range(2):
            stage_ref[half, pl.ds(base + PROJ_AT, D), :] = accproj_ref[:, half * HW : (half + 1) * HW].astype(BF)

        def tap_weight(direction, tap):
            return lepe_ref[direction, layer, pl.ds(tap_row(direction, tap), 1), :]

        def grad_of(direction, block):
            lanes = slice(direction * HW, (direction + 1) * HW)
            if direction == 0 or is_small(block):
                tiles = hf_ref[block * 7 : block * 7 + 7, :, :, lanes]
            else:
                side = block % 2
                tiles = hf_ref[(block - side) * 7 : (block - side) * 7 + TILES, side, :, lanes]
            return tiles.reshape(BLOCK, HW).astype(BF)

        def score(window, _):
            direction, block = window
            rows = block_rows(block)
            grad = grad_of(direction, block)
            values = qkv_ref[layer, direction, rows, 2 * HW :]
            return dot_nt(head_rows(values, heads_ref), pad_keys(grad))

        def weigh(window, dprobs):
            direction, block = window
            rows = block_rows(block)
            dscores = []
            for head in range(GH):
                part = probs_ref[layer, direction, rows, head * KEYS : (head + 1) * KEYS].astype(F32)
                dpart = dprobs[head * BLOCK : (head + 1) * BLOCK]
                inner = jnp.sum(part * dpart, axis=0, keepdims=True)
                dscores.append((part * (dpart - inner)).astype(BF))
            return dscores

        def mix(window, dscores):
            direction, block = window
            rows = block_rows(block)
            grad = grad_of(direction, block)
            query = qkv_ref[layer, direction, rows, :HW]
            side = qkv_ref[layer, direction, rows, HW : 2 * HW].T
            dkeys = dot(jnp.concatenate(dscores, axis=1), head_stack(query, heads_ref))
            dvalues = dot(probs_ref[layer, direction, rows, :], head_stack(grad, heads_ref))
            dquery = [dot(side[head * HD : (head + 1) * HD], dscores[head]) for head in range(GH)]
            return jnp.concatenate(dquery, axis=0), dkeys, dvalues

        def finish(window, results):
            direction, block = window
            rows = block_rows(block)
            grad = grad_of(direction, block)
            lanes = slice(direction * HW, (direction + 1) * HW)
            dquery, dkeys, dvalues = results
            values = qkv_ref[layer, direction, rows, 2 * HW :]
            first = direction * 3 * HW
            dqkv_ref[rows, first : first + HW] = (dquery * SCALE).T[:BLOCK].astype(BF)
            dqkv_ref[rows, first + HW : first + 2 * HW] = (dkeys * SCALE).astype(BF)
            if is_small(block):
                dvalues = dvalues + local[block][:, lanes]
                dqkv_ref[rows, first + 2 * HW : first + 3 * HW] = dvalues.astype(BF)
                return None
            grad_tiles = as_tiles(grad.astype(F32))
            result = as_tiles(dvalues)
            for tap, cells in enumerate(tap_cells(grad_tiles, direction)):
                result = result + cells * tap_weight(direction, TAPS - 1 - tap).reshape(1, 1, HW)
            result = jnp.where(live_tiles(), result, 0.0).reshape(BLOCK, HW)
            dqkv_ref[rows, first + 2 * HW : first + 3 * HW] = result.astype(BF)
            tiles = jnp.where(live_tiles(), as_tiles(values.astype(F32)), 0.0)
            for tap, cells in enumerate(tap_cells(tiles, direction)):
                acclepe_ref[direction, tap_row(direction, tap)] += jnp.sum(grad_tiles * cells, axis=0)
            acclepe_ref[direction, TAPS] += jnp.sum(grad_tiles, axis=0)
            return None

        half_rows = rows_all // 2
        spans = [pl.ds(part * half_rows, half_rows) for part in range(2)]
        sides = {}

        def feed_weights(index):
            width = FF // (2 * images)
            cols = pl.ds(index * width, width)
            partial = []

            def first(part):
                rows = spans[part]
                if (0, part) not in sides:
                    sides[0, part] = normed2_ref[layer, rows, :].T
                partial.append(dot(sides[0, part], dhid_ref[rows, cols]))

            def second(part):
                rows = spans[part]
                if (1, part) not in sides:
                    sides[1, part] = dz_ref[rows, :].T
                partial.append(dot(sides[1, part], act_ref[layer, rows, cols]))

            def store(at):
                total = partial[0] + partial[1]
                if at == FC2_AT:
                    total = total * 0.5
                for piece in range(width // HW):
                    column = index * (width // HW) + piece
                    place = pl.multiple_of(base + at + column % 4 * 256, 16)
                    value = total[:, piece * HW : (piece + 1) * HW].astype(BF)
                    stage_ref[column // 4, pl.ds(place, 256), :] = value
                partial.clear()

            return [
                lambda: first(0),
                lambda: (first(1), store(FC1_AT)),
                lambda: second(0),
                lambda: (second(1), store(FC2_AT)),
            ]

        local = {}

        def filter_small(block):
            scaled = []
            for direction in range(2):
                padded = pad_keys(grad_of(direction, block).astype(F32))
                scaled.append(
                    jnp.concatenate(
                        [(padded * tap_weight(direction, TAPS - 1 - tap)).astype(BF) for tap in range(TAPS)], axis=0
                    )
                )
            local[block] = dot(wide_ref[2], jnp.concatenate(scaled, axis=1))

        def shift_small(block):
            values = [pad_keys(qkv_ref[layer, direction, block_rows(block), 2 * HW :]) for direction in range(2)]
            shifted = dot(tall_ref[...], jnp.concatenate(values, axis=1))
            for direction in range(2):
                lanes = slice(direction * HW, (direction + 1) * HW)
                grad = grad_of(direction, block).astype(F32)
                for tap in range(TAPS):
                    acclepe_ref[direction, tap_row(direction, tap)] += fold_rows(
                        grad * shifted[tap * BLOCK : (tap + 1) * BLOCK, lanes]
                    )
                acclepe_ref[direction, TAPS] += fold_rows(grad)

        order = [block for block in range(blocks) if not is_small(block)]
        order += [block for block in range(blocks) if is_small(block)]
        windows = [(direction, block) for block in order for direction in range(2)]
        fillers = [filler for index in range(2 * images) for filler in feed_weights(index)]
        for block in order:
            if is_small(block):
                fillers += [functools.partial(filter_small, block), functools.partial(shift_small, block)]
        pipeline((score, weigh, mix, finish), windows, fillers)

        accqkv_ref[...] = jnp.zeros_like(accqkv_ref)
        gain1 = g1_ref[pl.ds(layer, 1), :]

        def collect(index, _):
            rows = chunk_rows(index)
            return [
                dot_nt(dqkv_ref[rows, direction * 3 * HW : (direction + 1) * 3 * HW], wqkv_ref[direction, layer])
                for direction in range(2)
            ]

        def weigh_inputs(index, dnormed):
            if index % 2 == 1:
                rows = pair_rows(index)
                for direction in range(2):
                    accqkv_ref[direction] += dot(
                        normed_ref[layer, direction, rows, :].T,
                        dqkv_ref[rows, direction * 3 * HW : (direction + 1) * 3 * HW],
                    )
            return dnormed

        def spread(index, dnormed):
            rows = chunk_rows(index)
            straight, turned = dnormed
            dnormed = straight + (join_tiles(turned) if index % 3 < 2 else turned)
            dvalue, dgain = norm_back(dnormed, h_ref[layer, rows, :], gain1)
            acc_ref[0] += fold_rows(dgain)
            acc_ref[1] += fold_rows(dnormed)
            h_ref[LAYERS, rows, :] = h_ref[LAYERS, rows, :] + dvalue

        pipeline((collect, weigh_inputs, spread), range(chunks))
        small_ref[...] = jnp.zeros_like(small_ref)
        for direction in range(2):
            for piece in range(3):
                at = QKV_AT + 256 * piece
                stage_ref[direction, pl.ds(base + at, 256), :] = accqkv_ref[
                    direction, :, piece * HW : (piece + 1) * HW
                ].astype(BF)
            small_ref[direction, :10, :] = jnp.sum(acclepe_ref[direction], axis=1)
        sums = jnp.sum(acc_ref[...], axis=1)
        for piece in range(2):
            small_ref[0, 10 + 6 * piece : 16 + 6 * piece, :] = sums[:, piece * HW : (piece + 1) * HW]
        sums = jnp.sum(bfc1_sum_ref[...], axis=0, keepdims=True)
        for piece in range(8):
            small_ref[1, 10 + piece : 11 + piece, :] = sums[:, piece * HW : (piece + 1) * HW]
        stage_ref[:, pl.ds(base + SMALL_AT, SMALL), :] = small_ref[...].astype(BF)

        return carry

    stage_ref[:, ALL_PACKED:, :] = jnp.zeros((2, stage_ref.shape[1] - ALL_PACKED, HW), BF)
    lax.fori_loop(0, LAYERS, backward, 0)

    copies = []
    for slot, target in enumerate((keep_ref, send_ref)):
        half = jnp.bitwise_xor(core, slot)
        first = jnp.where(half == 0, place_of(mine, parts, 0), place_of(mine, parts, 1))
        for part in range(parts):
            change = jnp.where(half == 0, place_of(part, parts, 0), place_of(part, parts, 1))
            source = stage_ref.at[half, pl.ds(part * part_rows, part_rows), :]
            place = target.at[jnp.bitwise_xor(first, change)]
            copies.append(pltpu.make_async_copy(source, place, handed.at[slot, part]))
    for copy in copies:
        copy.start()
    for image in range(images):
        compact(dtok_ref, image, h_ref[LAYERS, pl.ds(image * IMG, IMG), :])
    for copy in copies:
        copy.wait()


def digits_of(parts, core):
    digits, stride = [], 1
    while stride < parts:
        size = 4 if parts // stride % 4 == 0 else 2
        digits.append((size, stride))
        stride *= size
    if len({size for size, _ in digits}) == 1 and core == 1:
        digits = digits[1:] + digits[:1]
    return digits


def place_of(index, parts, core):
    place = 0
    for size, stride in digits_of(parts, core):
        place = place * size + index // stride % size
    return place


def unpack_kernel(
    own_ref,
    other_ref,
    g1_ref,
    b1_ref,
    gqkv_ref,
    glepe_ref,
    glepeb_ref,
    gproj_ref,
    gbproj_ref,
    g2_ref,
    b2_ref,
    gfc1_ref,
    gbfc1_ref,
    gfc2_ref,
    gbfc2_ref,
    stage_ref,
):
    parts = own_ref.shape[0]
    part_rows = own_ref.shape[1]
    core = lax.axis_index("heads")
    mine = lax.axis_index("dp")
    for slot, ref in enumerate((own_ref, other_ref)):
        half = jnp.bitwise_xor(core, slot)
        first = jnp.where(half == 0, place_of(mine, parts, 0), place_of(mine, parts, 1))
        for part in range(parts):
            change = jnp.where(half == 0, place_of(part, parts, 0), place_of(part, parts, 1))
            stage_ref[half, part * part_rows : (part + 1) * part_rows, :] = ref[jnp.bitwise_xor(first, change)]

    for layer in range(LAYERS):
        base = layer * PACKED
        for half in range(2):
            for piece in range(4):
                lanes = slice(half * 512 + piece * HW, half * 512 + (piece + 1) * HW)
                at = base + FC1_AT + 256 * piece
                gfc1_ref[layer, :, lanes] = stage_ref[half, at : at + 256, :].astype(F32)
                at = base + FC2_AT + 256 * piece
                gfc2_ref[layer, lanes, :] = stage_ref[half, at : at + 256, :].astype(F32).T
            gproj_ref[layer, :, half * HW : (half + 1) * HW] = stage_ref[
                half, base + PROJ_AT : base + PROJ_AT + 256, :
            ].astype(F32)
        for piece in range(3):
            at = base + QKV_AT + 256 * piece
            gqkv_ref[layer, 0, :, piece * HW : (piece + 1) * HW] = stage_ref[core, at : at + 256, :].astype(F32)
        small = stage_ref[core, base + SMALL_AT : base + PACKED, :].astype(F32)
        glepe_ref[layer, :, 0] = small[:TAPS]
        glepeb_ref[layer] = small[TAPS : TAPS + 1]
        small = stage_ref[0, base + SMALL_AT : base + PACKED, :].astype(F32)
        for place, ref in enumerate((g1_ref, b1_ref, gbproj_ref, g2_ref, b2_ref, gbfc2_ref)):
            for piece in range(2):
                row = 10 + 6 * piece + place
                ref[layer : layer + 1, piece * HW : (piece + 1) * HW] = small[row : row + 1]
        small = stage_ref[1, base + SMALL_AT : base + PACKED, :].astype(F32)
        for piece in range(8):
            gbfc1_ref[layer : layer + 1, piece * HW : (piece + 1) * HW] = small[10 + piece : 11 + piece]


SMEM = pl.BlockSpec(memory_space=pltpu.SMEM)
VMEM = pl.BlockSpec(memory_space=pltpu.VMEM)
ANY = pl.BlockSpec(memory_space=pl.ANY)


def shards(
    dp,
    tokens,
    cotangent,
    counts,
    ln1_gain,
    ln1_bias,
    w_qkv,
    lepe_w,
    lepe_b,
    w_proj,
    b_proj,
    ln2_gain,
    ln2_bias,
    w_fc1,
    b_fc1,
    w_fc2,
    b_fc2,
):
    tokens_here = tokens.shape[0]
    images = tokens_here // TOK_IMG
    rows = images * IMG
    swap = [(0, 1), (1, 0)]

    def across(value):
        return lax.ppermute(value, "heads", swap)

    part_rows = -(-ALL_PACKED // (16 * dp)) * 16
    wide, tall = shift_tables()
    table = place_table()
    scratch = [
        pltpu.VMEM((tokens_here, D), BF),
        pltpu.VMEM((LAYERS, D, D), BF),
        pltpu.VMEM((LAYERS, D, FF), BF),
        pltpu.VMEM((LAYERS, FF, D), BF),
        pltpu.VMEM((3, BLOCK, TAPS * KEYS), BF),
        pltpu.VMEM((TAPS * BLOCK, KEYS), BF),
        pltpu.SemaphoreType.DMA((8,)),
        pltpu.SemaphoreType.DMA((2, dp)),
        pltpu.VMEM((2, LAYERS, D, 3 * HW), BF),
        pltpu.VMEM((2, LAYERS, 16, HW), F32),
        pltpu.VMEM((LAYERS + 1, rows, D), F32),
        pltpu.VMEM((LAYERS, 2, rows, D), BF),
        pltpu.VMEM((LAYERS, 2, rows, 3 * HW), BF),
        pltpu.VMEM((LAYERS, 2, rows, SPAN), BF),
        pltpu.VMEM((rows // 16, 2, TILE, D), F32),
        pltpu.VMEM((LAYERS, rows, D), BF),
        pltpu.VMEM((LAYERS, rows, D), F32),
        pltpu.VMEM((LAYERS, rows, D), BF),
        pltpu.VMEM((LAYERS, rows, FF), BF),
        pltpu.VMEM((LAYERS, rows, FF), BF),
        pltpu.VMEM((rows, D), BF),
        pltpu.VMEM((rows, D), BF),
        pltpu.VMEM((rows, FF), BF),
        pltpu.VMEM((rows, 6 * HW), BF),
        pltpu.VMEM((6, 8, D), F32),
        pltpu.VMEM((8, FF), F32),
        pltpu.VMEM((D, D), F32),
        pltpu.VMEM((2, D, 3 * HW), F32),
        pltpu.VMEM((2, TAPS + 1, 8, HW), F32),
        pltpu.VMEM((2, SMALL, HW), F32),
        pltpu.VMEM((2, part_rows * dp, HW), BF),
    ]
    result, grad, keep, send = pl.pallas_call(
        step_kernel,
        out_shape=(
            jax.ShapeDtypeStruct((tokens_here, D), BF),
            jax.ShapeDtypeStruct((tokens_here, D), F32),
            jax.ShapeDtypeStruct((dp, part_rows, HW), BF),
            jax.ShapeDtypeStruct((dp, part_rows, HW), BF),
        ),
        in_specs=[SMEM, VMEM, ANY, VMEM, VMEM, ANY, ANY] + [VMEM] * 4 + [ANY] + [VMEM] * 3 + [ANY, VMEM, ANY, VMEM, VMEM, ANY, ANY, VMEM, VMEM],
        out_specs=(VMEM, VMEM, ANY, ANY),
        scratch_shapes=scratch,
        compiler_params=pltpu.CompilerParams(vmem_limit_bytes=60 * 1024 * 1024),
        name="step",
    )(
        counts,
        tokens,
        cotangent,
        ln1_gain,
        ln1_bias,
        w_qkv,
        across(w_qkv),
        lepe_w.swapaxes(1, 2),
        across(lepe_w.swapaxes(1, 2)),
        lepe_b,
        across(lepe_b),
        w_proj,
        b_proj,
        ln2_gain,
        ln2_bias,
        w_fc1,
        b_fc1,
        w_fc2,
        b_fc2,
        jnp.asarray(table, BF),
        jnp.asarray(wide, BF),
        jnp.asarray(tall, BF),
        jnp.asarray(bias_table()),
        jnp.asarray(head_table(), BF),
    )

    def add(first, *rest):
        total = first.astype(F32)
        for item in rest:
            total = total + item.astype(F32)
        return total.astype(BF)

    own = add(keep, across(send))
    orders = [digits_of(dp, core) for core in range(2)]

    def exchange(step, pieces):
        arrived = []
        for hop in range(len(pieces) - 1, 0, -1):
            pairs = []
            for chip in range(dp):
                for core in range(2):
                    partner = chip ^ (hop * orders[core][step][1])
                    pairs.append((2 * chip + core, 2 * partner + core))
            arrived.append(lax.ppermute(pieces[hop], ("dp", "heads"), pairs))
        return lax.optimization_barrier(tuple(arrived))[::-1]

    for step, (size, _) in enumerate(orders[0]):
        pieces = own.reshape((size, own.shape[0] // size) + own.shape[1:])
        own = add(pieces[0], *exchange(step, pieces))
    for step, (size, _) in reversed(list(enumerate(orders[0]))):
        own = jnp.concatenate((own,) + tuple(exchange(step, [own] * size)), axis=0)
    other = across(own)
    grads = list(pl.pallas_call(
        unpack_kernel,
        out_shape=(
            jax.ShapeDtypeStruct((LAYERS, D), F32),
            jax.ShapeDtypeStruct((LAYERS, D), F32),
            jax.ShapeDtypeStruct((LAYERS, 1, D, 3 * HW), F32),
            jax.ShapeDtypeStruct((LAYERS, TAPS, 1, HW), F32),
            jax.ShapeDtypeStruct((LAYERS, 1, HW), F32),
            jax.ShapeDtypeStruct((LAYERS, D, D), F32),
            jax.ShapeDtypeStruct((LAYERS, D), F32),
            jax.ShapeDtypeStruct((LAYERS, D), F32),
            jax.ShapeDtypeStruct((LAYERS, D), F32),
            jax.ShapeDtypeStruct((LAYERS, D, FF), F32),
            jax.ShapeDtypeStruct((LAYERS, FF), F32),
            jax.ShapeDtypeStruct((LAYERS, FF, D), F32),
            jax.ShapeDtypeStruct((LAYERS, D), F32),
        ),
        in_specs=[VMEM] * 2,
        out_specs=(VMEM,) * 13,
        scratch_shapes=[pltpu.VMEM((2, part_rows * dp, HW), BF)],
        compiler_params=pltpu.CompilerParams(vmem_limit_bytes=48 * 1024 * 1024),
        name="unpack",
    )(own, other))
    grads[3] = grads[3].swapaxes(1, 2)
    return (result, grad) + tuple(grads)


def solution(mesh):
    spread = P(("dp", "heads"), None)
    group = (P(None, "heads", None, None), P(None, "heads", None, None), P(None, "heads", None))
    in_specs = (spread, spread, P("dp"), P(), P()) + group + (P(),) * 8
    out_specs = (spread, spread, P(), P()) + group + (P(),) * 8
    return jax.shard_map(
        functools.partial(shards, mesh.shape["dp"]),
        mesh=mesh,
        in_specs=in_specs,
        out_specs=out_specs,
        check_vma=False,
    )
```

```python
import functools
import math

import jax
import jax.numpy as jnp
import numpy as np
from jax import lax
from jax.experimental import pallas as pl
from jax.experimental.pallas import tpu as pltpu
from jax.sharding import PartitionSpec as P

D = 256
FF = 1024
HD = 32
GH = 4
HW = 128
LAYERS = 2
TOK_IMG = 608
SPLIT = 392
EPSILON = 1e-05

TILE = 8
TILES = 14
BLOCK = TILES * TILE
CHUNK = 2 * BLOCK
IMG = 6 * BLOCK
KEYS = 128
SPAN = GH * KEYS
TAPS = 9
SCALE = HD**-0.5
EXP_SCALE = SCALE * math.log2(math.e)
BF = jnp.bfloat16
F32 = jnp.float32

FC1_AT = 0
FC2_AT = 1024
PROJ_AT = 2048
QKV_AT = 2304
SMALL_AT = 3072
SMALL = 32
PACKED = SMALL_AT + SMALL
ALL_PACKED = LAYERS * PACKED


def place_table():
    table = np.zeros((IMG, TOK_IMG), np.float32)
    for crop in range(2):
        for row in range(14):
            for col in range(14):
                place = crop * CHUNK + row * 16 + (col // 7) * TILE + col % 7
                table[place, crop * 196 + row * 14 + col] = 1
    for group in range(2):
        for cell in range(108):
            table[2 * CHUNK + group * BLOCK + cell, SPLIT + group * 108 + cell] = 1
    return table


def window_cells(kind):
    cells = [None] * BLOCK
    if kind == 2:
        for place in range(108):
            cells[place] = (place // 36, place % 36 // 6, place % 6)
    else:
        for place in range(BLOCK):
            tile, col = divmod(place, TILE)
            if col < 7:
                cells[place] = (0, tile // 2, 7 * (tile % 2) + col) if kind == 0 else (0, tile, col)
    return cells


def shift_tables():
    wide = np.zeros((3, BLOCK, TAPS * KEYS), np.float32)
    tall = np.zeros((TAPS * BLOCK, KEYS), np.float32)
    for kind in range(3):
        cells = window_cells(kind)
        spots = {cell: place for place, cell in enumerate(cells) if cell is not None}
        for place, cell in enumerate(cells):
            for tap in range(TAPS):
                other = cell and spots.get((cell[0], cell[1] + tap // 3 - 1, cell[2] + tap % 3 - 1))
                if other is not None:
                    wide[kind, place, tap * KEYS + other] = 1
                    if kind == 2:
                        tall[tap * BLOCK + place, other] = 1
    return wide, tall


def bias_table():
    bias = np.full((2, BLOCK, KEYS), -1e30, np.float32)
    bias[0, [key for key in range(BLOCK) if key % TILE < 7]] = 0
    for query in range(KEYS):
        first, last = (36 * (query // 36), 36 * (query // 36) + 36) if query < 108 else (0, 108)
        bias[1, first:last, query] = 0
    return bias


def head_table():
    table = np.zeros((SPAN, HW), np.float32)
    for head in range(GH):
        table[head * KEYS : (head + 1) * KEYS, head * HD : (head + 1) * HD] = 1
    return table


def dot(left, right):
    return lax.dot_general(left, right, (((1,), (0,)), ((), ())), preferred_element_type=F32)


def dot_nt(left, right):
    return lax.dot_general(left, right, (((1,), (1,)), ((), ())), preferred_element_type=F32)


def dot_tn(left, right):
    return lax.dot_general(left, right, (((0,), (0,)), ((), ())), preferred_element_type=F32)


def norm_parts(value):
    center = value - jnp.mean(value, axis=-1, keepdims=True)
    scale = lax.rsqrt(jnp.mean(center * center, axis=-1, keepdims=True) + EPSILON)
    return center * scale, scale


def norm_back(dout, value, gain):
    xhat, scale = norm_parts(value)
    grown = dout * gain
    mean = jnp.mean(grown, axis=-1, keepdims=True)
    cross = jnp.mean(grown * xhat, axis=-1, keepdims=True)
    return scale * (grown - mean - xhat * cross), dout * xhat


def fold_rows(value):
    return jnp.sum(value.reshape(value.shape[0] // 8, 8, value.shape[1]), axis=0)


def head_rows(value, heads_ref):
    return jnp.concatenate(
        [value * heads_ref[head * KEYS : head * KEYS + 1, :] for head in range(GH)], axis=0
    )


def head_stack(value, heads_ref):
    rows = []
    pad = jnp.zeros((KEYS - BLOCK, HW), BF)
    for head in range(GH):
        rows.append(value * heads_ref[head * KEYS : head * KEYS + 1, :])
        rows.append(pad)
    return jnp.concatenate(rows, axis=0)


def pad_keys(value):
    return jnp.concatenate([value, jnp.zeros((KEYS - BLOCK, value.shape[1]), value.dtype)], axis=0)


def pipeline(stages, items, fillers=()):
    results = [None] * len(items)
    fillers = list(fillers)
    for step in range(len(items) + len(stages) - 1):
        if fillers:
            fillers.pop(0)()
        for place in range(len(stages)):
            item = step - place
            if 0 <= item < len(items):
                results[item] = stages[place](items[item], results[item])
    return results


def split_tiles(value):
    rows = value.shape[0] // 16
    return jnp.concatenate(
        [value[16 * row : 16 * row + 8] for row in range(rows)]
        + [value[16 * row + 8 : 16 * row + 16] for row in range(rows)],
        axis=0,
    )


def join_tiles(value):
    half = value.shape[0] // 2
    pieces = []
    for row in range(half // 8):
        pieces.append(value[8 * row : 8 * row + 8])
        pieces.append(value[half + 8 * row : half + 8 * row + 8])
    return jnp.concatenate(pieces, axis=0)


def as_tiles(value):
    return value.reshape(TILES, TILE, HW)


def live_tiles():
    return lax.broadcasted_iota(jnp.int32, (1, TILE, HW), 1) < TILE - 1


def side_cells(tiles, direction):
    if direction == 1:
        return pltpu.roll(tiles, 1, 1), tiles, pltpu.roll(tiles, TILE - 1, 1)
    last = lax.broadcasted_iota(jnp.int32, (1, TILE, HW), 1) == TILE - 1
    left, right = [], []
    for row in range(TILES // 2):
        near, far = tiles[2 * row : 2 * row + 1], tiles[2 * row + 1 : 2 * row + 2]
        near_left = pltpu.roll(near, 1, 1)
        far_right = pltpu.roll(far, TILE - 1, 1)
        left += [near_left, pltpu.roll(jnp.where(last, near_left, far), 1, 1)]
        right += [pltpu.roll(jnp.where(last, far_right, near), TILE - 1, 1), far_right]
    return jnp.concatenate(left, axis=0), tiles, jnp.concatenate(right, axis=0)


def tap_cells(tiles, direction):
    stride = 2 if direction == 0 else 1
    zeros = jnp.zeros((stride, TILE, HW), F32)
    padded = [jnp.concatenate([zeros, side, zeros], axis=0) for side in side_cells(tiles, direction)]
    return [padded[tap % 3][(tap // 3) * stride : (tap // 3) * stride + TILES] for tap in range(TAPS)]


def tap_row(direction, tap):
    return tap if direction == 0 else 3 * (tap % 3) + tap // 3


def compact(ref, image, value):
    first = image * TOK_IMG
    for tile in range(2 * 2 * TILES):
        ref[first + 7 * tile : first + 7 * tile + 7, :] = value[TILE * tile : TILE * tile + 7]
    for group in range(2):
        at = first + SPLIT + 108 * group
        row = 2 * CHUNK + BLOCK * group
        ref[at : at + 108, :] = value[row : row + 108]


def step_kernel(
    pieces,
    counts_ref,
    tok_ref,
    cot_from,
    g1_ref,
    b1_ref,
    own_wqkv_from,
    other_wqkv_from,
    own_lepe_ref,
    other_lepe_ref,
    own_lepeb_ref,
    other_lepeb_ref,
    wproj_from,
    bproj_ref,
    g2_ref,
    b2_ref,
    wfc1_from,
    bfc1_ref,
    wfc2_from,
    bfc2_ref,
    place_ref,
    wide_from,
    tall_from,
    bias_ref,
    heads_ref,
    out_to,
    dtok_to,
    *rest,
):
    keep_refs, send_refs, rest = rest[:pieces], rest[pieces : 2 * pieces], rest[2 * pieces :]
    (
    out_ref,
    dtok_ref,
    written,
    cot_ref,
    wproj_ref,
    wfc1_ref,
    half_wfc2_ref,
    wide_ref,
    tall_ref,
    fetched,
    handed,
    wqkv_ref,
    lepe_ref,
    h_ref,
    normed_ref,
    qkv_ref,
    probs_ref,
    hf_ref,
    hb_ref,
    inner_ref,
    normed2_ref,
    act_ref,
    slope_ref,
    dz_ref,
    dy_ref,
    dhid_ref,
    dqkv_ref,
    acc_ref,
    bfc1_sum_ref,
    accproj_ref,
    accqkv_ref,
    acclepe_ref,
    small_ref,
    stage_ref,
    ) = rest
    rows_all = h_ref.shape[1]
    images = rows_all // IMG
    chunks = rows_all // CHUNK
    blocks = rows_all // BLOCK
    parts = pieces * keep_refs[0].shape[0]
    part_rows = keep_refs[0].shape[1]
    core = lax.axis_index("heads")
    mine = lax.axis_index("dp")
    moves = (
        (own_wqkv_from.at[:, 0], wqkv_ref.at[core]),
        (other_wqkv_from.at[:, 0], wqkv_ref.at[1 - core]),
        (wproj_from, wproj_ref),
        (wfc1_from, wfc1_ref),
        (wfc2_from, half_wfc2_ref),
        (wide_from, wide_ref),
        (cot_from, cot_ref),
        (tall_from, tall_ref),
    )
    fetches = [pltpu.make_async_copy(*move, fetched.at[place]) for place, move in enumerate(moves)]
    for fetch in fetches:
        fetch.start()
    for direction, (lepe, lepeb) in (
        (core, (own_lepe_ref, own_lepeb_ref)),
        (1 - core, (other_lepe_ref, other_lepeb_ref)),
    ):
        lepe_ref[direction, :, :TAPS] = lepe[:, :, 0]
        lepe_ref[direction, :, TAPS : TAPS + 1] = lepeb[...]

    def chunk_rows(index):
        return pl.ds(index * CHUNK, CHUNK)

    def chunk_tiles(index):
        return pl.ds(index * TILES, TILES)

    def wide_rows(index):
        return pl.ds(index * 2 * CHUNK, 2 * CHUNK)

    def wide_tiles(index):
        return pl.ds(index * 2 * TILES, 2 * TILES)

    def block_rows(index):
        return pl.ds(index * BLOCK, BLOCK)

    def is_small(block):
        return block % 6 >= 4

    def keep_of(image):
        place = lax.broadcasted_iota(jnp.int32, (IMG, 1), 0)
        limit = counts_ref[core * images + image]
        group = (place - 448) // BLOCK
        inside = (place - 448) % BLOCK
        return (place < 448) | (inside < 36 * (limit - 3 * group))

    for image in range(images):
        spot = pl.ds(image * TOK_IMG, TOK_IMG)
        h_ref[0, pl.ds(image * IMG, IMG), :] = dot(place_ref[...], tok_ref[spot, :])

    for fetch in fetches[:6]:
        fetch.wait()
    half_wfc2_ref[...] = half_wfc2_ref[...] * jnp.asarray(0.5, BF)

    def forward(layer, carry):
        gain1, bias1 = g1_ref[pl.ds(layer, 1), :], b1_ref[pl.ds(layer, 1), :]

        def normalize(index, _):
            rows = chunk_rows(index)
            xhat, _ = norm_parts(h_ref[layer, rows, :])
            normed = xhat * gain1 + bias1
            turned = split_tiles(normed) if index % 3 < 2 else normed
            return normed.astype(BF), turned.astype(BF)

        def project(index, values):
            rows = chunk_rows(index)
            for direction, value in enumerate(values):
                normed_ref[layer, direction, rows, :] = value
                qkv_ref[layer, direction, rows, :] = dot(value, wqkv_ref[direction, layer]).astype(BF)

        pipeline((normalize, project), range(chunks))

        def tap_weight(direction, tap):
            return lepe_ref[direction, layer, pl.ds(tap_row(direction, tap), 1), :]

        def score(window, _):
            direction, block = window
            rows = block_rows(block)
            query = qkv_ref[layer, direction, rows, :HW]
            keyset = qkv_ref[layer, direction, rows, HW : 2 * HW]
            return dot_nt(head_rows(keyset, heads_ref), pad_keys(query))

        def weigh(window, scores):
            direction, block = window
            rows = block_rows(block)
            bias = bias_ref[int(is_small(block))]
            probs = []
            for head in range(GH):
                part = scores[head * BLOCK : (head + 1) * BLOCK] + bias
                part = jnp.exp2((part - jnp.max(part, axis=0, keepdims=True)) * EXP_SCALE)
                part = part * (1.0 / jnp.sum(part, axis=0, keepdims=True))
                probs.append(part.astype(BF))
                probs_ref[layer, direction, rows, head * KEYS : (head + 1) * KEYS] = probs[head]
            return probs

        def mix(window, probs):
            direction, block = window
            rows = block_rows(block)
            values = qkv_ref[layer, direction, rows, 2 * HW :]
            side = values.T
            mixed = [dot(side[head * HD : (head + 1) * HD], probs[head]) for head in range(GH)]
            return jnp.concatenate(mixed, axis=0)

        def finish(window, mixed):
            direction, block = window
            lanes = slice(direction * HW, (direction + 1) * HW)
            result = mixed.T[:BLOCK] + lepe_ref[direction, layer, TAPS : TAPS + 1, :] + local[window]
            if direction == 0 or is_small(block):
                hf_ref[block * 7 : block * 7 + 7, :, :, lanes] = result.reshape(7, 2, TILE, HW)
            else:
                side = block % 2
                rows = slice((block - side) * 7, (block - side) * 7 + TILES)
                hf_ref[rows, side, :, lanes] = as_tiles(result)

        local = {}

        def filter_pair(kind, windows):
            scaled = []
            for direction, block in windows:
                values = qkv_ref[layer, direction, block_rows(block), 2 * HW :]
                scaled.append(
                    jnp.concatenate(
                        [pad_keys(values * tap_weight(direction, tap).astype(BF)) for tap in range(TAPS)], axis=0
                    )
                )
            both = dot(wide_ref[kind], jnp.concatenate(scaled, axis=1))
            for place, window in enumerate(windows):
                local[window] = both[:, place * HW : (place + 1) * HW]

        windows, fillers = [], []
        for block in range(blocks):
            windows += [(direction, block) for direction in range(2)]
            if is_small(block):
                fillers.append(functools.partial(filter_pair, 2, windows[-2:]))
            elif block % 2 == 1:
                for direction in range(2):
                    pair = [(direction, block - 1), (direction, block)]
                    fillers.append(functools.partial(filter_pair, direction, pair))
        pipeline((score, weigh, mix, finish), windows, fillers)

        gain2, bias2 = g2_ref[pl.ds(layer, 1), :], b2_ref[pl.ds(layer, 1), :]

        def join(index, _):
            rows = chunk_rows(index)
            heads = hf_ref[chunk_tiles(index)].reshape(CHUNK, D).astype(BF)
            hb_ref[layer, rows, :] = heads
            inner = h_ref[layer, rows, :] + dot(heads, wproj_ref[layer]) + bproj_ref[pl.ds(layer, 1), :]
            inner_ref[layer, rows, :] = inner
            return inner

        def widen(index, inner):
            xhat, _ = norm_parts(inner)
            normed2 = (xhat * gain2 + bias2).astype(BF)
            normed2_ref[layer, chunk_rows(index), :] = normed2
            return dot(normed2, wfc1_ref[layer])

        def narrow(index, hidden):
            rows = chunk_rows(index)
            hidden = hidden + bfc1_ref[pl.ds(layer, 1), :]
            cdf = 1.0 + lax.erf(hidden * math.sqrt(0.5))
            act = (hidden * cdf).astype(BF)
            act_ref[layer, rows, :] = act
            bell = jnp.exp2(hidden * hidden * (-0.5 * math.log2(math.e)))
            slope_ref[layer, rows, :] = (cdf + hidden * bell * math.sqrt(2 / math.pi)).astype(BF)
            return dot(act, half_wfc2_ref[layer])

        def close(index, branch):
            rows = chunk_rows(index)
            h_ref[layer + 1, rows, :] = inner_ref[layer, rows, :] + branch + bfc2_ref[pl.ds(layer, 1), :]

        pipeline((join, widen, narrow, close), range(chunks))
        return carry

    lax.fori_loop(0, LAYERS, forward, 0)
    for fetch in fetches[6:]:
        fetch.wait()

    for image in range(images):
        spot = pl.ds(image * TOK_IMG, TOK_IMG)
        wide = pl.ds(image * IMG, IMG)
        keep = keep_of(image)
        compact(dtok_ref, image, jnp.where(keep, h_ref[LAYERS, wide, :], 0.0))
        h_ref[LAYERS, wide, :] = jnp.where(keep, dot(place_ref[...], cot_ref[spot, :]), 0.0)
    out_ref[...] = dtok_ref[...].astype(BF)
    out_copy = pltpu.make_async_copy(out_ref, out_to, written.at[0])
    out_copy.start()

    def backward(step, carry):
        layer = LAYERS - 1 - step
        base = pl.multiple_of(layer * PACKED, 16)
        acc_ref[...] = jnp.zeros_like(acc_ref)
        acclepe_ref[...] = jnp.zeros_like(acclepe_ref)

        accproj_ref[...] = jnp.zeros_like(accproj_ref)
        bfc1_sum_ref[...] = jnp.zeros_like(bfc1_sum_ref)
        gain2 = g2_ref[pl.ds(layer, 1), :]

        def pair_rows(index):
            return pl.ds((index - 1) * CHUNK, 2 * CHUNK)

        def widen(index, _):
            rows = wide_rows(index)
            dz = h_ref[LAYERS, rows, :].astype(BF)
            dz_ref[rows, :] = dz
            acc_ref[5] += fold_rows(dz.astype(F32))
            return dot_nt(dz, half_wfc2_ref[layer])

        def narrow(index, dact):
            rows = wide_rows(index)
            dhid = dact * slope_ref[layer, rows, :].astype(F32)
            bfc1_sum_ref[...] += fold_rows(dhid)
            dhid = dhid.astype(BF)
            dhid_ref[rows, :] = dhid
            return dot_nt(dhid, wfc1_ref[layer])

        def close(index, dnormed):
            rows = wide_rows(index)
            dvalue, dgain = norm_back(dnormed, inner_ref[layer, rows, :], gain2)
            acc_ref[3] += fold_rows(dgain)
            acc_ref[4] += fold_rows(dnormed)
            dinner = h_ref[LAYERS, rows, :] + dvalue
            h_ref[LAYERS, rows, :] = dinner
            dy = dinner.astype(BF)
            dy_ref[rows, :] = dy
            acc_ref[2] += fold_rows(dy.astype(F32))
            return dot_nt(dy, wproj_ref[layer])

        def project(index, dheads):
            hf_ref[wide_tiles(index)] = dheads.reshape(2 * TILES, 2, TILE, D)
            rows = wide_rows(index)
            accproj_ref[...] += dot_tn(hb_ref[layer, rows, :], dy_ref[rows, :])

        pipeline((widen, narrow, close, project), range(chunks // 2))
        for half in range(2):
            stage_ref[half, pl.ds(base + PROJ_AT, D), :] = accproj_ref[:, half * HW : (half + 1) * HW].astype(BF)

        def tap_weight(direction, tap):
            return lepe_ref[direction, layer, pl.ds(tap_row(direction, tap), 1), :]

        def grad_of(direction, block):
            lanes = slice(direction * HW, (direction + 1) * HW)
            if direction == 0 or is_small(block):
                tiles = hf_ref[block * 7 : block * 7 + 7, :, :, lanes]
            else:
                side = block % 2
                tiles = hf_ref[(block - side) * 7 : (block - side) * 7 + TILES, side, :, lanes]
            return tiles.reshape(BLOCK, HW).astype(BF)

        def score(window, _):
            direction, block = window
            rows = block_rows(block)
            grad = grad_of(direction, block)
            values = qkv_ref[layer, direction, rows, 2 * HW :]
            return dot_nt(head_rows(values, heads_ref), pad_keys(grad))

        def weigh(window, dprobs):
            direction, block = window
            rows = block_rows(block)
            dscores = []
            for head in range(GH):
                part = probs_ref[layer, direction, rows, head * KEYS : (head + 1) * KEYS].astype(F32)
                dpart = dprobs[head * BLOCK : (head + 1) * BLOCK]
                inner = jnp.sum(part * dpart, axis=0, keepdims=True)
                dscores.append((part * (dpart - inner)).astype(BF))
            return dscores

        def mix(window, dscores):
            direction, block = window
            rows = block_rows(block)
            grad = grad_of(direction, block)
            query = qkv_ref[layer, direction, rows, :HW]
            side = qkv_ref[layer, direction, rows, HW : 2 * HW].T
            dkeys = dot(jnp.concatenate(dscores, axis=1), head_stack(query, heads_ref))
            dvalues = dot(probs_ref[layer, direction, rows, :], head_stack(grad, heads_ref))
            dquery = [dot(side[head * HD : (head + 1) * HD], dscores[head]) for head in range(GH)]
            return jnp.concatenate(dquery, axis=0), dkeys, dvalues

        def finish(window, results):
            direction, block = window
            rows = block_rows(block)
            grad = grad_of(direction, block)
            lanes = slice(direction * HW, (direction + 1) * HW)
            dquery, dkeys, dvalues = results
            values = qkv_ref[layer, direction, rows, 2 * HW :]
            first = direction * 3 * HW
            dqkv_ref[rows, first : first + HW] = (dquery * SCALE).T[:BLOCK].astype(BF)
            dqkv_ref[rows, first + HW : first + 2 * HW] = (dkeys * SCALE).astype(BF)
            if is_small(block):
                dvalues = dvalues + local[block][:, lanes]
                dqkv_ref[rows, first + 2 * HW : first + 3 * HW] = dvalues.astype(BF)
                return None
            grad_tiles = as_tiles(grad.astype(F32))
            result = as_tiles(dvalues)
            for tap, cells in enumerate(tap_cells(grad_tiles, direction)):
                result = result + cells * tap_weight(direction, TAPS - 1 - tap).reshape(1, 1, HW)
            result = jnp.where(live_tiles(), result, 0.0).reshape(BLOCK, HW)
            dqkv_ref[rows, first + 2 * HW : first + 3 * HW] = result.astype(BF)
            tiles = jnp.where(live_tiles(), as_tiles(values.astype(F32)), 0.0)
            for tap, cells in enumerate(tap_cells(tiles, direction)):
                acclepe_ref[direction, tap_row(direction, tap)] += jnp.sum(grad_tiles * cells, axis=0)
            acclepe_ref[direction, TAPS] += jnp.sum(grad_tiles, axis=0)
            return None

        half_rows = rows_all // 2
        spans = [pl.ds(part * half_rows, half_rows) for part in range(2)]
        sides = {}

        def feed_weights(index):
            width = FF // (2 * images)
            cols = pl.ds(index * width, width)
            partial = []

            def first(part):
                rows = spans[part]
                if (0, part) not in sides:
                    sides[0, part] = normed2_ref[layer, rows, :].T
                partial.append(dot(sides[0, part], dhid_ref[rows, cols]))

            def second(part):
                rows = spans[part]
                if (1, part) not in sides:
                    sides[1, part] = dz_ref[rows, :].T
                partial.append(dot(sides[1, part], act_ref[layer, rows, cols]))

            def store(at):
                total = partial[0] + partial[1]
                if at == FC2_AT:
                    total = total * 0.5
                for piece in range(width // HW):
                    column = index * (width // HW) + piece
                    place = pl.multiple_of(base + at + column % 4 * 256, 16)
                    value = total[:, piece * HW : (piece + 1) * HW].astype(BF)
                    stage_ref[column // 4, pl.ds(place, 256), :] = value
                partial.clear()

            return [
                lambda: first(0),
                lambda: (first(1), store(FC1_AT)),
                lambda: second(0),
                lambda: (second(1), store(FC2_AT)),
            ]

        local = {}

        def filter_small(block):
            scaled = []
            for direction in range(2):
                padded = pad_keys(grad_of(direction, block).astype(F32))
                scaled.append(
                    jnp.concatenate(
                        [(padded * tap_weight(direction, TAPS - 1 - tap)).astype(BF) for tap in range(TAPS)], axis=0
                    )
                )
            local[block] = dot(wide_ref[2], jnp.concatenate(scaled, axis=1))

        def shift_small(block):
            values = [pad_keys(qkv_ref[layer, direction, block_rows(block), 2 * HW :]) for direction in range(2)]
            shifted = dot(tall_ref[...], jnp.concatenate(values, axis=1))
            for direction in range(2):
                lanes = slice(direction * HW, (direction + 1) * HW)
                grad = grad_of(direction, block).astype(F32)
                for tap in range(TAPS):
                    acclepe_ref[direction, tap_row(direction, tap)] += fold_rows(
                        grad * shifted[tap * BLOCK : (tap + 1) * BLOCK, lanes]
                    )
                acclepe_ref[direction, TAPS] += fold_rows(grad)

        order = [block for block in range(blocks) if not is_small(block)]
        order += [block for block in range(blocks) if is_small(block)]
        windows = [(direction, block) for block in order for direction in range(2)]
        fillers = [filler for index in range(2 * images) for filler in feed_weights(index)]
        for block in order:
            if is_small(block):
                fillers += [functools.partial(filter_small, block), functools.partial(shift_small, block)]
        pipeline((score, weigh, mix, finish), windows, fillers)

        accqkv_ref[...] = jnp.zeros_like(accqkv_ref)
        gain1 = g1_ref[pl.ds(layer, 1), :]

        def collect(index, _):
            rows = chunk_rows(index)
            return [
                dot_nt(dqkv_ref[rows, direction * 3 * HW : (direction + 1) * 3 * HW], wqkv_ref[direction, layer])
                for direction in range(2)
            ]

        def weigh_inputs(index, dnormed):
            if index % 2 == 1:
                rows = pair_rows(index)
                for direction in range(2):
                    accqkv_ref[direction] += dot(
                        normed_ref[layer, direction, rows, :].T,
                        dqkv_ref[rows, direction * 3 * HW : (direction + 1) * 3 * HW],
                    )
            return dnormed

        def spread(index, dnormed):
            rows = chunk_rows(index)
            straight, turned = dnormed
            dnormed = straight + (join_tiles(turned) if index % 3 < 2 else turned)
            dvalue, dgain = norm_back(dnormed, h_ref[layer, rows, :], gain1)
            acc_ref[0] += fold_rows(dgain)
            acc_ref[1] += fold_rows(dnormed)
            h_ref[LAYERS, rows, :] = h_ref[LAYERS, rows, :] + dvalue

        pipeline((collect, weigh_inputs, spread), range(chunks))
        small_ref[...] = jnp.zeros_like(small_ref)
        for direction in range(2):
            for piece in range(3):
                at = QKV_AT + 256 * piece
                stage_ref[direction, pl.ds(base + at, 256), :] = accqkv_ref[
                    direction, :, piece * HW : (piece + 1) * HW
                ].astype(BF)
            small_ref[direction, :10, :] = jnp.sum(acclepe_ref[direction], axis=1)
        sums = jnp.sum(acc_ref[...], axis=1)
        for piece in range(2):
            small_ref[0, 10 + 6 * piece : 16 + 6 * piece, :] = sums[:, piece * HW : (piece + 1) * HW]
        sums = jnp.sum(bfc1_sum_ref[...], axis=0, keepdims=True)
        for piece in range(8):
            small_ref[1, 10 + piece : 11 + piece, :] = sums[:, piece * HW : (piece + 1) * HW]
        stage_ref[:, pl.ds(base + SMALL_AT, SMALL), :] = small_ref[...].astype(BF)

        return carry

    stage_ref[:, ALL_PACKED:, :] = jnp.zeros((2, stage_ref.shape[1] - ALL_PACKED, HW), BF)
    lax.fori_loop(0, LAYERS, backward, 0)

    copies = []
    for slot, targets in enumerate((keep_refs, send_refs)):
        half = jnp.bitwise_xor(core, slot)
        for place in range(parts):
            part = jnp.bitwise_xor(part_at(place, parts, half), mine)
            source = stage_ref.at[half, pl.ds(pl.multiple_of(part * part_rows, 16), part_rows), :]
            target = targets[place * pieces // parts].at[place % (parts // pieces)]
            copies.append(pltpu.make_async_copy(source, target, handed.at[slot, place]))
    for copy in copies:
        copy.start()
    for image in range(images):
        compact(dtok_ref, image, h_ref[LAYERS, pl.ds(image * IMG, IMG), :])
    dtok_copy = pltpu.make_async_copy(dtok_ref, dtok_to, written.at[1])
    dtok_copy.start()
    out_copy.wait()
    for copy in copies:
        copy.wait()
    dtok_copy.wait()


def digits_of(parts, core):
    digits, stride = [], 1
    while stride < parts:
        size = 4 if parts // stride % 4 == 0 else 2
        digits.append((size, stride))
        stride *= size
    if len({size for size, _ in digits}) == 1 and core == 1:
        digits = digits[1:] + digits[:1]
    return digits


def part_at(place, parts, core):
    found = []
    for which in range(2):
        index, left = 0, place
        for size, stride in reversed(digits_of(parts, which)):
            index += left % size * stride
            left //= size
        found.append(index)
    return jnp.where(core == 0, found[0], found[1])


def unpack_kernel(
    pieces,
    *refs,
):
    own_refs, other_refs, refs = refs[:pieces], refs[pieces : 2 * pieces], refs[2 * pieces :]
    (
    g1_ref,
    b1_ref,
    gqkv_ref,
    glepe_ref,
    glepeb_ref,
    gproj_ref,
    gbproj_ref,
    g2_ref,
    b2_ref,
    gfc1_ref,
    gbfc1_ref,
    gfc2_ref,
    gbfc2_ref,
    stage_ref,
    ) = refs
    parts = pieces * own_refs[0].shape[0]
    part_rows = own_refs[0].shape[1]
    core = lax.axis_index("heads")
    mine = lax.axis_index("dp")
    for slot, sources in enumerate((own_refs, other_refs)):
        half = jnp.bitwise_xor(core, slot)
        for place in range(parts):
            part = jnp.bitwise_xor(part_at(place, parts, 0), mine)
            at = pl.ds(pl.multiple_of(part * part_rows, 16), part_rows)
            stage_ref[half, at, :] = sources[place * pieces // parts][place % (parts // pieces)]

    for layer in range(LAYERS):
        base = layer * PACKED
        for half in range(2):
            for piece in range(4):
                lanes = slice(half * 512 + piece * HW, half * 512 + (piece + 1) * HW)
                at = base + FC1_AT + 256 * piece
                gfc1_ref[layer, :, lanes] = stage_ref[half, at : at + 256, :].astype(F32)
                at = base + FC2_AT + 256 * piece
                gfc2_ref[layer, lanes, :] = stage_ref[half, at : at + 256, :].astype(F32).T
            gproj_ref[layer, :, half * HW : (half + 1) * HW] = stage_ref[
                half, base + PROJ_AT : base + PROJ_AT + 256, :
            ].astype(F32)
        for piece in range(3):
            at = base + QKV_AT + 256 * piece
            gqkv_ref[layer, 0, :, piece * HW : (piece + 1) * HW] = stage_ref[core, at : at + 256, :].astype(F32)
        small = stage_ref[core, base + SMALL_AT : base + PACKED, :].astype(F32)
        glepe_ref[layer, :, 0] = small[:TAPS]
        glepeb_ref[layer] = small[TAPS : TAPS + 1]
        small = stage_ref[0, base + SMALL_AT : base + PACKED, :].astype(F32)
        for place, ref in enumerate((g1_ref, b1_ref, gbproj_ref, g2_ref, b2_ref, gbfc2_ref)):
            for piece in range(2):
                row = 10 + 6 * piece + place
                ref[layer : layer + 1, piece * HW : (piece + 1) * HW] = small[row : row + 1]
        small = stage_ref[1, base + SMALL_AT : base + PACKED, :].astype(F32)
        for piece in range(8):
            gbfc1_ref[layer : layer + 1, piece * HW : (piece + 1) * HW] = small[10 + piece : 11 + piece]


SMEM = pl.BlockSpec(memory_space=pltpu.SMEM)
VMEM = pl.BlockSpec(memory_space=pltpu.VMEM)
ANY = pl.BlockSpec(memory_space=pl.ANY)


def shards(
    dp,
    tokens,
    cotangent,
    counts,
    ln1_gain,
    ln1_bias,
    w_qkv,
    lepe_w,
    lepe_b,
    w_proj,
    b_proj,
    ln2_gain,
    ln2_bias,
    w_fc1,
    b_fc1,
    w_fc2,
    b_fc2,
):
    tokens_here = tokens.shape[0]
    images = tokens_here // TOK_IMG
    rows = images * IMG
    swap = [(0, 1), (1, 0)]

    def across(value):
        return lax.ppermute(value, "heads", swap)

    part_rows = -(-ALL_PACKED // (16 * dp)) * 16
    wide, tall = shift_tables()
    table = place_table()
    scratch = [
        pltpu.VMEM((tokens_here, D), BF),
        pltpu.VMEM((tokens_here, D), F32),
        pltpu.SemaphoreType.DMA((2,)),
        pltpu.VMEM((tokens_here, D), BF),
        pltpu.VMEM((LAYERS, D, D), BF),
        pltpu.VMEM((LAYERS, D, FF), BF),
        pltpu.VMEM((LAYERS, FF, D), BF),
        pltpu.VMEM((3, BLOCK, TAPS * KEYS), BF),
        pltpu.VMEM((TAPS * BLOCK, KEYS), BF),
        pltpu.SemaphoreType.DMA((8,)),
        pltpu.SemaphoreType.DMA((2, dp)),
        pltpu.VMEM((2, LAYERS, D, 3 * HW), BF),
        pltpu.VMEM((2, LAYERS, 16, HW), F32),
        pltpu.VMEM((LAYERS + 1, rows, D), F32),
        pltpu.VMEM((LAYERS, 2, rows, D), BF),
        pltpu.VMEM((LAYERS, 2, rows, 3 * HW), BF),
        pltpu.VMEM((LAYERS, 2, rows, SPAN), BF),
        pltpu.VMEM((rows // 16, 2, TILE, D), F32),
        pltpu.VMEM((LAYERS, rows, D), BF),
        pltpu.VMEM((LAYERS, rows, D), F32),
        pltpu.VMEM((LAYERS, rows, D), BF),
        pltpu.VMEM((LAYERS, rows, FF), BF),
        pltpu.VMEM((LAYERS, rows, FF), BF),
        pltpu.VMEM((rows, D), BF),
        pltpu.VMEM((rows, D), BF),
        pltpu.VMEM((rows, FF), BF),
        pltpu.VMEM((rows, 6 * HW), BF),
        pltpu.VMEM((6, 8, D), F32),
        pltpu.VMEM((8, FF), F32),
        pltpu.VMEM((D, D), F32),
        pltpu.VMEM((2, D, 3 * HW), F32),
        pltpu.VMEM((2, TAPS + 1, 8, HW), F32),
        pltpu.VMEM((2, SMALL, HW), F32),
        pltpu.VMEM((2, part_rows * dp, HW), BF),
    ]
    pieces = digits_of(dp, 0)[0][0]
    piece = jax.ShapeDtypeStruct((dp // pieces, part_rows, HW), BF)
    result, grad, *packed = pl.pallas_call(
        functools.partial(step_kernel, pieces),
        out_shape=(
            jax.ShapeDtypeStruct((tokens_here, D), BF),
            jax.ShapeDtypeStruct((tokens_here, D), F32),
        )
        + (piece,) * (2 * pieces),
        in_specs=[SMEM, VMEM, ANY, VMEM, VMEM, ANY, ANY] + [VMEM] * 4 + [ANY] + [VMEM] * 3 + [ANY, VMEM, ANY, VMEM, VMEM, ANY, ANY, VMEM, VMEM],
        out_specs=(ANY,) * (2 + 2 * pieces),
        scratch_shapes=scratch,
        compiler_params=pltpu.CompilerParams(vmem_limit_bytes=60 * 1024 * 1024),
        name="step",
    )(
        counts,
        tokens,
        cotangent,
        ln1_gain,
        ln1_bias,
        w_qkv,
        across(w_qkv),
        lepe_w.swapaxes(1, 2),
        across(lepe_w.swapaxes(1, 2)),
        lepe_b,
        across(lepe_b),
        w_proj,
        b_proj,
        ln2_gain,
        ln2_bias,
        w_fc1,
        b_fc1,
        w_fc2,
        b_fc2,
        jnp.asarray(table, BF),
        jnp.asarray(wide, BF),
        jnp.asarray(tall, BF),
        jnp.asarray(bias_table()),
        jnp.asarray(head_table(), BF),
    )

    def add(first, *rest):
        total = first.astype(F32)
        for item in rest:
            total = total + item.astype(F32)
        return total.astype(BF)

    keep, send = packed[:pieces], packed[pieces:]
    orders = [digits_of(dp, core) for core in range(2)]

    def hop_pairs(orders, step, hop):
        pairs = []
        for chip in range(dp):
            for core in range(2):
                pairs.append((2 * chip + core, 2 * (chip ^ (hop * orders[core][step][1])) + core))
        return pairs

    def exchange(step, values, orders=orders):
        arrived = [
            lax.ppermute(values[hop], ("dp", "heads"), hop_pairs(orders, step, hop)) for hop in range(len(values) - 1, 0, -1)
        ]
        return arrived[::-1]

    received = [across(send[hop]) for hop in range(pieces - 1, -1, -1)][::-1]
    sums = [None] + [add(keep[hop], received[hop]) for hop in range(1, pieces)]
    arrived = lax.optimization_barrier(tuple(exchange(0, sums)))
    own = add(keep[0], received[0], *arrived)
    for step in range(1, len(orders[0])):
        size = orders[0][step][0]
        cuts = own.reshape((size, own.shape[0] // size) + own.shape[1:])
        own = add(cuts[0], *lax.optimization_barrier(tuple(exchange(step, cuts))))
    for step in range(len(orders[0]) - 1, 0, -1):
        arrived = lax.optimization_barrier(tuple(exchange(step, [own] * orders[0][step][0], orders[:1] * 2)))
        own = jnp.concatenate((own,) + tuple(arrived), axis=0)
    whole = [own] + exchange(0, [own] * pieces, orders[:1] * 2)
    others = [across(value) for value in whole]
    grads = list(pl.pallas_call(
        functools.partial(unpack_kernel, pieces),
        out_shape=(
            jax.ShapeDtypeStruct((LAYERS, D), F32),
            jax.ShapeDtypeStruct((LAYERS, D), F32),
            jax.ShapeDtypeStruct((LAYERS, 1, D, 3 * HW), F32),
            jax.ShapeDtypeStruct((LAYERS, TAPS, 1, HW), F32),
            jax.ShapeDtypeStruct((LAYERS, 1, HW), F32),
            jax.ShapeDtypeStruct((LAYERS, D, D), F32),
            jax.ShapeDtypeStruct((LAYERS, D), F32),
            jax.ShapeDtypeStruct((LAYERS, D), F32),
            jax.ShapeDtypeStruct((LAYERS, D), F32),
            jax.ShapeDtypeStruct((LAYERS, D, FF), F32),
            jax.ShapeDtypeStruct((LAYERS, FF), F32),
            jax.ShapeDtypeStruct((LAYERS, FF, D), F32),
            jax.ShapeDtypeStruct((LAYERS, D), F32),
        ),
        in_specs=[VMEM] * (2 * pieces),
        out_specs=(VMEM,) * 13,
        scratch_shapes=[pltpu.VMEM((2, part_rows * dp, HW), BF)],
        compiler_params=pltpu.CompilerParams(vmem_limit_bytes=48 * 1024 * 1024),
        name="unpack",
    )(*whole, *others))
    grads[3] = grads[3].swapaxes(1, 2)
    return (result, grad) + tuple(grads)


def solution(mesh):
    spread = P(("dp", "heads"), None)
    group = (P(None, "heads", None, None), P(None, "heads", None, None), P(None, "heads", None))
    in_specs = (spread, spread, P("dp"), P(), P()) + group + (P(),) * 8
    out_specs = (spread, spread, P(), P()) + group + (P(),) * 8
    return jax.shard_map(
        functools.partial(shards, mesh.shape["dp"]),
        mesh=mesh,
        in_specs=in_specs,
        out_specs=out_specs,
        check_vma=False,
    )
```

```python
import functools
import math

import jax
import jax.numpy as jnp
import numpy as np
from jax import lax
from jax.experimental import pallas as pl
from jax.experimental.pallas import tpu as pltpu
from jax.sharding import PartitionSpec as P

D = 256
FF = 1024
HD = 32
GH = 4
HW = 128
LAYERS = 2
TOK_IMG = 608
SPLIT = 392
EPSILON = 1e-05

TILE = 8
TILES = 14
BLOCK = TILES * TILE
CHUNK = 2 * BLOCK
IMG = 6 * BLOCK
KEYS = 128
SPAN = GH * KEYS
TAPS = 9
SCALE = HD**-0.5
EXP_SCALE = SCALE * math.log2(math.e)
BF = jnp.bfloat16
F32 = jnp.float32

FC1_AT = 0
FC2_AT = 1024
PROJ_AT = 2048
QKV_AT = 2304
SMALL_AT = 3072
SMALL = 32
PACKED = SMALL_AT + SMALL
ALL_PACKED = LAYERS * PACKED


def place_table():
    table = np.zeros((IMG, TOK_IMG), np.float32)
    for crop in range(2):
        for row in range(14):
            for col in range(14):
                place = crop * CHUNK + row * 16 + (col // 7) * TILE + col % 7
                table[place, crop * 196 + row * 14 + col] = 1
    for group in range(2):
        for cell in range(108):
            table[2 * CHUNK + group * BLOCK + cell, SPLIT + group * 108 + cell] = 1
    return table


def window_cells(kind):
    cells = [None] * BLOCK
    if kind == 2:
        for place in range(108):
            cells[place] = (place // 36, place % 36 // 6, place % 6)
    else:
        for place in range(BLOCK):
            tile, col = divmod(place, TILE)
            if col < 7:
                cells[place] = (0, tile // 2, 7 * (tile % 2) + col) if kind == 0 else (0, tile, col)
    return cells


def shift_tables():
    wide = np.zeros((3, BLOCK, TAPS * KEYS), np.float32)
    tall = np.zeros((TAPS * BLOCK, KEYS), np.float32)
    for kind in range(3):
        cells = window_cells(kind)
        spots = {cell: place for place, cell in enumerate(cells) if cell is not None}
        for place, cell in enumerate(cells):
            for tap in range(TAPS):
                other = cell and spots.get((cell[0], cell[1] + tap // 3 - 1, cell[2] + tap % 3 - 1))
                if other is not None:
                    wide[kind, place, tap * KEYS + other] = 1
                    if kind == 2:
                        tall[tap * BLOCK + place, other] = 1
    return wide, tall


def bias_table():
    bias = np.full((2, BLOCK, KEYS), -1e30, np.float32)
    bias[0, [key for key in range(BLOCK) if key % TILE < 7]] = 0
    for query in range(KEYS):
        first, last = (36 * (query // 36), 36 * (query // 36) + 36) if query < 108 else (0, 108)
        bias[1, first:last, query] = 0
    return bias


def head_table():
    table = np.zeros((SPAN, HW), np.float32)
    for head in range(GH):
        table[head * KEYS : (head + 1) * KEYS, head * HD : (head + 1) * HD] = 1
    return table


def dot(left, right):
    return lax.dot_general(left, right, (((1,), (0,)), ((), ())), preferred_element_type=F32)


def dot_nt(left, right):
    return lax.dot_general(left, right, (((1,), (1,)), ((), ())), preferred_element_type=F32)


def dot_tn(left, right):
    return lax.dot_general(left, right, (((0,), (0,)), ((), ())), preferred_element_type=F32)


def norm_parts(value):
    center = value - jnp.mean(value, axis=-1, keepdims=True)
    scale = lax.rsqrt(jnp.mean(center * center, axis=-1, keepdims=True) + EPSILON)
    return center * scale, scale


def norm_back(dout, value, gain):
    xhat, scale = norm_parts(value)
    grown = dout * gain
    mean = jnp.mean(grown, axis=-1, keepdims=True)
    cross = jnp.mean(grown * xhat, axis=-1, keepdims=True)
    return scale * (grown - mean - xhat * cross), dout * xhat


def fold_rows(value):
    return jnp.sum(value.reshape(value.shape[0] // 8, 8, value.shape[1]), axis=0)


def head_rows(value, heads_ref):
    return jnp.concatenate(
        [value * heads_ref[head * KEYS : head * KEYS + 1, :] for head in range(GH)], axis=0
    )


def head_stack(value, heads_ref):
    rows = []
    pad = jnp.zeros((KEYS - BLOCK, HW), BF)
    for head in range(GH):
        rows.append(value * heads_ref[head * KEYS : head * KEYS + 1, :])
        rows.append(pad)
    return jnp.concatenate(rows, axis=0)


def pad_keys(value):
    return jnp.concatenate([value, jnp.zeros((KEYS - BLOCK, value.shape[1]), value.dtype)], axis=0)


def pipeline(stages, items, fillers=()):
    results = [None] * len(items)
    fillers = list(fillers)
    for step in range(len(items) + len(stages) - 1):
        if fillers:
            fillers.pop(0)()
        for place in range(len(stages)):
            item = step - place
            if 0 <= item < len(items):
                results[item] = stages[place](items[item], results[item])
    return results


def split_tiles(value):
    rows = value.shape[0] // 16
    return jnp.concatenate(
        [value[16 * row : 16 * row + 8] for row in range(rows)]
        + [value[16 * row + 8 : 16 * row + 16] for row in range(rows)],
        axis=0,
    )


def join_tiles(value):
    half = value.shape[0] // 2
    pieces = []
    for row in range(half // 8):
        pieces.append(value[8 * row : 8 * row + 8])
        pieces.append(value[half + 8 * row : half + 8 * row + 8])
    return jnp.concatenate(pieces, axis=0)


def as_tiles(value):
    return value.reshape(TILES, TILE, HW)


def live_tiles():
    return lax.broadcasted_iota(jnp.int32, (1, TILE, HW), 1) < TILE - 1


def side_cells(tiles, direction):
    if direction == 1:
        return pltpu.roll(tiles, 1, 1), tiles, pltpu.roll(tiles, TILE - 1, 1)
    last = lax.broadcasted_iota(jnp.int32, (1, TILE, HW), 1) == TILE - 1
    left, right = [], []
    for row in range(TILES // 2):
        near, far = tiles[2 * row : 2 * row + 1], tiles[2 * row + 1 : 2 * row + 2]
        near_left = pltpu.roll(near, 1, 1)
        far_right = pltpu.roll(far, TILE - 1, 1)
        left += [near_left, pltpu.roll(jnp.where(last, near_left, far), 1, 1)]
        right += [pltpu.roll(jnp.where(last, far_right, near), TILE - 1, 1), far_right]
    return jnp.concatenate(left, axis=0), tiles, jnp.concatenate(right, axis=0)


def tap_cells(tiles, direction):
    stride = 2 if direction == 0 else 1
    zeros = jnp.zeros((stride, TILE, HW), F32)
    padded = [jnp.concatenate([zeros, side, zeros], axis=0) for side in side_cells(tiles, direction)]
    return [padded[tap % 3][(tap // 3) * stride : (tap // 3) * stride + TILES] for tap in range(TAPS)]


def tap_row(direction, tap):
    return tap if direction == 0 else 3 * (tap % 3) + tap // 3


def compact(ref, image, value):
    first = image * TOK_IMG
    for tile in range(2 * 2 * TILES):
        ref[first + 7 * tile : first + 7 * tile + 7, :] = value[TILE * tile : TILE * tile + 7]
    for group in range(2):
        at = first + SPLIT + 108 * group
        row = 2 * CHUNK + BLOCK * group
        ref[at : at + 108, :] = value[row : row + 108]


def step_kernel(
    pieces,
    counts_ref,
    tok_ref,
    cot_from,
    g1_ref,
    b1_ref,
    own_wqkv_from,
    other_wqkv_from,
    own_lepe_ref,
    other_lepe_ref,
    own_lepeb_ref,
    other_lepeb_ref,
    wproj_from,
    bproj_ref,
    g2_ref,
    b2_ref,
    wfc1_from,
    bfc1_ref,
    wfc2_from,
    bfc2_ref,
    place_ref,
    wide_from,
    tall_from,
    bias_ref,
    heads_ref,
    out_to,
    dtok_to,
    *rest,
):
    keep_refs, send_refs, rest = rest[:pieces], rest[pieces : 2 * pieces], rest[2 * pieces :]
    (
    out_ref,
    dtok_ref,
    written,
    cot_ref,
    wproj_ref,
    wfc1_ref,
    half_wfc2_ref,
    wide_ref,
    tall_ref,
    fetched,
    handed,
    wqkv_ref,
    lepe_ref,
    h_ref,
    normed_ref,
    qkv_ref,
    probs_ref,
    hf_ref,
    hb_ref,
    inner_ref,
    normed2_ref,
    act_ref,
    slope_ref,
    dz_ref,
    dy_ref,
    dhid_ref,
    dqkv_ref,
    acc_ref,
    bfc1_sum_ref,
    accproj_ref,
    accqkv_ref,
    acclepe_ref,
    small_ref,
    stage_ref,
    ) = rest
    rows_all = h_ref.shape[1]
    images = rows_all // IMG
    chunks = rows_all // CHUNK
    blocks = rows_all // BLOCK
    parts = pieces * keep_refs[0].shape[0]
    part_rows = keep_refs[0].shape[1]
    core = lax.axis_index("heads")
    mine = lax.axis_index("dp")
    moves = (
        (own_wqkv_from.at[:, 0], wqkv_ref.at[core]),
        (other_wqkv_from.at[:, 0], wqkv_ref.at[1 - core]),
        (wproj_from, wproj_ref),
        (wfc1_from, wfc1_ref),
        (wfc2_from, half_wfc2_ref),
        (wide_from, wide_ref),
        (cot_from, cot_ref),
        (tall_from, tall_ref),
    )
    fetches = [pltpu.make_async_copy(*move, fetched.at[place]) for place, move in enumerate(moves)]
    for fetch in fetches:
        fetch.start()
    for direction, (lepe, lepeb) in (
        (core, (own_lepe_ref, own_lepeb_ref)),
        (1 - core, (other_lepe_ref, other_lepeb_ref)),
    ):
        lepe_ref[direction, :, :TAPS] = lepe[:, :, 0]
        lepe_ref[direction, :, TAPS : TAPS + 1] = lepeb[...]

    def chunk_rows(index):
        return pl.ds(index * CHUNK, CHUNK)

    def chunk_tiles(index):
        return pl.ds(index * TILES, TILES)

    def wide_rows(index):
        return pl.ds(index * 2 * CHUNK, 2 * CHUNK)

    def wide_tiles(index):
        return pl.ds(index * 2 * TILES, 2 * TILES)

    def block_rows(index):
        return pl.ds(index * BLOCK, BLOCK)

    def is_small(block):
        return block % 6 >= 4

    def keep_of(image):
        place = lax.broadcasted_iota(jnp.int32, (IMG, 1), 0)
        limit = counts_ref[core * images + image]
        group = (place - 448) // BLOCK
        inside = (place - 448) % BLOCK
        return (place < 448) | (inside < 36 * (limit - 3 * group))

    for image in range(images):
        spot = pl.ds(image * TOK_IMG, TOK_IMG)
        h_ref[0, pl.ds(image * IMG, IMG), :] = dot(place_ref[...], tok_ref[spot, :])

    def project_stages(layer):
        gain1, bias1 = g1_ref[pl.ds(layer, 1), :], b1_ref[pl.ds(layer, 1), :]

        def normalize(index, value):
            rows = chunk_rows(index)
            xhat, _ = norm_parts(h_ref[layer, rows, :] if value is None else value)
            normed = xhat * gain1 + bias1
            turned = split_tiles(normed) if index % 3 < 2 else normed
            return normed.astype(BF), turned.astype(BF)

        def project(index, values):
            rows = chunk_rows(index)
            for direction, value in enumerate(values):
                normed_ref[layer, direction, rows, :] = value
                qkv_ref[layer, direction, rows, :] = dot(value, wqkv_ref[direction, layer]).astype(BF)

        return normalize, project

    def forward(layer):
        if layer == 0:
            for fetch in fetches[:2]:
                fetch.wait()
            pipeline(project_stages(layer), range(chunks))
            fetches[5].wait()

        def tap_weight(direction, tap):
            return lepe_ref[direction, layer, pl.ds(tap_row(direction, tap), 1), :]

        def score(window, _):
            direction, block = window
            rows = block_rows(block)
            query = qkv_ref[layer, direction, rows, :HW]
            keyset = qkv_ref[layer, direction, rows, HW : 2 * HW]
            return dot_nt(head_rows(keyset, heads_ref), pad_keys(query))

        def weigh(window, scores):
            direction, block = window
            rows = block_rows(block)
            bias = bias_ref[int(is_small(block))]
            probs = []
            for head in range(GH):
                part = scores[head * BLOCK : (head + 1) * BLOCK] + bias
                part = jnp.exp2((part - jnp.max(part, axis=0, keepdims=True)) * EXP_SCALE)
                part = part * (1.0 / jnp.sum(part, axis=0, keepdims=True))
                probs.append(part.astype(BF))
                probs_ref[layer, direction, rows, head * KEYS : (head + 1) * KEYS] = probs[head]
            return probs

        def mix(window, probs):
            direction, block = window
            rows = block_rows(block)
            values = qkv_ref[layer, direction, rows, 2 * HW :]
            side = values.T
            mixed = [dot(side[head * HD : (head + 1) * HD], probs[head]) for head in range(GH)]
            return jnp.concatenate(mixed, axis=0)

        def finish(window, mixed):
            direction, block = window
            lanes = slice(direction * HW, (direction + 1) * HW)
            result = mixed.T[:BLOCK] + lepe_ref[direction, layer, TAPS : TAPS + 1, :] + local[window]
            if direction == 0 or is_small(block):
                hf_ref[block * 7 : block * 7 + 7, :, :, lanes] = result.reshape(7, 2, TILE, HW)
            else:
                side = block % 2
                rows = slice((block - side) * 7, (block - side) * 7 + TILES)
                hf_ref[rows, side, :, lanes] = as_tiles(result)

        local = {}

        def filter_pair(kind, windows):
            scaled = []
            for direction, block in windows:
                values = qkv_ref[layer, direction, block_rows(block), 2 * HW :]
                scaled.append(
                    jnp.concatenate(
                        [pad_keys(values * tap_weight(direction, tap).astype(BF)) for tap in range(TAPS)], axis=0
                    )
                )
            both = dot(wide_ref[kind], jnp.concatenate(scaled, axis=1))
            for place, window in enumerate(windows):
                local[window] = both[:, place * HW : (place + 1) * HW]

        windows, fillers = [], []
        for block in range(blocks):
            windows += [(direction, block) for direction in range(2)]
            if is_small(block):
                fillers.append(functools.partial(filter_pair, 2, windows[-2:]))
            elif block % 2 == 1:
                for direction in range(2):
                    pair = [(direction, block - 1), (direction, block)]
                    fillers.append(functools.partial(filter_pair, direction, pair))
        pipeline((score, weigh, mix, finish), windows, fillers)

        if layer == 0:
            for fetch in fetches[2:5]:
                fetch.wait()
            half_wfc2_ref[...] = half_wfc2_ref[...] * jnp.asarray(0.5, BF)
        gain2, bias2 = g2_ref[pl.ds(layer, 1), :], b2_ref[pl.ds(layer, 1), :]

        def join(index, _):
            rows = chunk_rows(index)
            heads = hf_ref[chunk_tiles(index)].reshape(CHUNK, D).astype(BF)
            hb_ref[layer, rows, :] = heads
            inner = h_ref[layer, rows, :] + dot(heads, wproj_ref[layer]) + bproj_ref[pl.ds(layer, 1), :]
            inner_ref[layer, rows, :] = inner
            return inner

        def widen(index, inner):
            xhat, _ = norm_parts(inner)
            normed2 = (xhat * gain2 + bias2).astype(BF)
            normed2_ref[layer, chunk_rows(index), :] = normed2
            return dot(normed2, wfc1_ref[layer])

        def narrow(index, hidden):
            rows = chunk_rows(index)
            hidden = hidden + bfc1_ref[pl.ds(layer, 1), :]
            cdf = 1.0 + lax.erf(hidden * math.sqrt(0.5))
            act = (hidden * cdf).astype(BF)
            act_ref[layer, rows, :] = act
            bell = jnp.exp2(hidden * hidden * (-0.5 * math.log2(math.e)))
            slope_ref[layer, rows, :] = (cdf + hidden * bell * math.sqrt(2 / math.pi)).astype(BF)
            return dot(act, half_wfc2_ref[layer])

        def close(index, branch):
            rows = chunk_rows(index)
            value = inner_ref[layer, rows, :] + branch + bfc2_ref[pl.ds(layer, 1), :]
            h_ref[layer + 1, rows, :] = value
            return value

        stages = (join, widen, narrow, close)
        if layer + 1 < LAYERS:
            stages += project_stages(layer + 1)
        pipeline(stages, range(chunks))

    for layer in range(LAYERS):
        forward(layer)
    for fetch in fetches[6:]:
        fetch.wait()

    for image in range(images):
        spot = pl.ds(image * TOK_IMG, TOK_IMG)
        wide = pl.ds(image * IMG, IMG)
        keep = keep_of(image)
        compact(dtok_ref, image, jnp.where(keep, h_ref[LAYERS, wide, :], 0.0))
        h_ref[LAYERS, wide, :] = jnp.where(keep, dot(place_ref[...], cot_ref[spot, :]), 0.0)
    out_ref[...] = dtok_ref[...].astype(BF)
    out_copy = pltpu.make_async_copy(out_ref, out_to, written.at[0])
    out_copy.start()

    def backward(step, carry):
        layer = LAYERS - 1 - step
        base = layer * PACKED
        acc_ref[...] = jnp.zeros_like(acc_ref)
        acclepe_ref[...] = jnp.zeros_like(acclepe_ref)

        accproj_ref[...] = jnp.zeros_like(accproj_ref)
        bfc1_sum_ref[...] = jnp.zeros_like(bfc1_sum_ref)
        gain2 = g2_ref[pl.ds(layer, 1), :]

        def pair_rows(index):
            return pl.ds((index - 1) * CHUNK, 2 * CHUNK)

        def widen(index, _):
            rows = wide_rows(index)
            dz = h_ref[LAYERS, rows, :].astype(BF)
            dz_ref[rows, :] = dz
            acc_ref[5] += fold_rows(dz.astype(F32))
            return dot_nt(dz, half_wfc2_ref[layer])

        def narrow(index, dact):
            rows = wide_rows(index)
            dhid = dact * slope_ref[layer, rows, :].astype(F32)
            bfc1_sum_ref[...] += fold_rows(dhid)
            dhid = dhid.astype(BF)
            dhid_ref[rows, :] = dhid
            return dot_nt(dhid, wfc1_ref[layer])

        def close(index, dnormed):
            rows = wide_rows(index)
            dvalue, dgain = norm_back(dnormed, inner_ref[layer, rows, :], gain2)
            acc_ref[3] += fold_rows(dgain)
            acc_ref[4] += fold_rows(dnormed)
            dinner = h_ref[LAYERS, rows, :] + dvalue
            h_ref[LAYERS, rows, :] = dinner
            dy = dinner.astype(BF)
            dy_ref[rows, :] = dy
            acc_ref[2] += fold_rows(dy.astype(F32))
            return dot_nt(dy, wproj_ref[layer])

        def project(index, dheads):
            hf_ref[wide_tiles(index)] = dheads.reshape(2 * TILES, 2, TILE, D)
            rows = wide_rows(index)
            accproj_ref[...] += dot_tn(hb_ref[layer, rows, :], dy_ref[rows, :])

        pipeline((widen, narrow, close, project), range(chunks // 2))
        for half in range(2):
            stage_ref[half, pl.ds(base + PROJ_AT, D), :] = accproj_ref[:, half * HW : (half + 1) * HW].astype(BF)

        def tap_weight(direction, tap):
            return lepe_ref[direction, layer, pl.ds(tap_row(direction, tap), 1), :]

        def grad_of(direction, block):
            lanes = slice(direction * HW, (direction + 1) * HW)
            if direction == 0 or is_small(block):
                tiles = hf_ref[block * 7 : block * 7 + 7, :, :, lanes]
            else:
                side = block % 2
                tiles = hf_ref[(block - side) * 7 : (block - side) * 7 + TILES, side, :, lanes]
            return tiles.reshape(BLOCK, HW).astype(BF)

        def score(window, _):
            direction, block = window
            rows = block_rows(block)
            grad = grad_of(direction, block)
            values = qkv_ref[layer, direction, rows, 2 * HW :]
            return dot_nt(head_rows(values, heads_ref), pad_keys(grad))

        def weigh(window, dprobs):
            direction, block = window
            rows = block_rows(block)
            dscores = []
            for head in range(GH):
                part = probs_ref[layer, direction, rows, head * KEYS : (head + 1) * KEYS].astype(F32)
                dpart = dprobs[head * BLOCK : (head + 1) * BLOCK]
                inner = jnp.sum(part * dpart, axis=0, keepdims=True)
                dscores.append((part * (dpart - inner)).astype(BF))
            return dscores

        def mix(window, dscores):
            direction, block = window
            rows = block_rows(block)
            grad = grad_of(direction, block)
            query = qkv_ref[layer, direction, rows, :HW]
            side = qkv_ref[layer, direction, rows, HW : 2 * HW].T
            dkeys = dot(jnp.concatenate(dscores, axis=1), head_stack(query, heads_ref))
            dvalues = dot(probs_ref[layer, direction, rows, :], head_stack(grad, heads_ref))
            dquery = [dot(side[head * HD : (head + 1) * HD], dscores[head]) for head in range(GH)]
            return jnp.concatenate(dquery, axis=0), dkeys, dvalues

        def finish(window, results):
            direction, block = window
            rows = block_rows(block)
            grad = grad_of(direction, block)
            lanes = slice(direction * HW, (direction + 1) * HW)
            dquery, dkeys, dvalues = results
            values = qkv_ref[layer, direction, rows, 2 * HW :]
            first = direction * 3 * HW
            dqkv_ref[rows, first : first + HW] = (dquery * SCALE).T[:BLOCK].astype(BF)
            dqkv_ref[rows, first + HW : first + 2 * HW] = (dkeys * SCALE).astype(BF)
            if is_small(block):
                dvalues = dvalues + local[block][:, lanes]
                dqkv_ref[rows, first + 2 * HW : first + 3 * HW] = dvalues.astype(BF)
                return None
            grad_tiles = as_tiles(grad.astype(F32))
            result = as_tiles(dvalues)
            for tap, cells in enumerate(tap_cells(grad_tiles, direction)):
                result = result + cells * tap_weight(direction, TAPS - 1 - tap).reshape(1, 1, HW)
            result = jnp.where(live_tiles(), result, 0.0).reshape(BLOCK, HW)
            dqkv_ref[rows, first + 2 * HW : first + 3 * HW] = result.astype(BF)
            tiles = jnp.where(live_tiles(), as_tiles(values.astype(F32)), 0.0)
            for tap, cells in enumerate(tap_cells(tiles, direction)):
                acclepe_ref[direction, tap_row(direction, tap)] += jnp.sum(grad_tiles * cells, axis=0)
            acclepe_ref[direction, TAPS] += jnp.sum(grad_tiles, axis=0)
            return None

        half_rows = rows_all // 2
        spans = [pl.ds(part * half_rows, half_rows) for part in range(2)]
        sides = {}

        def feed_weights(index):
            width = FF // (2 * images)
            cols = pl.ds(index * width, width)
            partial = []

            def first(part):
                rows = spans[part]
                if (0, part) not in sides:
                    sides[0, part] = normed2_ref[layer, rows, :].T
                partial.append(dot(sides[0, part], dhid_ref[rows, cols]))

            def second(part):
                rows = spans[part]
                if (1, part) not in sides:
                    sides[1, part] = dz_ref[rows, :].T
                partial.append(dot(sides[1, part], act_ref[layer, rows, cols]))

            def store(at):
                total = partial[0] + partial[1]
                if at == FC2_AT:
                    total = total * 0.5
                for piece in range(width // HW):
                    column = index * (width // HW) + piece
                    place = base + at + column % 4 * 256
                    value = total[:, piece * HW : (piece + 1) * HW].astype(BF)
                    stage_ref[column // 4, pl.ds(place, 256), :] = value
                partial.clear()

            return [
                lambda: first(0),
                lambda: (first(1), store(FC1_AT)),
                lambda: second(0),
                lambda: (second(1), store(FC2_AT)),
            ]

        local = {}

        def filter_small(block):
            scaled = []
            for direction in range(2):
                padded = pad_keys(grad_of(direction, block).astype(F32))
                scaled.append(
                    jnp.concatenate(
                        [(padded * tap_weight(direction, TAPS - 1 - tap)).astype(BF) for tap in range(TAPS)], axis=0
                    )
                )
            local[block] = dot(wide_ref[2], jnp.concatenate(scaled, axis=1))

        def shift_small(block):
            values = [pad_keys(qkv_ref[layer, direction, block_rows(block), 2 * HW :]) for direction in range(2)]
            shifted = dot(tall_ref[...], jnp.concatenate(values, axis=1))
            for direction in range(2):
                lanes = slice(direction * HW, (direction + 1) * HW)
                grad = grad_of(direction, block).astype(F32)
                for tap in range(TAPS):
                    acclepe_ref[direction, tap_row(direction, tap)] += fold_rows(
                        grad * shifted[tap * BLOCK : (tap + 1) * BLOCK, lanes]
                    )
                acclepe_ref[direction, TAPS] += fold_rows(grad)

        order = [block for block in range(blocks) if not is_small(block)]
        order += [block for block in range(blocks) if is_small(block)]
        windows = [(direction, block) for block in order for direction in range(2)]
        fillers = [filler for index in range(2 * images) for filler in feed_weights(index)]
        for block in order:
            if is_small(block):
                fillers += [functools.partial(filter_small, block), functools.partial(shift_small, block)]
        pipeline((score, weigh, mix, finish), windows, fillers)

        accqkv_ref[...] = jnp.zeros_like(accqkv_ref)
        gain1 = g1_ref[pl.ds(layer, 1), :]

        def collect(index, _):
            rows = chunk_rows(index)
            return [
                dot_nt(dqkv_ref[rows, direction * 3 * HW : (direction + 1) * 3 * HW], wqkv_ref[direction, layer])
                for direction in range(2)
            ]

        def weigh_inputs(index, dnormed):
            if index % 2 == 1:
                rows = pair_rows(index)
                for direction in range(2):
                    accqkv_ref[direction] += dot(
                        normed_ref[layer, direction, rows, :].T,
                        dqkv_ref[rows, direction * 3 * HW : (direction + 1) * 3 * HW],
                    )
            return dnormed

        def spread(index, dnormed):
            rows = chunk_rows(index)
            straight, turned = dnormed
            dnormed = straight + (join_tiles(turned) if index % 3 < 2 else turned)
            dvalue, dgain = norm_back(dnormed, h_ref[layer, rows, :], gain1)
            acc_ref[0] += fold_rows(dgain)
            acc_ref[1] += fold_rows(dnormed)
            h_ref[LAYERS, rows, :] = h_ref[LAYERS, rows, :] + dvalue

        pipeline((collect, weigh_inputs, spread), range(chunks))
        small_ref[...] = jnp.zeros_like(small_ref)
        for direction in range(2):
            for piece in range(3):
                at = QKV_AT + 256 * piece
                stage_ref[direction, pl.ds(base + at, 256), :] = accqkv_ref[
                    direction, :, piece * HW : (piece + 1) * HW
                ].astype(BF)
            small_ref[direction, :10, :] = jnp.sum(acclepe_ref[direction], axis=1)
        sums = jnp.sum(acc_ref[...], axis=1)
        for piece in range(2):
            small_ref[0, 10 + 6 * piece : 16 + 6 * piece, :] = sums[:, piece * HW : (piece + 1) * HW]
        sums = jnp.sum(bfc1_sum_ref[...], axis=0, keepdims=True)
        for piece in range(8):
            small_ref[1, 10 + piece : 11 + piece, :] = sums[:, piece * HW : (piece + 1) * HW]
        stage_ref[:, pl.ds(base + SMALL_AT, SMALL), :] = small_ref[...].astype(BF)

        return carry

    stage_ref[:, ALL_PACKED:, :] = jnp.zeros((2, stage_ref.shape[1] - ALL_PACKED, HW), BF)
    for step in range(LAYERS):
        backward(step, 0)

    copies = []
    for slot, targets in enumerate((keep_refs, send_refs)):
        half = jnp.bitwise_xor(core, slot)
        for place in range(parts):
            part = jnp.bitwise_xor(part_at(place, parts, half), mine)
            source = stage_ref.at[half, pl.ds(pl.multiple_of(part * part_rows, 16), part_rows), :]
            target = targets[place * pieces // parts].at[place % (parts // pieces)]
            copies.append(pltpu.make_async_copy(source, target, handed.at[slot, place]))
    for copy in copies:
        copy.start()
    for image in range(images):
        compact(dtok_ref, image, h_ref[LAYERS, pl.ds(image * IMG, IMG), :])
    dtok_copy = pltpu.make_async_copy(dtok_ref, dtok_to, written.at[1])
    dtok_copy.start()
    out_copy.wait()
    for copy in copies:
        copy.wait()
    dtok_copy.wait()


def digits_of(parts, core):
    digits, stride = [], 1
    while stride < parts:
        size = 4 if parts // stride % 4 == 0 else 2
        digits.append((size, stride))
        stride *= size
    if len({size for size, _ in digits}) == 1 and core == 1:
        digits = digits[1:] + digits[:1]
    return digits


def part_at(place, parts, core):
    found = []
    for which in range(2):
        index, left = 0, place
        for size, stride in reversed(digits_of(parts, which)):
            index += left % size * stride
            left //= size
        found.append(index)
    return jnp.where(core == 0, found[0], found[1])


def unpack_kernel(
    pieces,
    *refs,
):
    own_refs, other_refs, refs = refs[:pieces], refs[pieces : 2 * pieces], refs[2 * pieces :]
    (
    g1_ref,
    b1_ref,
    gqkv_ref,
    glepe_ref,
    glepeb_ref,
    gproj_ref,
    gbproj_ref,
    g2_ref,
    b2_ref,
    gfc1_ref,
    gbfc1_ref,
    gfc2_ref,
    gbfc2_ref,
    stage_ref,
    ) = refs
    parts = pieces * own_refs[0].shape[0]
    part_rows = own_refs[0].shape[1]
    core = lax.axis_index("heads")
    mine = lax.axis_index("dp")
    for slot, sources in enumerate((own_refs, other_refs)):
        half = jnp.bitwise_xor(core, slot)
        for place in range(parts):
            part = jnp.bitwise_xor(part_at(place, parts, 0), mine)
            at = pl.ds(pl.multiple_of(part * part_rows, 16), part_rows)
            stage_ref[half, at, :] = sources[place * pieces // parts][place % (parts // pieces)]

    for layer in range(LAYERS):
        base = layer * PACKED
        for half in range(2):
            for piece in range(4):
                lanes = slice(half * 512 + piece * HW, half * 512 + (piece + 1) * HW)
                at = base + FC1_AT + 256 * piece
                gfc1_ref[layer, :, lanes] = stage_ref[half, at : at + 256, :].astype(F32)
                at = base + FC2_AT + 256 * piece
                gfc2_ref[layer, lanes, :] = stage_ref[half, at : at + 256, :].astype(F32).T
            gproj_ref[layer, :, half * HW : (half + 1) * HW] = stage_ref[
                half, base + PROJ_AT : base + PROJ_AT + 256, :
            ].astype(F32)
        for piece in range(3):
            at = base + QKV_AT + 256 * piece
            gqkv_ref[layer, 0, :, piece * HW : (piece + 1) * HW] = stage_ref[core, at : at + 256, :].astype(F32)
        small = stage_ref[core, base + SMALL_AT : base + PACKED, :].astype(F32)
        glepe_ref[layer, :, 0] = small[:TAPS]
        glepeb_ref[layer] = small[TAPS : TAPS + 1]
        small = stage_ref[0, base + SMALL_AT : base + PACKED, :].astype(F32)
        for place, ref in enumerate((g1_ref, b1_ref, gbproj_ref, g2_ref, b2_ref, gbfc2_ref)):
            for piece in range(2):
                row = 10 + 6 * piece + place
                ref[layer : layer + 1, piece * HW : (piece + 1) * HW] = small[row : row + 1]
        small = stage_ref[1, base + SMALL_AT : base + PACKED, :].astype(F32)
        for piece in range(8):
            gbfc1_ref[layer : layer + 1, piece * HW : (piece + 1) * HW] = small[10 + piece : 11 + piece]


SMEM = pl.BlockSpec(memory_space=pltpu.SMEM)
VMEM = pl.BlockSpec(memory_space=pltpu.VMEM)
ANY = pl.BlockSpec(memory_space=pl.ANY)


def shards(
    dp,
    tokens,
    cotangent,
    counts,
    ln1_gain,
    ln1_bias,
    w_qkv,
    lepe_w,
    lepe_b,
    w_proj,
    b_proj,
    ln2_gain,
    ln2_bias,
    w_fc1,
    b_fc1,
    w_fc2,
    b_fc2,
):
    tokens_here = tokens.shape[0]
    images = tokens_here // TOK_IMG
    rows = images * IMG
    swap = [(0, 1), (1, 0)]

    def across(value):
        return lax.ppermute(value, "heads", swap)

    part_rows = -(-ALL_PACKED // (16 * dp)) * 16
    wide, tall = shift_tables()
    table = place_table()
    scratch = [
        pltpu.VMEM((tokens_here, D), BF),
        pltpu.VMEM((tokens_here, D), F32),
        pltpu.SemaphoreType.DMA((2,)),
        pltpu.VMEM((tokens_here, D), BF),
        pltpu.VMEM((LAYERS, D, D), BF),
        pltpu.VMEM((LAYERS, D, FF), BF),
        pltpu.VMEM((LAYERS, FF, D), BF),
        pltpu.VMEM((3, BLOCK, TAPS * KEYS), BF),
        pltpu.VMEM((TAPS * BLOCK, KEYS), BF),
        pltpu.SemaphoreType.DMA((8,)),
        pltpu.SemaphoreType.DMA((2, dp)),
        pltpu.VMEM((2, LAYERS, D, 3 * HW), BF),
        pltpu.VMEM((2, LAYERS, 16, HW), F32),
        pltpu.VMEM((LAYERS + 1, rows, D), F32),
        pltpu.VMEM((LAYERS, 2, rows, D), BF),
        pltpu.VMEM((LAYERS, 2, rows, 3 * HW), BF),
        pltpu.VMEM((LAYERS, 2, rows, SPAN), BF),
        pltpu.VMEM((rows // 16, 2, TILE, D), F32),
        pltpu.VMEM((LAYERS, rows, D), BF),
        pltpu.VMEM((LAYERS, rows, D), F32),
        pltpu.VMEM((LAYERS, rows, D), BF),
        pltpu.VMEM((LAYERS, rows, FF), BF),
        pltpu.VMEM((LAYERS, rows, FF), BF),
        pltpu.VMEM((rows, D), BF),
        pltpu.VMEM((rows, D), BF),
        pltpu.VMEM((rows, FF), BF),
        pltpu.VMEM((rows, 6 * HW), BF),
        pltpu.VMEM((6, 8, D), F32),
        pltpu.VMEM((8, FF), F32),
        pltpu.VMEM((D, D), F32),
        pltpu.VMEM((2, D, 3 * HW), F32),
        pltpu.VMEM((2, TAPS + 1, 8, HW), F32),
        pltpu.VMEM((2, SMALL, HW), F32),
        pltpu.VMEM((2, part_rows * dp, HW), BF),
    ]
    pieces = digits_of(dp, 0)[0][0]
    piece = jax.ShapeDtypeStruct((dp // pieces, part_rows, HW), BF)
    result, grad, *packed = pl.pallas_call(
        functools.partial(step_kernel, pieces),
        out_shape=(
            jax.ShapeDtypeStruct((tokens_here, D), BF),
            jax.ShapeDtypeStruct((tokens_here, D), F32),
        )
        + (piece,) * (2 * pieces),
        in_specs=[SMEM, VMEM, ANY, VMEM, VMEM, ANY, ANY] + [VMEM] * 4 + [ANY] + [VMEM] * 3 + [ANY, VMEM, ANY, VMEM, VMEM, ANY, ANY, VMEM, VMEM],
        out_specs=(ANY,) * (2 + 2 * pieces),
        scratch_shapes=scratch,
        compiler_params=pltpu.CompilerParams(vmem_limit_bytes=60 * 1024 * 1024),
        name="step",
    )(
        counts,
        tokens,
        cotangent,
        ln1_gain,
        ln1_bias,
        w_qkv,
        across(w_qkv),
        lepe_w.swapaxes(1, 2),
        across(lepe_w.swapaxes(1, 2)),
        lepe_b,
        across(lepe_b),
        w_proj,
        b_proj,
        ln2_gain,
        ln2_bias,
        w_fc1,
        b_fc1,
        w_fc2,
        b_fc2,
        jnp.asarray(table, BF),
        jnp.asarray(wide, BF),
        jnp.asarray(tall, BF),
        jnp.asarray(bias_table()),
        jnp.asarray(head_table(), BF),
    )

    def add(first, *rest):
        total = first.astype(F32)
        for item in rest:
            total = total + item.astype(F32)
        return total.astype(BF)

    keep, send = packed[:pieces], packed[pieces:]
    orders = [digits_of(dp, core) for core in range(2)]

    def hop_pairs(orders, step, hop):
        pairs = []
        for chip in range(dp):
            for core in range(2):
                pairs.append((2 * chip + core, 2 * (chip ^ (hop * orders[core][step][1])) + core))
        return pairs

    def exchange(step, values, orders=orders):
        arrived = [
            lax.ppermute(values[hop], ("dp", "heads"), hop_pairs(orders, step, hop)) for hop in range(len(values) - 1, 0, -1)
        ]
        return arrived[::-1]

    received = [across(send[hop]) for hop in range(pieces - 1, -1, -1)][::-1]
    sums = [None] + [add(keep[hop], received[hop]) for hop in range(1, pieces)]
    arrived = lax.optimization_barrier(tuple(exchange(0, sums)))
    own = add(keep[0], received[0], *arrived)
    for step in range(1, len(orders[0])):
        size = orders[0][step][0]
        cuts = own.reshape((size, own.shape[0] // size) + own.shape[1:])
        own = add(cuts[0], *lax.optimization_barrier(tuple(exchange(step, cuts))))
    for step in range(len(orders[0]) - 1, 0, -1):
        arrived = lax.optimization_barrier(tuple(exchange(step, [own] * orders[0][step][0], orders[:1] * 2)))
        own = jnp.concatenate((own,) + tuple(arrived), axis=0)
    whole = [own] + exchange(0, [own] * pieces, orders[:1] * 2)
    others = [across(value) for value in whole]
    grads = list(pl.pallas_call(
        functools.partial(unpack_kernel, pieces),
        out_shape=(
            jax.ShapeDtypeStruct((LAYERS, D), F32),
            jax.ShapeDtypeStruct((LAYERS, D), F32),
            jax.ShapeDtypeStruct((LAYERS, 1, D, 3 * HW), F32),
            jax.ShapeDtypeStruct((LAYERS, TAPS, 1, HW), F32),
            jax.ShapeDtypeStruct((LAYERS, 1, HW), F32),
            jax.ShapeDtypeStruct((LAYERS, D, D), F32),
            jax.ShapeDtypeStruct((LAYERS, D), F32),
            jax.ShapeDtypeStruct((LAYERS, D), F32),
            jax.ShapeDtypeStruct((LAYERS, D), F32),
            jax.ShapeDtypeStruct((LAYERS, D, FF), F32),
            jax.ShapeDtypeStruct((LAYERS, FF), F32),
            jax.ShapeDtypeStruct((LAYERS, FF, D), F32),
            jax.ShapeDtypeStruct((LAYERS, D), F32),
        ),
        in_specs=[VMEM] * (2 * pieces),
        out_specs=(VMEM,) * 13,
        scratch_shapes=[pltpu.VMEM((2, part_rows * dp, HW), BF)],
        compiler_params=pltpu.CompilerParams(vmem_limit_bytes=48 * 1024 * 1024),
        name="unpack",
    )(*whole, *others))
    grads[3] = grads[3].swapaxes(1, 2)
    return (result, grad) + tuple(grads)


def solution(mesh):
    spread = P(("dp", "heads"), None)
    group = (P(None, "heads", None, None), P(None, "heads", None, None), P(None, "heads", None))
    in_specs = (spread, spread, P("dp"), P(), P()) + group + (P(),) * 8
    out_specs = (spread, spread, P(), P()) + group + (P(),) * 8
    return jax.shard_map(
        functools.partial(shards, mesh.shape["dp"]),
        mesh=mesh,
        in_specs=in_specs,
        out_specs=out_specs,
        check_vma=False,
    )
```

```python
import functools
import math

import jax
import jax.numpy as jnp
import numpy as np
from jax import lax
from jax.experimental import pallas as pl
from jax.experimental.pallas import tpu as pltpu
from jax.sharding import PartitionSpec as P

D = 256
FF = 1024
HD = 32
GH = 4
HW = 128
LAYERS = 2
TOK_IMG = 608
SPLIT = 392
EPSILON = 1e-05

TILE = 8
TILES = 14
BLOCK = TILES * TILE
CHUNK = 2 * BLOCK
IMG = 6 * BLOCK
KEYS = 128
SPAN = GH * KEYS
TAPS = 9
SCALE = HD**-0.5
EXP_SCALE = SCALE * math.log2(math.e)
BF = jnp.bfloat16
F32 = jnp.float32

FC1_AT = 0
FC2_AT = 1024
PROJ_AT = 2048
QKV_AT = 2304
SMALL_AT = 3072
SMALL = 32
PACKED = SMALL_AT + SMALL
ALL_PACKED = LAYERS * PACKED


def shift_block(kind, tap):
    down, along = tap // 3 - 1, tap % 3 - 1
    place = lax.broadcasted_iota(jnp.int32, (BLOCK, 1), 0)
    if kind == 0:
        row = place >> 4
        half = (place >> 3) & 1
        cell = place & 7
        moved = 7 * half + cell + along
        target = 16 * (row + down) + moved + jnp.where(moved >= 7, 1, 0)
        inside = (cell < 7) & (moved >= 0) & (moved < 14) & (row + down >= 0) & (row + down < 7)
    elif kind == 1:
        row = place >> 3
        cell = place & 7
        moved = cell + along
        target = place + 8 * down + along
        inside = (cell < 7) & (moved >= 0) & (moved < 7) & (row + down >= 0) & (row + down < 14)
    else:
        cell = place - jnp.where(place >= 36, 36, 0) - jnp.where(place >= 72, 36, 0)
        row = (cell * 43) >> 8
        moved = cell - 6 * row + along
        target = place + 6 * down + along
        inside = (place < 108) & (moved >= 0) & (moved < 6) & (row + down >= 0) & (row + down < 6)
    column = lax.broadcasted_iota(jnp.int32, (BLOCK, KEYS), 1)
    return jnp.where(column == jnp.where(inside, target, -1), 1.0, 0.0).astype(BF)


def bias_table():
    bias = np.full((2, BLOCK, KEYS), -1e30, np.float32)
    bias[0, [key for key in range(BLOCK) if key % TILE < 7]] = 0
    for query in range(KEYS):
        first, last = (36 * (query // 36), 36 * (query // 36) + 36) if query < 108 else (0, 108)
        bias[1, first:last, query] = 0
    return bias


def head_table():
    table = np.zeros((16, HW), np.float32)
    for head in range(GH):
        table[head, head * HD : (head + 1) * HD] = 1
    return table


def dot(left, right):
    return lax.dot_general(left, right, (((1,), (0,)), ((), ())), preferred_element_type=F32)


def dot_nt(left, right):
    return lax.dot_general(left, right, (((1,), (1,)), ((), ())), preferred_element_type=F32)


def dot_tn(left, right):
    return lax.dot_general(left, right, (((0,), (0,)), ((), ())), preferred_element_type=F32)


def norm_parts(value):
    center = value - jnp.mean(value, axis=-1, keepdims=True)
    scale = lax.rsqrt(jnp.mean(center * center, axis=-1, keepdims=True) + EPSILON)
    return center * scale, scale


def norm_back(dout, value, gain):
    xhat, scale = norm_parts(value)
    grown = dout * gain
    mean = jnp.mean(grown, axis=-1, keepdims=True)
    cross = jnp.mean(grown * xhat, axis=-1, keepdims=True)
    return scale * (grown - mean - xhat * cross), dout * xhat


def fold_rows(value):
    return jnp.sum(value.reshape(value.shape[0] // 8, 8, value.shape[1]), axis=0)


def head_rows(value, heads_ref):
    return jnp.concatenate(
        [value * heads_ref[head : head + 1, :].astype(BF) for head in range(GH)], axis=0
    )


def head_stack(value, heads_ref):
    rows = []
    pad = jnp.zeros((KEYS - BLOCK, HW), BF)
    for head in range(GH):
        rows.append(value * heads_ref[head : head + 1, :].astype(BF))
        rows.append(pad)
    return jnp.concatenate(rows, axis=0)


def pad_keys(value):
    return jnp.concatenate([value, jnp.zeros((KEYS - BLOCK, value.shape[1]), value.dtype)], axis=0)


def pipeline(stages, items, fillers=()):
    results = [None] * len(items)
    fillers = list(fillers)
    for step in range(len(items) + len(stages) - 1):
        if fillers:
            fillers.pop(0)()
        for place in range(len(stages)):
            item = step - place
            if 0 <= item < len(items):
                results[item] = stages[place](items[item], results[item])
    return results


def split_tiles(value):
    rows = value.shape[0] // 16
    return jnp.concatenate(
        [value[16 * row : 16 * row + 8] for row in range(rows)]
        + [value[16 * row + 8 : 16 * row + 16] for row in range(rows)],
        axis=0,
    )


def join_tiles(value):
    half = value.shape[0] // 2
    pieces = []
    for row in range(half // 8):
        pieces.append(value[8 * row : 8 * row + 8])
        pieces.append(value[half + 8 * row : half + 8 * row + 8])
    return jnp.concatenate(pieces, axis=0)


def as_tiles(value):
    return value.reshape(TILES, TILE, HW)


def live_tiles():
    return lax.broadcasted_iota(jnp.int32, (1, TILE, HW), 1) < TILE - 1


def side_cells(tiles, direction):
    if direction == 1:
        return pltpu.roll(tiles, 1, 1), tiles, pltpu.roll(tiles, TILE - 1, 1)
    last = lax.broadcasted_iota(jnp.int32, (1, TILE, HW), 1) == TILE - 1
    left, right = [], []
    for row in range(TILES // 2):
        near, far = tiles[2 * row : 2 * row + 1], tiles[2 * row + 1 : 2 * row + 2]
        near_left = pltpu.roll(near, 1, 1)
        far_right = pltpu.roll(far, TILE - 1, 1)
        left += [near_left, pltpu.roll(jnp.where(last, near_left, far), 1, 1)]
        right += [pltpu.roll(jnp.where(last, far_right, near), TILE - 1, 1), far_right]
    return jnp.concatenate(left, axis=0), tiles, jnp.concatenate(right, axis=0)


def tap_cells(tiles, direction):
    stride = 2 if direction == 0 else 1
    zeros = jnp.zeros((stride, TILE, HW), F32)
    padded = [jnp.concatenate([zeros, side, zeros], axis=0) for side in side_cells(tiles, direction)]
    return [padded[tap % 3][(tap // 3) * stride : (tap // 3) * stride + TILES] for tap in range(TAPS)]


def tap_row(direction, tap):
    return tap if direction == 0 else 3 * (tap % 3) + tap // 3


def compact(ref, image, value):
    first = image * TOK_IMG
    for tile in range(2 * 2 * TILES):
        ref[first + 7 * tile : first + 7 * tile + 7, :] = value[TILE * tile : TILE * tile + 7]
    for group in range(2):
        at = first + SPLIT + 108 * group
        row = 2 * CHUNK + BLOCK * group
        ref[at : at + 108, :] = value[row : row + 108]


def expand(ref, image):
    first = image * TOK_IMG
    live = lax.broadcasted_iota(jnp.int32, (TILE, 1), 0) < 7
    rows = []
    for tile in range(2 * 2 * TILES):
        rows.append(jnp.where(live, ref[first + 7 * tile : first + 7 * tile + 8, :], 0.0))
    for group in range(2):
        at = first + SPLIT + 108 * group
        rows.append(ref[at : at + 108, :])
        rows.append(jnp.zeros((4, D), F32))
    return jnp.concatenate(rows[: 2 * 2 * TILES], axis=0), rows[2 * 2 * TILES :]


def step_kernel(
    pieces,
    counts_ref,
    tok_ref,
    cot_from,
    g1_ref,
    b1_ref,
    own_wqkv_from,
    other_wqkv_from,
    own_lepe_ref,
    other_lepe_ref,
    own_lepeb_ref,
    other_lepeb_ref,
    wproj_from,
    bproj_ref,
    g2_ref,
    b2_ref,
    wfc1_from,
    bfc1_ref,
    wfc2_from,
    bfc2_ref,
    bias_ref,
    heads_ref,
    out_to,
    dtok_to,
    *rest,
):
    keep_refs, send_refs, rest = rest[:pieces], rest[pieces : 2 * pieces], rest[2 * pieces :]
    (
    out_ref,
    dtok_ref,
    written,
    cot_ref,
    wproj_ref,
    wfc1_ref,
    half_wfc2_ref,
    wide_ref,
    tall_ref,
    fetched,
    handed,
    wqkv_ref,
    lepe_ref,
    h_ref,
    normed_ref,
    qkv_ref,
    probs_ref,
    hf_ref,
    hb_ref,
    inner_ref,
    normed2_ref,
    act_ref,
    slope_ref,
    dz_ref,
    dy_ref,
    dhid_ref,
    dqkv_ref,
    acc_ref,
    bfc1_sum_ref,
    accproj_ref,
    accqkv_ref,
    acclepe_ref,
    small_ref,
    stage_ref,
    ) = rest
    rows_all = h_ref.shape[1]
    images = rows_all // IMG
    chunks = rows_all // CHUNK
    blocks = rows_all // BLOCK
    parts = pieces * keep_refs[0].shape[0]
    part_rows = keep_refs[0].shape[1]
    core = lax.axis_index("heads")
    mine = lax.axis_index("dp")
    moves = (
        (own_wqkv_from.at[:, 0], wqkv_ref.at[core]),
        (other_wqkv_from.at[:, 0], wqkv_ref.at[1 - core]),
        (wproj_from, wproj_ref),
        (wfc1_from, wfc1_ref),
        (wfc2_from, half_wfc2_ref),
        (cot_from, cot_ref),
    )
    fetches = [pltpu.make_async_copy(*move, fetched.at[place]) for place, move in enumerate(moves)]
    for fetch in fetches:
        fetch.start()
    for direction, (lepe, lepeb) in (
        (core, (own_lepe_ref, own_lepeb_ref)),
        (1 - core, (other_lepe_ref, other_lepeb_ref)),
    ):
        lepe_ref[direction, :, :TAPS] = lepe[:, :, 0]
        lepe_ref[direction, :, TAPS : TAPS + 1] = lepeb[...]

    def chunk_rows(index):
        return pl.ds(index * CHUNK, CHUNK)

    def chunk_tiles(index):
        return pl.ds(index * TILES, TILES)

    def wide_rows(index):
        return pl.ds(index * 2 * CHUNK, 2 * CHUNK)

    def wide_tiles(index):
        return pl.ds(index * 2 * TILES, 2 * TILES)

    def block_rows(index):
        return pl.ds(index * BLOCK, BLOCK)

    def is_small(block):
        return block % 6 >= 4

    def keep_of(image):
        place = lax.broadcasted_iota(jnp.int32, (IMG, 1), 0)
        limit = counts_ref[core * images + image]
        group = (place - 448) // BLOCK
        inside = (place - 448) % BLOCK
        return (place < 448) | (inside < 36 * (limit - 3 * group))

    def place_rows(target, value, image, keep=None):
        large, small = expand(value, image)
        first = image * IMG
        if keep is not None:
            large = jnp.where(keep[: 2 * CHUNK], large, 0.0)
        target[first : first + 2 * CHUNK, :] = large
        for group in range(2):
            at = first + 2 * CHUNK + group * BLOCK
            rows = small[2 * group]
            if keep is not None:
                rows = jnp.where(keep[2 * CHUNK + group * BLOCK :][:108], rows, 0.0)
            target[at : at + 108, :] = rows
            target[at + 108 : at + BLOCK, :] = small[2 * group + 1]

    dtok_ref[...] = tok_ref[...].astype(F32)
    for image in range(images):
        place_rows(h_ref.at[0], dtok_ref, image)
    for kind in range(3):
        for tap in range(TAPS):
            block = shift_block(kind, tap)
            wide_ref[kind, :, tap * KEYS : (tap + 1) * KEYS] = block
            if kind == 2:
                tall_ref[tap * BLOCK : (tap + 1) * BLOCK, :] = block

    def project_stages(layer):
        gain1, bias1 = g1_ref[pl.ds(layer, 1), :], b1_ref[pl.ds(layer, 1), :]

        def normalize(index, value):
            rows = chunk_rows(index)
            xhat, _ = norm_parts(h_ref[layer, rows, :] if value is None else value)
            normed = xhat * gain1 + bias1
            turned = split_tiles(normed) if index % 3 < 2 else normed
            return normed.astype(BF), turned.astype(BF)

        def project(index, values):
            rows = chunk_rows(index)
            for direction, value in enumerate(values):
                normed_ref[layer, direction, rows, :] = value
                qkv_ref[layer, direction, rows, :] = dot(value, wqkv_ref[direction, layer]).astype(BF)

        return normalize, project

    def forward(layer):
        if layer == 0:
            for fetch in fetches[:2]:
                fetch.wait()
            pipeline(project_stages(layer), range(chunks))

        def tap_weight(direction, tap):
            return lepe_ref[direction, layer, pl.ds(tap_row(direction, tap), 1), :]

        def score(window, _):
            direction, block = window
            rows = block_rows(block)
            query = qkv_ref[layer, direction, rows, :HW]
            keyset = qkv_ref[layer, direction, rows, HW : 2 * HW]
            return dot_nt(head_rows(keyset, heads_ref), pad_keys(query))

        def weigh(window, scores):
            direction, block = window
            rows = block_rows(block)
            bias = bias_ref[int(is_small(block))]
            probs = []
            for head in range(GH):
                part = scores[head * BLOCK : (head + 1) * BLOCK] + bias
                part = jnp.exp2((part - jnp.max(part, axis=0, keepdims=True)) * EXP_SCALE)
                part = part * (1.0 / jnp.sum(part, axis=0, keepdims=True))
                probs.append(part.astype(BF))
                probs_ref[layer, direction, rows, head * KEYS : (head + 1) * KEYS] = probs[head]
            return probs

        def mix(window, probs):
            direction, block = window
            rows = block_rows(block)
            values = qkv_ref[layer, direction, rows, 2 * HW :]
            side = values.T
            mixed = [dot(side[head * HD : (head + 1) * HD], probs[head]) for head in range(GH)]
            return jnp.concatenate(mixed, axis=0)

        def finish(window, mixed):
            direction, block = window
            lanes = slice(direction * HW, (direction + 1) * HW)
            result = mixed.T[:BLOCK] + lepe_ref[direction, layer, TAPS : TAPS + 1, :] + local[window]
            if direction == 0 or is_small(block):
                hf_ref[block * 7 : block * 7 + 7, :, :, lanes] = result.reshape(7, 2, TILE, HW)
            else:
                side = block % 2
                rows = slice((block - side) * 7, (block - side) * 7 + TILES)
                hf_ref[rows, side, :, lanes] = as_tiles(result)

        local = {}

        def filter_pair(kind, windows):
            scaled = []
            for direction, block in windows:
                values = qkv_ref[layer, direction, block_rows(block), 2 * HW :]
                scaled.append(
                    jnp.concatenate(
                        [pad_keys(values * tap_weight(direction, tap).astype(BF)) for tap in range(TAPS)], axis=0
                    )
                )
            both = dot(wide_ref[kind], jnp.concatenate(scaled, axis=1))
            for place, window in enumerate(windows):
                local[window] = both[:, place * HW : (place + 1) * HW]

        windows, fillers = [], []
        for block in range(blocks):
            windows += [(direction, block) for direction in range(2)]
            if is_small(block):
                fillers.append(functools.partial(filter_pair, 2, windows[-2:]))
            elif block % 2 == 1:
                for direction in range(2):
                    pair = [(direction, block - 1), (direction, block)]
                    fillers.append(functools.partial(filter_pair, direction, pair))
        pipeline((score, weigh, mix, finish), windows, fillers)

        if layer == 0:
            for fetch in fetches[2:5]:
                fetch.wait()
            half_wfc2_ref[...] = half_wfc2_ref[...] * jnp.asarray(0.5, BF)
        gain2, bias2 = g2_ref[pl.ds(layer, 1), :], b2_ref[pl.ds(layer, 1), :]

        def join(index, _):
            rows = chunk_rows(index)
            heads = hf_ref[chunk_tiles(index)].reshape(CHUNK, D).astype(BF)
            hb_ref[layer, rows, :] = heads
            inner = h_ref[layer, rows, :] + dot(heads, wproj_ref[layer]) + bproj_ref[pl.ds(layer, 1), :]
            inner_ref[layer, rows, :] = inner
            return inner

        def widen(index, inner):
            xhat, _ = norm_parts(inner)
            normed2 = (xhat * gain2 + bias2).astype(BF)
            normed2_ref[layer, chunk_rows(index), :] = normed2
            return dot(normed2, wfc1_ref[layer])

        def narrow(index, hidden):
            rows = chunk_rows(index)
            hidden = hidden + bfc1_ref[pl.ds(layer, 1), :]
            cdf = 1.0 + lax.erf(hidden * math.sqrt(0.5))
            act = (hidden * cdf).astype(BF)
            act_ref[layer, rows, :] = act
            bell = jnp.exp2(hidden * hidden * (-0.5 * math.log2(math.e)))
            slope_ref[layer, rows, :] = (cdf + hidden * bell * math.sqrt(2 / math.pi)).astype(BF)
            return dot(act, half_wfc2_ref[layer])

        def close(index, branch):
            rows = chunk_rows(index)
            value = inner_ref[layer, rows, :] + branch + bfc2_ref[pl.ds(layer, 1), :]
            h_ref[layer + 1, rows, :] = value
            return value

        stages = (join, widen, narrow, close)
        if layer + 1 < LAYERS:
            stages += project_stages(layer + 1)
        pipeline(stages, range(chunks))

    for layer in range(LAYERS):
        forward(layer)
    fetches[5].wait()

    for image in range(images):
        wide = pl.ds(image * IMG, IMG)
        keep = keep_of(image)
        compact(dtok_ref, image, jnp.where(keep, h_ref[LAYERS, wide, :], 0.0))
    out_ref[...] = dtok_ref[...].astype(BF)
    out_copy = pltpu.make_async_copy(out_ref, out_to, written.at[0])
    out_copy.start()
    dtok_ref[...] = cot_ref[...].astype(F32)
    for image in range(images):
        place_rows(h_ref.at[LAYERS], dtok_ref, image, keep_of(image))

    def backward(step, carry):
        layer = LAYERS - 1 - step
        base = layer * PACKED
        acc_ref[...] = jnp.zeros_like(acc_ref)
        acclepe_ref[...] = jnp.zeros_like(acclepe_ref)

        accproj_ref[...] = jnp.zeros_like(accproj_ref)
        bfc1_sum_ref[...] = jnp.zeros_like(bfc1_sum_ref)
        gain2 = g2_ref[pl.ds(layer, 1), :]

        def pair_rows(index):
            return pl.ds((index - 1) * CHUNK, 2 * CHUNK)

        def widen(index, _):
            rows = wide_rows(index)
            dz = h_ref[LAYERS, rows, :].astype(BF)
            dz_ref[rows, :] = dz
            acc_ref[5] += fold_rows(dz.astype(F32))
            return dot_nt(dz, half_wfc2_ref[layer])

        def narrow(index, dact):
            rows = wide_rows(index)
            dhid = dact * slope_ref[layer, rows, :].astype(F32)
            bfc1_sum_ref[...] += fold_rows(dhid)
            dhid = dhid.astype(BF)
            dhid_ref[rows, :] = dhid
            return dot_nt(dhid, wfc1_ref[layer])

        def close(index, dnormed):
            rows = wide_rows(index)
            dvalue, dgain = norm_back(dnormed, inner_ref[layer, rows, :], gain2)
            acc_ref[3] += fold_rows(dgain)
            acc_ref[4] += fold_rows(dnormed)
            dinner = h_ref[LAYERS, rows, :] + dvalue
            h_ref[LAYERS, rows, :] = dinner
            dy = dinner.astype(BF)
            dy_ref[rows, :] = dy
            acc_ref[2] += fold_rows(dy.astype(F32))
            return dot_nt(dy, wproj_ref[layer])

        def project(index, dheads):
            hf_ref[wide_tiles(index)] = dheads.reshape(2 * TILES, 2, TILE, D)
            rows = wide_rows(index)
            accproj_ref[...] += dot_tn(hb_ref[layer, rows, :], dy_ref[rows, :])

        pipeline((widen, narrow, close, project), range(chunks // 2))
        for half in range(2):
            stage_ref[half, pl.ds(base + PROJ_AT, D), :] = accproj_ref[:, half * HW : (half + 1) * HW].astype(BF)

        def tap_weight(direction, tap):
            return lepe_ref[direction, layer, pl.ds(tap_row(direction, tap), 1), :]

        def grad_of(direction, block):
            lanes = slice(direction * HW, (direction + 1) * HW)
            if direction == 0 or is_small(block):
                tiles = hf_ref[block * 7 : block * 7 + 7, :, :, lanes]
            else:
                side = block % 2
                tiles = hf_ref[(block - side) * 7 : (block - side) * 7 + TILES, side, :, lanes]
            return tiles.reshape(BLOCK, HW).astype(BF)

        def score(window, _):
            direction, block = window
            rows = block_rows(block)
            grad = grad_of(direction, block)
            values = qkv_ref[layer, direction, rows, 2 * HW :]
            return dot_nt(head_rows(values, heads_ref), pad_keys(grad))

        def weigh(window, dprobs):
            direction, block = window
            rows = block_rows(block)
            dscores = []
            for head in range(GH):
                part = probs_ref[layer, direction, rows, head * KEYS : (head + 1) * KEYS].astype(F32)
                dpart = dprobs[head * BLOCK : (head + 1) * BLOCK]
                inner = jnp.sum(part * dpart, axis=0, keepdims=True)
                dscores.append((part * (dpart - inner)).astype(BF))
            return dscores

        def mix(window, dscores):
            direction, block = window
            rows = block_rows(block)
            grad = grad_of(direction, block)
            query = qkv_ref[layer, direction, rows, :HW]
            side = qkv_ref[layer, direction, rows, HW : 2 * HW].T
            dkeys = dot(jnp.concatenate(dscores, axis=1), head_stack(query, heads_ref))
            dvalues = dot(probs_ref[layer, direction, rows, :], head_stack(grad, heads_ref))
            dquery = [dot(side[head * HD : (head + 1) * HD], dscores[head]) for head in range(GH)]
            return jnp.concatenate(dquery, axis=0), dkeys, dvalues

        def finish(window, results):
            direction, block = window
            rows = block_rows(block)
            grad = grad_of(direction, block)
            lanes = slice(direction * HW, (direction + 1) * HW)
            dquery, dkeys, dvalues = results
            values = qkv_ref[layer, direction, rows, 2 * HW :]
            first = direction * 3 * HW
            dqkv_ref[rows, first : first + HW] = (dquery * SCALE).T[:BLOCK].astype(BF)
            dqkv_ref[rows, first + HW : first + 2 * HW] = (dkeys * SCALE).astype(BF)
            if is_small(block):
                dvalues = dvalues + local[block][:, lanes]
                dqkv_ref[rows, first + 2 * HW : first + 3 * HW] = dvalues.astype(BF)
                return None
            grad_tiles = as_tiles(grad.astype(F32))
            result = as_tiles(dvalues)
            for tap, cells in enumerate(tap_cells(grad_tiles, direction)):
                result = result + cells * tap_weight(direction, TAPS - 1 - tap).reshape(1, 1, HW)
            result = jnp.where(live_tiles(), result, 0.0).reshape(BLOCK, HW)
            dqkv_ref[rows, first + 2 * HW : first + 3 * HW] = result.astype(BF)
            tiles = jnp.where(live_tiles(), as_tiles(values.astype(F32)), 0.0)
            for tap, cells in enumerate(tap_cells(tiles, direction)):
                acclepe_ref[direction, tap_row(direction, tap)] += jnp.sum(grad_tiles * cells, axis=0)
            acclepe_ref[direction, TAPS] += jnp.sum(grad_tiles, axis=0)
            return None

        half_rows = rows_all // 2
        spans = [pl.ds(part * half_rows, half_rows) for part in range(2)]
        sides = {}

        def feed_weights(index):
            width = FF // (2 * images)
            cols = pl.ds(index * width, width)
            partial = []

            def first(part):
                rows = spans[part]
                if (0, part) not in sides:
                    sides[0, part] = normed2_ref[layer, rows, :].T
                partial.append(dot(sides[0, part], dhid_ref[rows, cols]))

            def second(part):
                rows = spans[part]
                if (1, part) not in sides:
                    sides[1, part] = dz_ref[rows, :].T
                partial.append(dot(sides[1, part], act_ref[layer, rows, cols]))

            def store(at):
                total = partial[0] + partial[1]
                if at == FC2_AT:
                    total = total * 0.5
                for piece in range(width // HW):
                    column = index * (width // HW) + piece
                    place = base + at + column % 4 * 256
                    value = total[:, piece * HW : (piece + 1) * HW].astype(BF)
                    stage_ref[column // 4, pl.ds(place, 256), :] = value
                partial.clear()

            return [
                lambda: first(0),
                lambda: (first(1), store(FC1_AT)),
                lambda: second(0),
                lambda: (second(1), store(FC2_AT)),
            ]

        local = {}

        def filter_small(block):
            scaled = []
            for direction in range(2):
                padded = pad_keys(grad_of(direction, block).astype(F32))
                scaled.append(
                    jnp.concatenate(
                        [(padded * tap_weight(direction, TAPS - 1 - tap)).astype(BF) for tap in range(TAPS)], axis=0
                    )
                )
            local[block] = dot(wide_ref[2], jnp.concatenate(scaled, axis=1))

        def shift_small(block):
            values = [pad_keys(qkv_ref[layer, direction, block_rows(block), 2 * HW :]) for direction in range(2)]
            shifted = dot(tall_ref[...], jnp.concatenate(values, axis=1))
            for direction in range(2):
                lanes = slice(direction * HW, (direction + 1) * HW)
                grad = grad_of(direction, block).astype(F32)
                for tap in range(TAPS):
                    acclepe_ref[direction, tap_row(direction, tap)] += fold_rows(
                        grad * shifted[tap * BLOCK : (tap + 1) * BLOCK, lanes]
                    )
                acclepe_ref[direction, TAPS] += fold_rows(grad)

        order = [block for block in range(blocks) if not is_small(block)]
        order += [block for block in range(blocks) if is_small(block)]
        windows = [(direction, block) for block in order for direction in range(2)]
        fillers = [filler for index in range(2 * images) for filler in feed_weights(index)]
        for block in order:
            if is_small(block):
                fillers += [functools.partial(filter_small, block), functools.partial(shift_small, block)]
        pipeline((score, weigh, mix, finish), windows, fillers)

        accqkv_ref[...] = jnp.zeros_like(accqkv_ref)
        gain1 = g1_ref[pl.ds(layer, 1), :]

        def collect(index, _):
            rows = chunk_rows(index)
            return [
                dot_nt(dqkv_ref[rows, direction * 3 * HW : (direction + 1) * 3 * HW], wqkv_ref[direction, layer])
                for direction in range(2)
            ]

        def weigh_inputs(index, dnormed):
            if index % 2 == 1:
                rows = pair_rows(index)
                for direction in range(2):
                    accqkv_ref[direction] += dot(
                        normed_ref[layer, direction, rows, :].T,
                        dqkv_ref[rows, direction * 3 * HW : (direction + 1) * 3 * HW],
                    )
            return dnormed

        def spread(index, dnormed):
            rows = chunk_rows(index)
            straight, turned = dnormed
            dnormed = straight + (join_tiles(turned) if index % 3 < 2 else turned)
            dvalue, dgain = norm_back(dnormed, h_ref[layer, rows, :], gain1)
            acc_ref[0] += fold_rows(dgain)
            acc_ref[1] += fold_rows(dnormed)
            h_ref[LAYERS, rows, :] = h_ref[LAYERS, rows, :] + dvalue

        pipeline((collect, weigh_inputs, spread), range(chunks))
        small_ref[...] = jnp.zeros_like(small_ref)
        for direction in range(2):
            for piece in range(3):
                at = QKV_AT + 256 * piece
                stage_ref[direction, pl.ds(base + at, 256), :] = accqkv_ref[
                    direction, :, piece * HW : (piece + 1) * HW
                ].astype(BF)
            small_ref[direction, :10, :] = jnp.sum(acclepe_ref[direction], axis=1)
        sums = jnp.sum(acc_ref[...], axis=1)
        for piece in range(2):
            small_ref[0, 10 + 6 * piece : 16 + 6 * piece, :] = sums[:, piece * HW : (piece + 1) * HW]
        sums = jnp.sum(bfc1_sum_ref[...], axis=0, keepdims=True)
        for piece in range(8):
            small_ref[1, 10 + piece : 11 + piece, :] = sums[:, piece * HW : (piece + 1) * HW]
        stage_ref[:, pl.ds(base + SMALL_AT, SMALL), :] = small_ref[...].astype(BF)

        return carry

    stage_ref[:, ALL_PACKED:, :] = jnp.zeros((2, stage_ref.shape[1] - ALL_PACKED, HW), BF)
    for step in range(LAYERS):
        backward(step, 0)

    copies = []
    for slot, targets in enumerate((keep_refs, send_refs)):
        half = jnp.bitwise_xor(core, slot)
        for place in range(parts):
            part = jnp.bitwise_xor(part_at(place, parts, half), mine)
            source = stage_ref.at[half, pl.ds(pl.multiple_of(part * part_rows, 16), part_rows), :]
            target = targets[place * pieces // parts].at[place % (parts // pieces)]
            copies.append(pltpu.make_async_copy(source, target, handed.at[slot, place]))
    for copy in copies:
        copy.start()
    for image in range(images):
        compact(dtok_ref, image, h_ref[LAYERS, pl.ds(image * IMG, IMG), :])
    dtok_copy = pltpu.make_async_copy(dtok_ref, dtok_to, written.at[1])
    dtok_copy.start()
    out_copy.wait()
    for copy in copies:
        copy.wait()
    dtok_copy.wait()


def digits_of(parts, core):
    digits, stride = [], 1
    while stride < parts:
        size = 4 if parts // stride % 4 == 0 else 2
        digits.append((size, stride))
        stride *= size
    if len({size for size, _ in digits}) == 1 and core == 1:
        digits = digits[1:] + digits[:1]
    return digits


def part_at(place, parts, core):
    found = []
    for which in range(2):
        index, left = 0, place
        for size, stride in reversed(digits_of(parts, which)):
            index += left % size * stride
            left //= size
        found.append(index)
    return jnp.where(core == 0, found[0], found[1])


def unpack_kernel(
    pieces,
    *refs,
):
    own_refs, other_refs, refs = refs[:pieces], refs[pieces : 2 * pieces], refs[2 * pieces :]
    (
    g1_ref,
    b1_ref,
    gqkv_ref,
    glepe_ref,
    glepeb_ref,
    gproj_ref,
    gbproj_ref,
    g2_ref,
    b2_ref,
    gfc1_ref,
    gbfc1_ref,
    gfc2_ref,
    gbfc2_ref,
    stage_ref,
    ) = refs
    parts = pieces * own_refs[0].shape[0]
    part_rows = own_refs[0].shape[1]
    core = lax.axis_index("heads")
    mine = lax.axis_index("dp")
    for slot, sources in enumerate((own_refs, other_refs)):
        half = jnp.bitwise_xor(core, slot)
        for place in range(parts):
            part = jnp.bitwise_xor(part_at(place, parts, 0), mine)
            at = pl.ds(pl.multiple_of(part * part_rows, 16), part_rows)
            stage_ref[half, at, :] = sources[place * pieces // parts][place % (parts // pieces)]

    for layer in range(LAYERS):
        base = layer * PACKED
        for half in range(2):
            for piece in range(4):
                lanes = slice(half * 512 + piece * HW, half * 512 + (piece + 1) * HW)
                at = base + FC1_AT + 256 * piece
                gfc1_ref[layer, :, lanes] = stage_ref[half, at : at + 256, :].astype(F32)
                at = base + FC2_AT + 256 * piece
                gfc2_ref[layer, lanes, :] = stage_ref[half, at : at + 256, :].astype(F32).T
            gproj_ref[layer, :, half * HW : (half + 1) * HW] = stage_ref[
                half, base + PROJ_AT : base + PROJ_AT + 256, :
            ].astype(F32)
        for piece in range(3):
            at = base + QKV_AT + 256 * piece
            gqkv_ref[layer, 0, :, piece * HW : (piece + 1) * HW] = stage_ref[core, at : at + 256, :].astype(F32)
        small = stage_ref[core, base + SMALL_AT : base + PACKED, :].astype(F32)
        glepe_ref[layer, :, 0] = small[:TAPS]
        glepeb_ref[layer] = small[TAPS : TAPS + 1]
        small = stage_ref[0, base + SMALL_AT : base + PACKED, :].astype(F32)
        for place, ref in enumerate((g1_ref, b1_ref, gbproj_ref, g2_ref, b2_ref, gbfc2_ref)):
            for piece in range(2):
                row = 10 + 6 * piece + place
                ref[layer : layer + 1, piece * HW : (piece + 1) * HW] = small[row : row + 1]
        small = stage_ref[1, base + SMALL_AT : base + PACKED, :].astype(F32)
        for piece in range(8):
            gbfc1_ref[layer : layer + 1, piece * HW : (piece + 1) * HW] = small[10 + piece : 11 + piece]


SMEM = pl.BlockSpec(memory_space=pltpu.SMEM)
VMEM = pl.BlockSpec(memory_space=pltpu.VMEM)
ANY = pl.BlockSpec(memory_space=pl.ANY)


def shards(
    dp,
    tokens,
    cotangent,
    counts,
    ln1_gain,
    ln1_bias,
    w_qkv,
    lepe_w,
    lepe_b,
    w_proj,
    b_proj,
    ln2_gain,
    ln2_bias,
    w_fc1,
    b_fc1,
    w_fc2,
    b_fc2,
):
    tokens_here = tokens.shape[0]
    images = tokens_here // TOK_IMG
    rows = images * IMG
    swap = [(0, 1), (1, 0)]

    def across(value):
        return lax.ppermute(value, "heads", swap)

    part_rows = -(-ALL_PACKED // (16 * dp)) * 16
    scratch = [
        pltpu.VMEM((tokens_here, D), BF),
        pltpu.VMEM((tokens_here, D), F32),
        pltpu.SemaphoreType.DMA((2,)),
        pltpu.VMEM((tokens_here, D), BF),
        pltpu.VMEM((LAYERS, D, D), BF),
        pltpu.VMEM((LAYERS, D, FF), BF),
        pltpu.VMEM((LAYERS, FF, D), BF),
        pltpu.VMEM((3, BLOCK, TAPS * KEYS), BF),
        pltpu.VMEM((TAPS * BLOCK, KEYS), BF),
        pltpu.SemaphoreType.DMA((6,)),
        pltpu.SemaphoreType.DMA((2, dp)),
        pltpu.VMEM((2, LAYERS, D, 3 * HW), BF),
        pltpu.VMEM((2, LAYERS, 16, HW), F32),
        pltpu.VMEM((LAYERS + 1, rows, D), F32),
        pltpu.VMEM((LAYERS, 2, rows, D), BF),
        pltpu.VMEM((LAYERS, 2, rows, 3 * HW), BF),
        pltpu.VMEM((LAYERS, 2, rows, SPAN), BF),
        pltpu.VMEM((rows // 16, 2, TILE, D), F32),
        pltpu.VMEM((LAYERS, rows, D), BF),
        pltpu.VMEM((LAYERS, rows, D), F32),
        pltpu.VMEM((LAYERS, rows, D), BF),
        pltpu.VMEM((LAYERS, rows, FF), BF),
        pltpu.VMEM((LAYERS, rows, FF), BF),
        pltpu.VMEM((rows, D), BF),
        pltpu.VMEM((rows, D), BF),
        pltpu.VMEM((rows, FF), BF),
        pltpu.VMEM((rows, 6 * HW), BF),
        pltpu.VMEM((6, 8, D), F32),
        pltpu.VMEM((8, FF), F32),
        pltpu.VMEM((D, D), F32),
        pltpu.VMEM((2, D, 3 * HW), F32),
        pltpu.VMEM((2, TAPS + 1, 8, HW), F32),
        pltpu.VMEM((2, SMALL, HW), F32),
        pltpu.VMEM((2, part_rows * dp, HW), BF),
    ]
    pieces = digits_of(dp, 0)[0][0]
    piece = jax.ShapeDtypeStruct((dp // pieces, part_rows, HW), BF)
    result, grad, *packed = pl.pallas_call(
        functools.partial(step_kernel, pieces),
        out_shape=(
            jax.ShapeDtypeStruct((tokens_here, D), BF),
            jax.ShapeDtypeStruct((tokens_here, D), F32),
        )
        + (piece,) * (2 * pieces),
        in_specs=[SMEM, VMEM, ANY, VMEM, VMEM, ANY, ANY] + [VMEM] * 4 + [ANY] + [VMEM] * 3 + [ANY, VMEM, ANY, VMEM, VMEM, VMEM],
        out_specs=(ANY,) * (2 + 2 * pieces),
        scratch_shapes=scratch,
        compiler_params=pltpu.CompilerParams(vmem_limit_bytes=60 * 1024 * 1024),
        name="step",
    )(
        counts,
        tokens,
        cotangent,
        ln1_gain,
        ln1_bias,
        w_qkv,
        across(w_qkv),
        lepe_w.swapaxes(1, 2),
        across(lepe_w.swapaxes(1, 2)),
        lepe_b,
        across(lepe_b),
        w_proj,
        b_proj,
        ln2_gain,
        ln2_bias,
        w_fc1,
        b_fc1,
        w_fc2,
        b_fc2,
        jnp.asarray(bias_table()),
        jnp.asarray(head_table()),
    )

    def add(first, *rest):
        total = first.astype(F32)
        for item in rest:
            total = total + item.astype(F32)
        return total.astype(BF)

    keep, send = packed[:pieces], packed[pieces:]
    orders = [digits_of(dp, core) for core in range(2)]

    def hop_pairs(orders, step, hop):
        pairs = []
        for chip in range(dp):
            for core in range(2):
                pairs.append((2 * chip + core, 2 * (chip ^ (hop * orders[core][step][1])) + core))
        return pairs

    def exchange(step, values, orders=orders):
        arrived = [
            lax.ppermute(values[hop], ("dp", "heads"), hop_pairs(orders, step, hop)) for hop in range(len(values) - 1, 0, -1)
        ]
        return arrived[::-1]

    received = [across(send[hop]) for hop in range(pieces - 1, -1, -1)][::-1]
    sums = [None] + [add(keep[hop], received[hop]) for hop in range(1, pieces)]
    arrived = lax.optimization_barrier(tuple(exchange(0, sums)))
    own = add(keep[0], received[0], *arrived)
    for step in range(1, len(orders[0])):
        size = orders[0][step][0]
        cuts = own.reshape((size, own.shape[0] // size) + own.shape[1:])
        own = add(cuts[0], *lax.optimization_barrier(tuple(exchange(step, cuts))))
    for step in range(len(orders[0]) - 1, 0, -1):
        arrived = lax.optimization_barrier(tuple(exchange(step, [own] * orders[0][step][0], orders[:1] * 2)))
        own = jnp.concatenate((own,) + tuple(arrived), axis=0)
    whole = [own] + exchange(0, [own] * pieces, orders[:1] * 2)
    others = [across(value) for value in whole]
    grads = list(pl.pallas_call(
        functools.partial(unpack_kernel, pieces),
        out_shape=(
            jax.ShapeDtypeStruct((LAYERS, D), F32),
            jax.ShapeDtypeStruct((LAYERS, D), F32),
            jax.ShapeDtypeStruct((LAYERS, 1, D, 3 * HW), F32),
            jax.ShapeDtypeStruct((LAYERS, TAPS, 1, HW), F32),
            jax.ShapeDtypeStruct((LAYERS, 1, HW), F32),
            jax.ShapeDtypeStruct((LAYERS, D, D), F32),
            jax.ShapeDtypeStruct((LAYERS, D), F32),
            jax.ShapeDtypeStruct((LAYERS, D), F32),
            jax.ShapeDtypeStruct((LAYERS, D), F32),
            jax.ShapeDtypeStruct((LAYERS, D, FF), F32),
            jax.ShapeDtypeStruct((LAYERS, FF), F32),
            jax.ShapeDtypeStruct((LAYERS, FF, D), F32),
            jax.ShapeDtypeStruct((LAYERS, D), F32),
        ),
        in_specs=[VMEM] * (2 * pieces),
        out_specs=(VMEM,) * 13,
        scratch_shapes=[pltpu.VMEM((2, part_rows * dp, HW), BF)],
        compiler_params=pltpu.CompilerParams(vmem_limit_bytes=48 * 1024 * 1024),
        name="unpack",
    )(*whole, *others))
    grads[3] = grads[3].swapaxes(1, 2)
    return (result, grad) + tuple(grads)


def solution(mesh):
    spread = P(("dp", "heads"), None)
    group = (P(None, "heads", None, None), P(None, "heads", None, None), P(None, "heads", None))
    in_specs = (spread, spread, P("dp"), P(), P()) + group + (P(),) * 8
    out_specs = (spread, spread, P(), P()) + group + (P(),) * 8
    return jax.shard_map(
        functools.partial(shards, mesh.shape["dp"]),
        mesh=mesh,
        in_specs=in_specs,
        out_specs=out_specs,
        check_vma=False,
    )
```

```python
import functools
import math

import jax
import jax.numpy as jnp
import numpy as np
from jax import lax
from jax.experimental import pallas as pl
from jax.experimental.pallas import tpu as pltpu
from jax.sharding import PartitionSpec as P

D = 256
FF = 1024
HD = 32
GH = 4
HW = 128
LAYERS = 2
TOK_IMG = 608
SPLIT = 392
EPSILON = 1e-05

TILE = 8
TILES = 14
BLOCK = TILES * TILE
CHUNK = 2 * BLOCK
IMG = 6 * BLOCK
KEYS = 128
SPAN = GH * KEYS
TAPS = 9
SCALE = HD**-0.5
EXP_SCALE = SCALE * math.log2(math.e)
BF = jnp.bfloat16
F32 = jnp.float32

FC1_AT = 0
FC2_AT = 1024
PROJ_AT = 2048
QKV_AT = 2304
SMALL_AT = 3072
SMALL = 32
PACKED = SMALL_AT + SMALL
ALL_PACKED = LAYERS * PACKED


def shift_block(kind, tap):
    down, along = tap // 3 - 1, tap % 3 - 1
    place = lax.broadcasted_iota(jnp.int32, (BLOCK, 1), 0)
    if kind == 0:
        row = place >> 4
        half = (place >> 3) & 1
        cell = place & 7
        moved = 7 * half + cell + along
        target = 16 * (row + down) + moved + jnp.where(moved >= 7, 1, 0)
        inside = (cell < 7) & (moved >= 0) & (moved < 14) & (row + down >= 0) & (row + down < 7)
    elif kind == 1:
        row = place >> 3
        cell = place & 7
        moved = cell + along
        target = place + 8 * down + along
        inside = (cell < 7) & (moved >= 0) & (moved < 7) & (row + down >= 0) & (row + down < 14)
    else:
        cell = place - jnp.where(place >= 36, 36, 0) - jnp.where(place >= 72, 36, 0)
        row = (cell * 43) >> 8
        moved = cell - 6 * row + along
        target = place + 6 * down + along
        inside = (place < 108) & (moved >= 0) & (moved < 6) & (row + down >= 0) & (row + down < 6)
    column = lax.broadcasted_iota(jnp.int32, (BLOCK, KEYS), 1)
    return jnp.where(column == jnp.where(inside, target, -1), 1.0, 0.0).astype(BF)


def bias_table():
    bias = np.full((2, BLOCK, KEYS), -1e30, np.float32)
    bias[0, [key for key in range(BLOCK) if key % TILE < 7]] = 0
    for query in range(KEYS):
        first, last = (36 * (query // 36), 36 * (query // 36) + 36) if query < 108 else (0, 108)
        bias[1, first:last, query] = 0
    return bias


def head_table():
    table = np.zeros((16, HW), np.float32)
    for head in range(GH):
        table[head, head * HD : (head + 1) * HD] = 1
    return table


def dot(left, right):
    return lax.dot_general(left, right, (((1,), (0,)), ((), ())), preferred_element_type=F32)


def dot_nt(left, right):
    return lax.dot_general(left, right, (((1,), (1,)), ((), ())), preferred_element_type=F32)


def dot_tn(left, right):
    return lax.dot_general(left, right, (((0,), (0,)), ((), ())), preferred_element_type=F32)


def norm_parts(value):
    center = value - jnp.mean(value, axis=-1, keepdims=True)
    scale = lax.rsqrt(jnp.mean(center * center, axis=-1, keepdims=True) + EPSILON)
    return center * scale, scale


def norm_back(dout, value, gain):
    xhat, scale = norm_parts(value)
    grown = dout * gain
    mean = jnp.mean(grown, axis=-1, keepdims=True)
    cross = jnp.mean(grown * xhat, axis=-1, keepdims=True)
    return scale * (grown - mean - xhat * cross), dout * xhat


def fold_rows(value):
    return jnp.sum(value.reshape(value.shape[0] // 8, 8, value.shape[1]), axis=0)


def head_rows(value, heads_ref):
    return jnp.concatenate(
        [value * heads_ref[head : head + 1, :].astype(BF) for head in range(GH)], axis=0
    )


def head_stack(value, heads_ref):
    rows = []
    pad = jnp.zeros((KEYS - BLOCK, HW), BF)
    for head in range(GH):
        rows.append(value * heads_ref[head : head + 1, :].astype(BF))
        rows.append(pad)
    return jnp.concatenate(rows, axis=0)


def pad_keys(value):
    return jnp.concatenate([value, jnp.zeros((KEYS - BLOCK, value.shape[1]), value.dtype)], axis=0)


def pipeline(stages, items, fillers=()):
    results = [None] * len(items)
    fillers = list(fillers)
    for step in range(len(items) + len(stages) - 1):
        if fillers:
            fillers.pop(0)()
        for place in range(len(stages)):
            item = step - place
            if 0 <= item < len(items):
                results[item] = stages[place](items[item], results[item])
    return results


def split_tiles(value):
    rows = value.shape[0] // 16
    return jnp.concatenate(
        [value[16 * row : 16 * row + 8] for row in range(rows)]
        + [value[16 * row + 8 : 16 * row + 16] for row in range(rows)],
        axis=0,
    )


def join_tiles(value):
    half = value.shape[0] // 2
    pieces = []
    for row in range(half // 8):
        pieces.append(value[8 * row : 8 * row + 8])
        pieces.append(value[half + 8 * row : half + 8 * row + 8])
    return jnp.concatenate(pieces, axis=0)


def as_tiles(value):
    return value.reshape(TILES, TILE, HW)


def live_tiles():
    return lax.broadcasted_iota(jnp.int32, (1, TILE, HW), 1) < TILE - 1


def side_cells(tiles, direction):
    if direction == 1:
        return pltpu.roll(tiles, 1, 1), tiles, pltpu.roll(tiles, TILE - 1, 1)
    last = lax.broadcasted_iota(jnp.int32, (1, TILE, HW), 1) == TILE - 1
    left, right = [], []
    for row in range(TILES // 2):
        near, far = tiles[2 * row : 2 * row + 1], tiles[2 * row + 1 : 2 * row + 2]
        near_left = pltpu.roll(near, 1, 1)
        far_right = pltpu.roll(far, TILE - 1, 1)
        left += [near_left, pltpu.roll(jnp.where(last, near_left, far), 1, 1)]
        right += [pltpu.roll(jnp.where(last, far_right, near), TILE - 1, 1), far_right]
    return jnp.concatenate(left, axis=0), tiles, jnp.concatenate(right, axis=0)


def tap_cells(tiles, direction):
    stride = 2 if direction == 0 else 1
    zeros = jnp.zeros((stride, TILE, HW), F32)
    padded = [jnp.concatenate([zeros, side, zeros], axis=0) for side in side_cells(tiles, direction)]
    return [padded[tap % 3][(tap // 3) * stride : (tap // 3) * stride + TILES] for tap in range(TAPS)]


def tap_row(direction, tap):
    return tap if direction == 0 else 3 * (tap % 3) + tap // 3


def compact(ref, image, value):
    first = image * TOK_IMG
    for tile in range(2 * 2 * TILES):
        ref[first + 7 * tile : first + 7 * tile + 7, :] = value[TILE * tile : TILE * tile + 7]
    for group in range(2):
        at = first + SPLIT + 108 * group
        row = 2 * CHUNK + BLOCK * group
        ref[at : at + 108, :] = value[row : row + 108]


def expand(ref, image):
    first = image * TOK_IMG
    live = lax.broadcasted_iota(jnp.int32, (TILE, 1), 0) < 7
    rows = []
    for tile in range(2 * 2 * TILES):
        rows.append(jnp.where(live, ref[first + 7 * tile : first + 7 * tile + 8, :], 0.0))
    for group in range(2):
        at = first + SPLIT + 108 * group
        rows.append(ref[at : at + 108, :])
        rows.append(jnp.zeros((4, D), F32))
    return jnp.concatenate(rows[: 2 * 2 * TILES], axis=0), rows[2 * 2 * TILES :]


def step_kernel(
    pieces,
    counts_ref,
    tok_ref,
    cot_from,
    g1_ref,
    b1_ref,
    own_wqkv_from,
    other_wqkv_from,
    own_lepe_ref,
    other_lepe_ref,
    own_lepeb_ref,
    other_lepeb_ref,
    wproj_from,
    bproj_ref,
    g2_ref,
    b2_ref,
    wfc1_from,
    bfc1_ref,
    wfc2_from,
    bfc2_ref,
    bias_ref,
    heads_ref,
    out_to,
    dtok_to,
    *rest,
):
    keep_refs, send_refs, rest = rest[:pieces], rest[pieces : 2 * pieces], rest[2 * pieces :]
    (
    out_ref,
    dtok_ref,
    written,
    cot_ref,
    wproj_ref,
    wfc1_ref,
    half_wfc2_ref,
    wide_ref,
    tall_ref,
    fetched,
    handed,
    wqkv_ref,
    lepe_ref,
    h_ref,
    normed_ref,
    qkv_ref,
    probs_ref,
    hf_ref,
    hb_ref,
    inner_ref,
    normed2_ref,
    act_ref,
    slope_ref,
    dz_ref,
    dy_ref,
    dhid_ref,
    dqkv_ref,
    acc_ref,
    bfc1_sum_ref,
    accproj_ref,
    accqkv_ref,
    acclepe_ref,
    small_ref,
    stage_ref,
    ) = rest
    rows_all = h_ref.shape[1]
    images = rows_all // IMG
    chunks = rows_all // CHUNK
    blocks = rows_all // BLOCK
    parts = pieces * keep_refs[0].shape[0]
    part_rows = keep_refs[0].shape[1]
    core = lax.axis_index("heads")
    mine = lax.axis_index("dp")
    moves = (
        (own_wqkv_from.at[:, 0], wqkv_ref.at[core]),
        (other_wqkv_from.at[:, 0], wqkv_ref.at[1 - core]),
        (wproj_from, wproj_ref),
        (wfc1_from, wfc1_ref),
        (wfc2_from, half_wfc2_ref),
        (cot_from, cot_ref),
    )
    fetches = [pltpu.make_async_copy(*move, fetched.at[place]) for place, move in enumerate(moves)]
    for fetch in fetches:
        fetch.start()
    for direction, (lepe, lepeb) in (
        (core, (own_lepe_ref, own_lepeb_ref)),
        (1 - core, (other_lepe_ref, other_lepeb_ref)),
    ):
        lepe_ref[direction, :, :TAPS] = lepe[:, :, 0]
        lepe_ref[direction, :, TAPS : TAPS + 1] = lepeb[...]

    def chunk_rows(index):
        return pl.ds(index * CHUNK, CHUNK)

    def chunk_tiles(index):
        return pl.ds(index * TILES, TILES)

    def wide_rows(index):
        return pl.ds(index * 2 * CHUNK, 2 * CHUNK)

    def wide_tiles(index):
        return pl.ds(index * 2 * TILES, 2 * TILES)

    def block_rows(index):
        return pl.ds(index * BLOCK, BLOCK)

    def is_small(block):
        return block % 6 >= 4

    def keep_of(image):
        place = lax.broadcasted_iota(jnp.int32, (IMG, 1), 0)
        limit = counts_ref[core * images + image]
        group = (place - 448) // BLOCK
        inside = (place - 448) % BLOCK
        return (place < 448) | (inside < 36 * (limit - 3 * group))

    def place_rows(target, value, image, keep=None):
        large, small = expand(value, image)
        first = image * IMG
        if keep is not None:
            large = jnp.where(keep[: 2 * CHUNK], large, 0.0)
        target[first : first + 2 * CHUNK, :] = large
        for group in range(2):
            at = first + 2 * CHUNK + group * BLOCK
            rows = small[2 * group]
            if keep is not None:
                rows = jnp.where(keep[2 * CHUNK + group * BLOCK :][:108], rows, 0.0)
            target[at : at + 108, :] = rows
            target[at + 108 : at + BLOCK, :] = small[2 * group + 1]

    dtok_ref[...] = tok_ref[...].astype(F32)
    for image in range(images):
        place_rows(h_ref.at[0], dtok_ref, image)
    for kind in range(3):
        for tap in range(TAPS):
            block = shift_block(kind, tap)
            wide_ref[kind, :, tap * KEYS : (tap + 1) * KEYS] = block
            if kind == 2:
                tall_ref[tap * BLOCK : (tap + 1) * BLOCK, :] = block

    def project_stages(layer):
        gain1, bias1 = g1_ref[pl.ds(layer, 1), :], b1_ref[pl.ds(layer, 1), :]

        def normalize(index, value):
            rows = chunk_rows(index)
            xhat, _ = norm_parts(h_ref[layer, rows, :] if value is None else value)
            normed = xhat * gain1 + bias1
            turned = split_tiles(normed) if index % 3 < 2 else normed
            return normed.astype(BF), turned.astype(BF)

        def project(index, values):
            rows = chunk_rows(index)
            for direction, value in enumerate(values):
                normed_ref[layer, direction, rows, :] = value
                qkv_ref[layer, direction, rows, :] = dot(value, wqkv_ref[direction, layer]).astype(BF)

        return normalize, project

    def forward(layer):
        if layer == 0:
            for fetch in fetches[:2]:
                fetch.wait()
            pipeline(project_stages(layer), range(chunks))

        def tap_weight(direction, tap):
            return lepe_ref[direction, layer, pl.ds(tap_row(direction, tap), 1), :]

        def score(window, _):
            direction, block = window
            rows = block_rows(block)
            query = qkv_ref[layer, direction, rows, :HW]
            keyset = qkv_ref[layer, direction, rows, HW : 2 * HW]
            return dot_nt(head_rows(keyset, heads_ref), pad_keys(query))

        def weigh(window, scores):
            direction, block = window
            rows = block_rows(block)
            bias = bias_ref[int(is_small(block))]
            probs = []
            for head in range(GH):
                part = scores[head * BLOCK : (head + 1) * BLOCK] + bias
                part = jnp.exp2((part - jnp.max(part, axis=0, keepdims=True)) * EXP_SCALE)
                part = part * (1.0 / jnp.sum(part, axis=0, keepdims=True))
                probs.append(part.astype(BF))
                probs_ref[layer, direction, rows, head * KEYS : (head + 1) * KEYS] = probs[head]
            return probs

        def mix(window, probs):
            direction, block = window
            rows = block_rows(block)
            values = qkv_ref[layer, direction, rows, 2 * HW :]
            side = values.T
            mixed = [dot(side[head * HD : (head + 1) * HD], probs[head]) for head in range(GH)]
            return jnp.concatenate(mixed, axis=0)

        def finish(window, mixed):
            direction, block = window
            lanes = slice(direction * HW, (direction + 1) * HW)
            result = mixed.T[:BLOCK] + lepe_ref[direction, layer, TAPS : TAPS + 1, :] + local[window]
            if direction == 0 or is_small(block):
                hf_ref[block * 7 : block * 7 + 7, :, :, lanes] = result.reshape(7, 2, TILE, HW)
            else:
                side = block % 2
                rows = slice((block - side) * 7, (block - side) * 7 + TILES)
                hf_ref[rows, side, :, lanes] = as_tiles(result)

        local = {}

        def filter_pair(kind, windows):
            scaled = []
            for direction, block in windows:
                values = qkv_ref[layer, direction, block_rows(block), 2 * HW :]
                scaled.append(
                    jnp.concatenate(
                        [pad_keys(values * tap_weight(direction, tap).astype(BF)) for tap in range(TAPS)], axis=0
                    )
                )
            both = dot(wide_ref[kind], jnp.concatenate(scaled, axis=1))
            for place, window in enumerate(windows):
                local[window] = both[:, place * HW : (place + 1) * HW]

        windows, fillers = [], []
        for block in range(blocks):
            windows += [(direction, block) for direction in range(2)]
            if is_small(block):
                fillers.append(functools.partial(filter_pair, 2, windows[-2:]))
            elif block % 2 == 1:
                for direction in range(2):
                    pair = [(direction, block - 1), (direction, block)]
                    fillers.append(functools.partial(filter_pair, direction, pair))
        pipeline((score, weigh, mix, finish), windows, fillers)

        if layer == 0:
            for fetch in fetches[2:5]:
                fetch.wait()
            half_wfc2_ref[...] = half_wfc2_ref[...] * jnp.asarray(0.5, BF)
        gain2, bias2 = g2_ref[pl.ds(layer, 1), :], b2_ref[pl.ds(layer, 1), :]

        def join(index, _):
            rows = chunk_rows(index)
            heads = hf_ref[chunk_tiles(index)].reshape(CHUNK, D).astype(BF)
            hb_ref[layer, rows, :] = heads
            inner = h_ref[layer, rows, :] + dot(heads, wproj_ref[layer]) + bproj_ref[pl.ds(layer, 1), :]
            inner_ref[layer, rows, :] = inner
            return inner

        def widen(index, inner):
            xhat, _ = norm_parts(inner)
            normed2 = (xhat * gain2 + bias2).astype(BF)
            normed2_ref[layer, chunk_rows(index), :] = normed2
            return dot(normed2, wfc1_ref[layer])

        def narrow(index, hidden):
            rows = chunk_rows(index)
            hidden = hidden + bfc1_ref[pl.ds(layer, 1), :]
            cdf = 1.0 + lax.erf(hidden * math.sqrt(0.5))
            act = (hidden * cdf).astype(BF)
            act_ref[layer, rows, :] = act
            bell = jnp.exp2(hidden * hidden * (-0.5 * math.log2(math.e)))
            slope_ref[layer, rows, :] = (cdf + hidden * bell * math.sqrt(2 / math.pi)).astype(BF)
            return dot(act, half_wfc2_ref[layer])

        def close(index, branch):
            rows = chunk_rows(index)
            value = inner_ref[layer, rows, :] + branch + bfc2_ref[pl.ds(layer, 1), :]
            h_ref[layer + 1, rows, :] = value
            return value

        stages = (join, widen, narrow, close)
        if layer + 1 < LAYERS:
            stages += project_stages(layer + 1)
        pipeline(stages, range(chunks))

    for layer in range(LAYERS):
        forward(layer)
    fetches[5].wait()

    for image in range(images):
        wide = pl.ds(image * IMG, IMG)
        keep = keep_of(image)
        compact(dtok_ref, image, jnp.where(keep, h_ref[LAYERS, wide, :], 0.0))
    out_ref[...] = dtok_ref[...].astype(BF)
    out_copy = pltpu.make_async_copy(out_ref, out_to, written.at[0])
    out_copy.start()
    dtok_ref[...] = cot_ref[...].astype(F32)
    for image in range(images):
        place_rows(h_ref.at[LAYERS], dtok_ref, image, keep_of(image))

    def backward(step, carry):
        layer = LAYERS - 1 - step
        base = pl.multiple_of(layer * PACKED, 16)
        acc_ref[...] = jnp.zeros_like(acc_ref)
        acclepe_ref[...] = jnp.zeros_like(acclepe_ref)

        accproj_ref[...] = jnp.zeros_like(accproj_ref)
        bfc1_sum_ref[...] = jnp.zeros_like(bfc1_sum_ref)
        gain2 = g2_ref[pl.ds(layer, 1), :]

        def pair_rows(index):
            return pl.ds((index - 1) * CHUNK, 2 * CHUNK)

        def widen(index, _):
            rows = wide_rows(index)
            dz = h_ref[LAYERS, rows, :].astype(BF)
            dz_ref[rows, :] = dz
            acc_ref[5] += fold_rows(dz.astype(F32))
            return dot_nt(dz, half_wfc2_ref[layer])

        def narrow(index, dact):
            rows = wide_rows(index)
            dhid = dact * slope_ref[layer, rows, :].astype(F32)
            bfc1_sum_ref[...] += fold_rows(dhid)
            dhid = dhid.astype(BF)
            dhid_ref[rows, :] = dhid
            return dot_nt(dhid, wfc1_ref[layer])

        def close(index, dnormed):
            rows = wide_rows(index)
            dvalue, dgain = norm_back(dnormed, inner_ref[layer, rows, :], gain2)
            acc_ref[3] += fold_rows(dgain)
            acc_ref[4] += fold_rows(dnormed)
            dinner = h_ref[LAYERS, rows, :] + dvalue
            h_ref[LAYERS, rows, :] = dinner
            dy = dinner.astype(BF)
            dy_ref[rows, :] = dy
            acc_ref[2] += fold_rows(dy.astype(F32))
            return dot_nt(dy, wproj_ref[layer])

        def project(index, dheads):
            hf_ref[wide_tiles(index)] = dheads.reshape(2 * TILES, 2, TILE, D)
            rows = wide_rows(index)
            accproj_ref[...] += dot_tn(hb_ref[layer, rows, :], dy_ref[rows, :])

        pipeline((widen, narrow, close, project), range(chunks // 2))
        for half in range(2):
            stage_ref[half, pl.ds(base + PROJ_AT, D), :] = accproj_ref[:, half * HW : (half + 1) * HW].astype(BF)

        def tap_weight(direction, tap):
            return lepe_ref[direction, layer, pl.ds(tap_row(direction, tap), 1), :]

        def grad_of(direction, block):
            lanes = slice(direction * HW, (direction + 1) * HW)
            if direction == 0 or is_small(block):
                tiles = hf_ref[block * 7 : block * 7 + 7, :, :, lanes]
            else:
                side = block % 2
                tiles = hf_ref[(block - side) * 7 : (block - side) * 7 + TILES, side, :, lanes]
            return tiles.reshape(BLOCK, HW).astype(BF)

        def score(window, _):
            direction, block = window
            rows = block_rows(block)
            grad = grad_of(direction, block)
            values = qkv_ref[layer, direction, rows, 2 * HW :]
            return dot_nt(head_rows(values, heads_ref), pad_keys(grad))

        def weigh(window, dprobs):
            direction, block = window
            rows = block_rows(block)
            dscores = []
            for head in range(GH):
                part = probs_ref[layer, direction, rows, head * KEYS : (head + 1) * KEYS].astype(F32)
                dpart = dprobs[head * BLOCK : (head + 1) * BLOCK]
                inner = jnp.sum(part * dpart, axis=0, keepdims=True)
                dscores.append((part * (dpart - inner)).astype(BF))
            return dscores

        def mix(window, dscores):
            direction, block = window
            rows = block_rows(block)
            grad = grad_of(direction, block)
            query = qkv_ref[layer, direction, rows, :HW]
            side = qkv_ref[layer, direction, rows, HW : 2 * HW].T
            dkeys = dot(jnp.concatenate(dscores, axis=1), head_stack(query, heads_ref))
            dvalues = dot(probs_ref[layer, direction, rows, :], head_stack(grad, heads_ref))
            dquery = [dot(side[head * HD : (head + 1) * HD], dscores[head]) for head in range(GH)]
            return jnp.concatenate(dquery, axis=0), dkeys, dvalues

        def finish(window, results):
            direction, block = window
            rows = block_rows(block)
            grad = grad_of(direction, block)
            lanes = slice(direction * HW, (direction + 1) * HW)
            dquery, dkeys, dvalues = results
            values = qkv_ref[layer, direction, rows, 2 * HW :]
            first = direction * 3 * HW
            dqkv_ref[rows, first : first + HW] = (dquery * SCALE).T[:BLOCK].astype(BF)
            dqkv_ref[rows, first + HW : first + 2 * HW] = (dkeys * SCALE).astype(BF)
            if is_small(block):
                dvalues = dvalues + local[block][:, lanes]
                dqkv_ref[rows, first + 2 * HW : first + 3 * HW] = dvalues.astype(BF)
                return None
            grad_tiles = as_tiles(grad.astype(F32))
            result = as_tiles(dvalues)
            for tap, cells in enumerate(tap_cells(grad_tiles, direction)):
                result = result + cells * tap_weight(direction, TAPS - 1 - tap).reshape(1, 1, HW)
            result = jnp.where(live_tiles(), result, 0.0).reshape(BLOCK, HW)
            dqkv_ref[rows, first + 2 * HW : first + 3 * HW] = result.astype(BF)
            tiles = jnp.where(live_tiles(), as_tiles(values.astype(F32)), 0.0)
            for tap, cells in enumerate(tap_cells(tiles, direction)):
                acclepe_ref[direction, tap_row(direction, tap)] += jnp.sum(grad_tiles * cells, axis=0)
            acclepe_ref[direction, TAPS] += jnp.sum(grad_tiles, axis=0)
            return None

        half_rows = rows_all // 2
        spans = [pl.ds(part * half_rows, half_rows) for part in range(2)]
        sides = {}

        def feed_weights(index):
            width = FF // (2 * images)
            cols = pl.ds(index * width, width)
            partial = []

            def first(part):
                rows = spans[part]
                if (0, part) not in sides:
                    sides[0, part] = normed2_ref[layer, rows, :].T
                partial.append(dot(sides[0, part], dhid_ref[rows, cols]))

            def second(part):
                rows = spans[part]
                if (1, part) not in sides:
                    sides[1, part] = dz_ref[rows, :].T
                partial.append(dot(sides[1, part], act_ref[layer, rows, cols]))

            def store(at):
                total = partial[0] + partial[1]
                if at == FC2_AT:
                    total = total * 0.5
                for piece in range(width // HW):
                    column = index * (width // HW) + piece
                    place = pl.multiple_of(base + at + column % 4 * 256, 16)
                    value = total[:, piece * HW : (piece + 1) * HW].astype(BF)
                    stage_ref[column // 4, pl.ds(place, 256), :] = value
                partial.clear()

            return [
                lambda: first(0),
                lambda: (first(1), store(FC1_AT)),
                lambda: second(0),
                lambda: (second(1), store(FC2_AT)),
            ]

        local = {}

        def filter_small(block):
            scaled = []
            for direction in range(2):
                padded = pad_keys(grad_of(direction, block).astype(F32))
                scaled.append(
                    jnp.concatenate(
                        [(padded * tap_weight(direction, TAPS - 1 - tap)).astype(BF) for tap in range(TAPS)], axis=0
                    )
                )
            local[block] = dot(wide_ref[2], jnp.concatenate(scaled, axis=1))

        def shift_small(block):
            values = [pad_keys(qkv_ref[layer, direction, block_rows(block), 2 * HW :]) for direction in range(2)]
            shifted = dot(tall_ref[...], jnp.concatenate(values, axis=1))
            for direction in range(2):
                lanes = slice(direction * HW, (direction + 1) * HW)
                grad = grad_of(direction, block).astype(F32)
                for tap in range(TAPS):
                    acclepe_ref[direction, tap_row(direction, tap)] += fold_rows(
                        grad * shifted[tap * BLOCK : (tap + 1) * BLOCK, lanes]
                    )
                acclepe_ref[direction, TAPS] += fold_rows(grad)

        order = [block for block in range(blocks) if not is_small(block)]
        order += [block for block in range(blocks) if is_small(block)]
        windows = [(direction, block) for block in order for direction in range(2)]
        fillers = [filler for index in range(2 * images) for filler in feed_weights(index)]
        for block in order:
            if is_small(block):
                fillers += [functools.partial(filter_small, block), functools.partial(shift_small, block)]
        pipeline((score, weigh, mix, finish), windows, fillers)

        accqkv_ref[...] = jnp.zeros_like(accqkv_ref)
        gain1 = g1_ref[pl.ds(layer, 1), :]

        def collect(index, _):
            rows = chunk_rows(index)
            return [
                dot_nt(dqkv_ref[rows, direction * 3 * HW : (direction + 1) * 3 * HW], wqkv_ref[direction, layer])
                for direction in range(2)
            ]

        def weigh_inputs(index, dnormed):
            if index % 2 == 1:
                rows = pair_rows(index)
                for direction in range(2):
                    accqkv_ref[direction] += dot(
                        normed_ref[layer, direction, rows, :].T,
                        dqkv_ref[rows, direction * 3 * HW : (direction + 1) * 3 * HW],
                    )
            return dnormed

        def spread(index, dnormed):
            rows = chunk_rows(index)
            straight, turned = dnormed
            dnormed = straight + (join_tiles(turned) if index % 3 < 2 else turned)
            dvalue, dgain = norm_back(dnormed, h_ref[layer, rows, :], gain1)
            acc_ref[0] += fold_rows(dgain)
            acc_ref[1] += fold_rows(dnormed)
            h_ref[LAYERS, rows, :] = h_ref[LAYERS, rows, :] + dvalue

        pipeline((collect, weigh_inputs, spread), range(chunks))
        small_ref[...] = jnp.zeros_like(small_ref)
        for direction in range(2):
            for piece in range(3):
                at = QKV_AT + 256 * piece
                stage_ref[direction, pl.ds(base + at, 256), :] = accqkv_ref[
                    direction, :, piece * HW : (piece + 1) * HW
                ].astype(BF)
            small_ref[direction, :10, :] = jnp.sum(acclepe_ref[direction], axis=1)
        sums = jnp.sum(acc_ref[...], axis=1)
        for piece in range(2):
            small_ref[0, 10 + 6 * piece : 16 + 6 * piece, :] = sums[:, piece * HW : (piece + 1) * HW]
        sums = jnp.sum(bfc1_sum_ref[...], axis=0, keepdims=True)
        for piece in range(8):
            small_ref[1, 10 + piece : 11 + piece, :] = sums[:, piece * HW : (piece + 1) * HW]
        stage_ref[:, pl.ds(base + SMALL_AT, SMALL), :] = small_ref[...].astype(BF)

        return carry

    stage_ref[:, ALL_PACKED:, :] = jnp.zeros((2, stage_ref.shape[1] - ALL_PACKED, HW), BF)
    lax.fori_loop(0, LAYERS, backward, 0)

    copies = []
    for slot, targets in enumerate((keep_refs, send_refs)):
        half = jnp.bitwise_xor(core, slot)
        for place in range(parts):
            part = jnp.bitwise_xor(part_at(place, parts, half), mine)
            source = stage_ref.at[half, pl.ds(pl.multiple_of(part * part_rows, 16), part_rows), :]
            target = targets[place * pieces // parts].at[place % (parts // pieces)]
            copies.append(pltpu.make_async_copy(source, target, handed.at[slot, place]))
    for copy in copies:
        copy.start()
    for image in range(images):
        compact(dtok_ref, image, h_ref[LAYERS, pl.ds(image * IMG, IMG), :])
    dtok_copy = pltpu.make_async_copy(dtok_ref, dtok_to, written.at[1])
    dtok_copy.start()
    out_copy.wait()
    for copy in copies:
        copy.wait()
    dtok_copy.wait()


def digits_of(parts, core):
    digits, stride = [], 1
    while stride < parts:
        size = 4 if parts // stride % 4 == 0 else 2
        digits.append((size, stride))
        stride *= size
    if len({size for size, _ in digits}) == 1 and core == 1:
        digits = digits[1:] + digits[:1]
    return digits


def part_at(place, parts, core):
    found = []
    for which in range(2):
        index, left = 0, place
        for size, stride in reversed(digits_of(parts, which)):
            index += left % size * stride
            left //= size
        found.append(index)
    return jnp.where(core == 0, found[0], found[1])


def unpack_kernel(
    pieces,
    *refs,
):
    own_refs, other_refs, refs = refs[:pieces], refs[pieces : 2 * pieces], refs[2 * pieces :]
    (
    g1_ref,
    b1_ref,
    gqkv_ref,
    glepe_ref,
    glepeb_ref,
    gproj_ref,
    gbproj_ref,
    g2_ref,
    b2_ref,
    gfc1_ref,
    gbfc1_ref,
    gfc2_ref,
    gbfc2_ref,
    stage_ref,
    ) = refs
    parts = pieces * own_refs[0].shape[0]
    part_rows = own_refs[0].shape[1]
    core = lax.axis_index("heads")
    mine = lax.axis_index("dp")
    for slot, sources in enumerate((own_refs, other_refs)):
        half = jnp.bitwise_xor(core, slot)
        for place in range(parts):
            part = jnp.bitwise_xor(part_at(place, parts, 0), mine)
            at = pl.ds(pl.multiple_of(part * part_rows, 16), part_rows)
            stage_ref[half, at, :] = sources[place * pieces // parts][place % (parts // pieces)]

    for layer in range(LAYERS):
        base = layer * PACKED
        for half in range(2):
            for piece in range(4):
                lanes = slice(half * 512 + piece * HW, half * 512 + (piece + 1) * HW)
                at = base + FC1_AT + 256 * piece
                gfc1_ref[layer, :, lanes] = stage_ref[half, at : at + 256, :].astype(F32)
                at = base + FC2_AT + 256 * piece
                gfc2_ref[layer, lanes, :] = stage_ref[half, at : at + 256, :].astype(F32).T
            gproj_ref[layer, :, half * HW : (half + 1) * HW] = stage_ref[
                half, base + PROJ_AT : base + PROJ_AT + 256, :
            ].astype(F32)
        for piece in range(3):
            at = base + QKV_AT + 256 * piece
            gqkv_ref[layer, 0, :, piece * HW : (piece + 1) * HW] = stage_ref[core, at : at + 256, :].astype(F32)
        small = stage_ref[core, base + SMALL_AT : base + PACKED, :].astype(F32)
        glepe_ref[layer, :, 0] = small[:TAPS]
        glepeb_ref[layer] = small[TAPS : TAPS + 1]
        small = stage_ref[0, base + SMALL_AT : base + PACKED, :].astype(F32)
        for place, ref in enumerate((g1_ref, b1_ref, gbproj_ref, g2_ref, b2_ref, gbfc2_ref)):
            for piece in range(2):
                row = 10 + 6 * piece + place
                ref[layer : layer + 1, piece * HW : (piece + 1) * HW] = small[row : row + 1]
        small = stage_ref[1, base + SMALL_AT : base + PACKED, :].astype(F32)
        for piece in range(8):
            gbfc1_ref[layer : layer + 1, piece * HW : (piece + 1) * HW] = small[10 + piece : 11 + piece]


SMEM = pl.BlockSpec(memory_space=pltpu.SMEM)
VMEM = pl.BlockSpec(memory_space=pltpu.VMEM)
ANY = pl.BlockSpec(memory_space=pl.ANY)


def shards(
    dp,
    tokens,
    cotangent,
    counts,
    ln1_gain,
    ln1_bias,
    w_qkv,
    lepe_w,
    lepe_b,
    w_proj,
    b_proj,
    ln2_gain,
    ln2_bias,
    w_fc1,
    b_fc1,
    w_fc2,
    b_fc2,
):
    tokens_here = tokens.shape[0]
    images = tokens_here // TOK_IMG
    rows = images * IMG
    swap = [(0, 1), (1, 0)]

    def across(value):
        return lax.ppermute(value, "heads", swap)

    part_rows = -(-ALL_PACKED // (16 * dp)) * 16
    scratch = [
        pltpu.VMEM((tokens_here, D), BF),
        pltpu.VMEM((tokens_here, D), F32),
        pltpu.SemaphoreType.DMA((2,)),
        pltpu.VMEM((tokens_here, D), BF),
        pltpu.VMEM((LAYERS, D, D), BF),
        pltpu.VMEM((LAYERS, D, FF), BF),
        pltpu.VMEM((LAYERS, FF, D), BF),
        pltpu.VMEM((3, BLOCK, TAPS * KEYS), BF),
        pltpu.VMEM((TAPS * BLOCK, KEYS), BF),
        pltpu.SemaphoreType.DMA((6,)),
        pltpu.SemaphoreType.DMA((2, dp)),
        pltpu.VMEM((2, LAYERS, D, 3 * HW), BF),
        pltpu.VMEM((2, LAYERS, 16, HW), F32),
        pltpu.VMEM((LAYERS + 1, rows, D), F32),
        pltpu.VMEM((LAYERS, 2, rows, D), BF),
        pltpu.VMEM((LAYERS, 2, rows, 3 * HW), BF),
        pltpu.VMEM((LAYERS, 2, rows, SPAN), BF),
        pltpu.VMEM((rows // 16, 2, TILE, D), F32),
        pltpu.VMEM((LAYERS, rows, D), BF),
        pltpu.VMEM((LAYERS, rows, D), F32),
        pltpu.VMEM((LAYERS, rows, D), BF),
        pltpu.VMEM((LAYERS, rows, FF), BF),
        pltpu.VMEM((LAYERS, rows, FF), BF),
        pltpu.VMEM((rows, D), BF),
        pltpu.VMEM((rows, D), BF),
        pltpu.VMEM((rows, FF), BF),
        pltpu.VMEM((rows, 6 * HW), BF),
        pltpu.VMEM((6, 8, D), F32),
        pltpu.VMEM((8, FF), F32),
        pltpu.VMEM((D, D), F32),
        pltpu.VMEM((2, D, 3 * HW), F32),
        pltpu.VMEM((2, TAPS + 1, 8, HW), F32),
        pltpu.VMEM((2, SMALL, HW), F32),
        pltpu.VMEM((2, part_rows * dp, HW), BF),
    ]
    pieces = digits_of(dp, 0)[0][0]
    piece = jax.ShapeDtypeStruct((dp // pieces, part_rows, HW), BF)
    result, grad, *packed = pl.pallas_call(
        functools.partial(step_kernel, pieces),
        out_shape=(
            jax.ShapeDtypeStruct((tokens_here, D), BF),
            jax.ShapeDtypeStruct((tokens_here, D), F32),
        )
        + (piece,) * (2 * pieces),
        in_specs=[SMEM, VMEM, ANY, VMEM, VMEM, ANY, ANY] + [VMEM] * 4 + [ANY] + [VMEM] * 3 + [ANY, VMEM, ANY, VMEM, VMEM, VMEM],
        out_specs=(ANY,) * (2 + 2 * pieces),
        scratch_shapes=scratch,
        compiler_params=pltpu.CompilerParams(vmem_limit_bytes=60 * 1024 * 1024),
        name="step",
    )(
        counts,
        tokens,
        cotangent,
        ln1_gain,
        ln1_bias,
        w_qkv,
        across(w_qkv),
        lepe_w.swapaxes(1, 2),
        across(lepe_w.swapaxes(1, 2)),
        lepe_b,
        across(lepe_b),
        w_proj,
        b_proj,
        ln2_gain,
        ln2_bias,
        w_fc1,
        b_fc1,
        w_fc2,
        b_fc2,
        jnp.asarray(bias_table()),
        jnp.asarray(head_table()),
    )

    def add(first, *rest):
        total = first.astype(F32)
        for item in rest:
            total = total + item.astype(F32)
        return total.astype(BF)

    keep, send = packed[:pieces], packed[pieces:]
    orders = [digits_of(dp, core) for core in range(2)]

    def hop_pairs(orders, step, hop):
        pairs = []
        for chip in range(dp):
            for core in range(2):
                pairs.append((2 * chip + core, 2 * (chip ^ (hop * orders[core][step][1])) + core))
        return pairs

    def exchange(step, values, orders=orders):
        arrived = [
            lax.ppermute(values[hop], ("dp", "heads"), hop_pairs(orders, step, hop)) for hop in range(len(values) - 1, 0, -1)
        ]
        return arrived[::-1]

    received = [across(send[hop]) for hop in range(pieces - 1, -1, -1)][::-1]
    sums = [None] + [add(keep[hop], received[hop]) for hop in range(1, pieces)]
    arrived = lax.optimization_barrier(tuple(exchange(0, sums)))
    own = add(keep[0], received[0], *arrived)
    for step in range(1, len(orders[0])):
        size = orders[0][step][0]
        cuts = own.reshape((size, own.shape[0] // size) + own.shape[1:])
        own = add(cuts[0], *lax.optimization_barrier(tuple(exchange(step, cuts))))
    for step in range(len(orders[0]) - 1, 0, -1):
        arrived = lax.optimization_barrier(tuple(exchange(step, [own] * orders[0][step][0], orders[:1] * 2)))
        own = jnp.concatenate((own,) + tuple(arrived), axis=0)
    whole = [own] + exchange(0, [own] * pieces, orders[:1] * 2)
    others = [across(value) for value in whole]
    grads = list(pl.pallas_call(
        functools.partial(unpack_kernel, pieces),
        out_shape=(
            jax.ShapeDtypeStruct((LAYERS, D), F32),
            jax.ShapeDtypeStruct((LAYERS, D), F32),
            jax.ShapeDtypeStruct((LAYERS, 1, D, 3 * HW), F32),
            jax.ShapeDtypeStruct((LAYERS, TAPS, 1, HW), F32),
            jax.ShapeDtypeStruct((LAYERS, 1, HW), F32),
            jax.ShapeDtypeStruct((LAYERS, D, D), F32),
            jax.ShapeDtypeStruct((LAYERS, D), F32),
            jax.ShapeDtypeStruct((LAYERS, D), F32),
            jax.ShapeDtypeStruct((LAYERS, D), F32),
            jax.ShapeDtypeStruct((LAYERS, D, FF), F32),
            jax.ShapeDtypeStruct((LAYERS, FF), F32),
            jax.ShapeDtypeStruct((LAYERS, FF, D), F32),
            jax.ShapeDtypeStruct((LAYERS, D), F32),
        ),
        in_specs=[VMEM] * (2 * pieces),
        out_specs=(VMEM,) * 13,
        scratch_shapes=[pltpu.VMEM((2, part_rows * dp, HW), BF)],
        compiler_params=pltpu.CompilerParams(vmem_limit_bytes=48 * 1024 * 1024),
        name="unpack",
    )(*whole, *others))
    grads[3] = grads[3].swapaxes(1, 2)
    return (result, grad) + tuple(grads)


def solution(mesh):
    spread = P(("dp", "heads"), None)
    group = (P(None, "heads", None, None), P(None, "heads", None, None), P(None, "heads", None))
    in_specs = (spread, spread, P("dp"), P(), P()) + group + (P(),) * 8
    out_specs = (spread, spread, P(), P()) + group + (P(),) * 8
    return jax.shard_map(
        functools.partial(shards, mesh.shape["dp"]),
        mesh=mesh,
        in_specs=in_specs,
        out_specs=out_specs,
        check_vma=False,
    )
```
